512 devices in a mesh: site: 64 (over y_hi, z, core), probe: 8 (over y_lo, x).
Axes of the slice: x: 4, y: 4 (y_hi: 2, y_lo: 2; y = y_hi * 2 + y_lo), z: 16, core: 2. Of those that a mesh axis runs over, the one named last changes fastest.
Arguments:
- angles: float32 [128, 4, 256], P('site'), may hold values from -3.140625 to 3.140625
- coupling: float32 [128, 4, 256], P('site'), may hold values from 0.03 to 0.46, as said below
- thermal_noise: float32 [128, 4, 256], P('site'), may hold values from -6 to 6
- coefficients: float32 [5], replicated, may hold values from 0.3 to 1.5
- probes: bfloat16 [128, 4, 2, 512, 256], P('site', None, None, 'probe'), may hold values from -6 to 6
- hopping: bfloat16 [128, 4, 4, 256, 256], P('site'), as said below
- offsets: int32 [128, 4, 4], P('site'), may hold values from 1 to 7, as said below
Outputs:
- angle_next: float32 [128, 4, 256], P('site')
- spin_force: float32 [128, 4, 256], P('site')
The draws below stay inside these ranges and needn't reach their ends.
Inputs may be any that keep to these rules, and one draw needn't show every extreme that they name: `offsets`: each tile names the four codes 1, 3, 5, 7 in some order; code o points to the tile o // 3 - 1 tile rows and o % 3 - 1 tile columns away. `hopping`: reciprocal tiles: the tile of code c at a tile is the transpose of the tile of code 8 - c at the tile it points to. `coupling`: positive couplings.
All inputs are finite; a program needn't handle non-finite values. Where the reference program divides by a largest or mean magnitude, that divisor is 1e-20 or more.
Results may differ from the reference program's by a relative error of at most 0.0037.
Values may be sent and summed in bfloat16 or wider, within the bound.
No kernel may reach another device: no remote copies, remote signals or barrier semaphores. Data moves between devices by JAX's collectives and lax.ppermute only.
A program may use at most 64 MiB of HBM per device.

```python
import math
import jax
import jax.numpy as jnp
from jax import lax

TILE = 256
NBR = 4
STEPS = 4
TW = 4
P_DEV = 64
TROWS = 128
PROBES = 512
N_PROBE = 8


def tile_codes(key):
    key = jax.random.fold_in(key, 11)
    scores = jax.random.randint(key, (TROWS, TW, NBR), 0, 1 << 20) * NBR + jnp.arange(NBR, dtype=jnp.int32)
    ranked = jnp.argsort(scores, axis=-1).astype(jnp.int32)
    return (2 * ranked + 1).astype(jnp.int32)


def draw_coupling(key, part):
    key = jax.random.fold_in(key, 5)
    height = jnp.arange(TROWS).astype(jnp.float32)[:, None, None] / TROWS
    roughness = jnp.exp(jax.random.uniform(key, (TROWS, TW, TILE), jnp.float32, jnp.log(2.0 / 3.0), jnp.log(1.5)))
    baseline = 0.1 * jnp.exp(jnp.log(3.0) * height)
    return (baseline * roughness).astype(jnp.float32)


def draw_offsets(key, part):
    return tile_codes(key)


def draw_hopping(key, part):
    codes = tile_codes(key)
    key = jax.random.fold_in(key, 13)
    key_vert, key_across = jax.random.split(key)
    scale = (4.0 * NBR * TILE) ** (-0.5)
    vertical = jax.random.normal(key_vert, (TROWS, TW, TILE, TILE), jnp.float32) * scale
    across = jax.random.normal(key_across, (TROWS, TW, TILE, TILE), jnp.float32) * scale
    from_below = jnp.swapaxes(jnp.roll(vertical, 1, axis=0), 2, 3)
    from_left = jnp.swapaxes(jnp.roll(across, 1, axis=1), 2, 3)
    tiles = []
    for slot in range(NBR):
        code = codes[:, :, slot][:, :, None, None]
        chosen = jnp.where(code == 7, vertical, jnp.where(code == 1, from_below, jnp.where(code == 5, across, from_left)))
        tiles.append(chosen.astype(jnp.bfloat16))
    return jnp.stack(tiles, axis=2)


def steps_of(stream_key, extent, cuts, low, high):
    gain = 1.0
    for axis_at, blocks in cuts:
        draws = jax.random.uniform(jax.random.fold_in(jax.random.fold_in(stream_key, 6), axis_at), (blocks,), jnp.float32, low / len(cuts), high / len(cuts))
        gain = gain * jnp.repeat(jnp.exp(draws), extent[axis_at] // blocks).reshape((-1,) + (1,) * (len(extent) - 1 - axis_at))
    return gain


def normal_values(key, extent, scale, reach, pieces=(), held_as=jnp.bfloat16):
    values = jax.random.normal(key, extent, jnp.float32) * scale
    if len(pieces) > 0:
        values = steps_of(key, extent, pieces, -0.22, 0.18) * values
    return jnp.clip(values, min=-reach, max=reach).astype(held_as)


def setup_inputs(seed: int = 0) -> dict:
    streams_of = jax.random.split(jax.random.key(seed), 8)
    angles = jnp.clip(jax.random.uniform(streams_of[0], (TROWS, TW, TILE), jnp.float32, -3.140625, 3.140625), -3.140625, 3.140625)
    coupling = draw_coupling(jax.random.fold_in(streams_of[7], 71), 0)
    thermal_noise = normal_values(streams_of[2], (TROWS, TW, TILE), 1.0, 6.0, ((0, 64),), jnp.float32)
    coefficients = jnp.clip(jnp.exp(jax.random.uniform(streams_of[3], (STEPS + 1,), jnp.float32, math.log(0.3), math.log(1.5))), 0.3, 1.5)
    probes = normal_values(streams_of[4], (TROWS, TW, 2, PROBES, TILE), 1.0, 6.0, ((0, 64), (3, 8)))
    hopping = draw_hopping(jax.random.fold_in(streams_of[7], 71), 0)
    offsets = draw_offsets(jax.random.fold_in(streams_of[7], 71), 0)
    return {"angles": angles, "coupling": coupling, "thermal_noise": thermal_noise, "coefficients": coefficients, "probes": probes, "hopping": hopping, "offsets": offsets}


BAND = 8.0
STEP_MAX = 0.3
TWO_TEMP = 0.1

def tile_sources(offsets):
    tile_rows = jnp.arange(TROWS).astype(jnp.int32)[:, None, None]
    tile_cols = jnp.arange(TW).astype(jnp.int32)[None, :, None]
    row_move = offsets // 3 - 1
    col_move = offsets % 3 - 1
    return ((tile_rows + 1 + row_move) * TW + jnp.mod(tile_cols + col_move, TW)).astype(jnp.int32)

def apply_hop(vectors_low, hopping_wide, sources):
    extended = jnp.concatenate([vectors_low[-1:], vectors_low, vectors_low[:1]], axis=0)
    flattened = extended.reshape((-1,) + extended.shape[2:])
    picked = flattened[sources].astype(jnp.float32)
    return jnp.einsum('abkopj,abkij->abopi', picked, hopping_wide, precision=lax.Precision.HIGHEST)

def kondo_term(vectors, coupled_cos, coupled_sin):
    upper = vectors[:, :, 0]
    lower = vectors[:, :, 1]
    first_orb = coupled_cos[:, :, None, :] * upper + coupled_sin[:, :, None, :] * lower
    second_orb = coupled_sin[:, :, None, :] * upper - coupled_cos[:, :, None, :] * lower
    return jnp.stack([first_orb, second_orb], axis=2)

def reference(angles, coupling, thermal_noise, coefficients, probes, hopping, offsets):
    cosines = jnp.cos(angles)
    sine_values = jnp.sin(angles)
    coupled_cos = coupling * cosines
    coupled_sin = coupling * sine_values
    hopping_wide = hopping.astype(jnp.float32)
    sources = tile_sources(offsets)
    probe_blocks = probes.reshape(TROWS, TW, 2, N_PROBE, P_DEV, TILE)
    probe_blocks = jnp.moveaxis(probe_blocks, 3, 0)

    def part_total(probe_block):
        start_vec = probe_block.astype(jnp.float32)
        previous = start_vec
        current = start_vec
        current_low = probe_block
        weighted = coefficients[0] * start_vec
        for level in range(STEPS):
            product = apply_hop(current_low, hopping_wide, sources) + kondo_term(current, coupled_cos, coupled_sin)
            if level == 0:
                following = 2.0 * product
            else:
                following = 2.0 * product - previous
            weighted = weighted + (level + 2) * coefficients[level + 1] * following
            previous = current
            current = following
            current_low = following.astype(jnp.bfloat16)
        upper_r = start_vec[:, :, 0]
        lower_r = start_vec[:, :, 1]
        upper_w = weighted[:, :, 0]
        lower_w = weighted[:, :, 1]
        terms = -sine_values[:, :, None, :] * (upper_r * upper_w - lower_r * lower_w) + cosines[:, :, None, :] * (upper_r * lower_w + lower_r * upper_w)
        return lax.optimization_barrier(jnp.sum(terms, axis=2))
    summed = lax.optimization_barrier(jnp.sum(lax.map(part_total, probe_blocks), axis=0))
    spin_force = -BAND * coupling * summed / PROBES
    largest = jnp.max(jnp.abs(spin_force))
    step_size = STEP_MAX / (largest + 1e-06)
    angle_next = angles + step_size * spin_force + jnp.sqrt(TWO_TEMP * step_size) * thermal_noise
    return (angle_next, spin_force)
```

```python
import functools
import jax
import jax.numpy as jnp
from jax import lax
from jax.experimental import pallas as pl
from jax.experimental.pallas import tpu as pltpu
from jax.sharding import PartitionSpec as P

BAND = 8.0
STEP_MAX = 0.3
TWO_TEMP = 0.1

VERT, LEFT, RIGHT, RIM = range(4)
IN_VMEM = pl.BlockSpec(memory_space=pltpu.VMEM)
IN_SMEM = pl.BlockSpec(memory_space=pltpu.SMEM)
IN_HBM = pl.BlockSpec(memory_space=pltpu.HBM)


def held(array, space=pltpu.VMEM):
    return pltpu.with_memory_space_constraint(array, space)


def call(body, outs, in_specs, args, scratch=(), flops=0, moved=0):
    return pl.pallas_call(
        body,
        out_shape=[pltpu.VMEM(shape, dtype) for shape, dtype in outs],
        in_specs=in_specs,
        out_specs=[IN_VMEM] * len(outs),
        scratch_shapes=list(scratch),
        compiler_params=pltpu.CompilerParams(vmem_limit_bytes=16 * 1024 * 1024),
        cost_estimate=pl.CostEstimate(flops=flops, bytes_accessed=moved, transcendentals=0),
    )(*args)


def product(vectors, matrix):
    return jnp.dot(vectors, matrix, preferred_element_type=jnp.float32)


def folded(values):
    return jnp.sum(values.reshape(-1, 8, values.shape[-1]), axis=0)


def overlap_terms(probe, vectors):
    half = probe.shape[0] // 2
    upper_r = probe[:half].astype(jnp.float32)
    lower_r = probe[half:].astype(jnp.float32)
    upper_w, lower_w = vectors[:half], vectors[half:]
    same = folded(upper_r * upper_w - lower_r * lower_w)
    cross = folded(upper_r * lower_w + lower_r * upper_w)
    return same, cross


def split_body(parity_ref, probes_ref, outer_ref, inner_ref, sems):
    parity = parity_ref[0]
    copies = [
        pltpu.make_async_copy(probes_ref.at[parity], outer_ref, sems.at[0]),
        pltpu.make_async_copy(probes_ref.at[1 - parity], inner_ref, sems.at[1]),
    ]
    for copy in copies:
        copy.start()
    for copy in copies:
        copy.wait()


def local_hop(cols, rows, outer_ref, inner_ref, tile, matrix):
    refs = (outer_ref, inner_ref)
    row, col = divmod(tile, cols)

    def vectors(r, c):
        return refs[r][pl.ds(c * rows, rows), :]

    right, left = (col + 1) % cols, (col - 1) % cols
    total = product(vectors(1 - row, col), matrix(VERT, (1 - row) * cols + col))
    total += product(vectors(row, right), matrix(LEFT, row * cols + right))
    total += product(vectors(row, left), matrix(RIGHT, row * cols + left))
    return total


def kondo(vectors, twice_cos, twice_sin):
    half = vectors.shape[0] // 2
    upper, lower = vectors[:half], vectors[half:]
    return jnp.concatenate(
        [twice_cos * upper + twice_sin * lower, twice_sin * upper - twice_cos * lower], axis=0
    )


def first_body(cols, rows, parity_ref, offsets_ref, coef_ref, hopping_ref, outer_ref, inner_ref,
               cos_ref, sin_ref, sorted_ref, part_ref, terms_ref, rims_ref, sems):
    tiles = 2 * cols
    slots = hopping_ref.shape[0] // tiles
    parity = parity_ref[0]

    def fetch(kind, tile):
        row, col = divmod(tile, cols)
        origin = (row + parity - 2 * row * parity) * cols + col
        if kind == LEFT:
            code = 3
        elif kind == RIGHT:
            code = 5
        else:
            towards_high = (row == 0) == (kind == VERT)
            code = 7 - 6 * parity if towards_high else 1 + 6 * parity
        slot = jnp.int32(0)
        for k in range(1, slots):
            slot += jnp.where(offsets_ref[origin * slots + k] == code, k, 0)
        place = kind * tiles + tile
        target = rims_ref.at[tile] if kind == RIM else sorted_ref.at[place]
        return pltpu.make_async_copy(
            hopping_ref.at[origin * slots + slot], target, sems.at[place]
        )

    order = [(kind, tile) for kind in range(4) for tile in range(tiles)]
    copies = [fetch(kind, tile) for kind, tile in order]
    for copy in copies:
        copy.start()
    weight = coef_ref[0]
    for tile in range(tiles):
        row, col = divmod(tile, cols)
        probe = (outer_ref, inner_ref)[row][pl.ds(col * rows, rows), :]
        same, cross = overlap_terms(probe, probe.astype(jnp.float32))
        terms_ref[tile] = weight * same
        terms_ref[tiles + tile] = weight * cross
    for copy in copies:
        copy.wait()
    for tile in range(tiles):
        row, col = divmod(tile, cols)
        probe = (outer_ref, inner_ref)[row][pl.ds(col * rows, rows), :].astype(jnp.float32)
        total = local_hop(
            cols, rows, outer_ref, inner_ref, tile, lambda kind, t: sorted_ref[kind * tiles + t]
        )
        part_ref[tile] = 2.0 * total + kondo(
            probe, cos_ref[pl.ds(tile, 1), :], sin_ref[pl.ds(tile, 1), :]
        )
        sorted_ref[RIM * tiles + tile] = rims_ref[tile].T


def rim_body(cols, rows, rim_outer_ref, rim_inner_ref, sorted_ref, part_ref,
             field_ref, outer_ref, inner_ref):
    tiles = 2 * cols
    for tile in range(tiles):
        row, col = divmod(tile, cols)
        rim = (rim_outer_ref, rim_inner_ref)[row][pl.ds(col * rows, rows), :]
        field = part_ref[tile] + 2.0 * product(rim, sorted_ref[RIM * tiles + tile])
        field_ref[tile] = field
        (outer_ref, inner_ref)[row][pl.ds(col * rows, rows), :] = field.astype(jnp.bfloat16)


def local_body(cols, rows, level, last, coef_ref, probe_outer_ref, probe_inner_ref, field_ref,
               outer_ref, inner_ref, *rest):
    tiles = 2 * cols
    previous_ref = None
    if level > 1:
        previous_ref, *rest = rest
    sorted_ref, cos_ref, sin_ref, terms_ref = rest[:4]
    outs = rest[4:]
    weight = (level + 1) * coef_ref[level]
    weight_next = (level + 2) * coef_ref[level + 1]
    for tile in range(tiles):
        row, col = divmod(tile, cols)
        place = pl.ds(col * rows, rows)
        probe = (probe_outer_ref, probe_inner_ref)[row][place, :]
        field = field_ref[tile]
        total = local_hop(
            cols, rows, outer_ref, inner_ref, tile, lambda kind, t: sorted_ref[kind * tiles + t]
        )
        following = 2.0 * total + kondo(
            field, cos_ref[pl.ds(tile, 1), :], sin_ref[pl.ds(tile, 1), :]
        )
        if previous_ref is None:
            following -= probe.astype(jnp.float32)
        else:
            following -= previous_ref[tile]
        if last:
            same, cross = overlap_terms(probe, weight * field + weight_next * following)
        else:
            same, cross = overlap_terms(probe, field)
            same, cross = weight * same, weight * cross
            outs[1][tile] = following
        outs[0][tile] = terms_ref[tile] + same
        outs[0][tiles + tile] = terms_ref[tiles + tile] + cross


def last_body(cols, rows, level, coef_ref, probe_outer_ref, probe_inner_ref, rim_outer_ref,
              rim_inner_ref, sorted_ref, terms_ref, same_ref, cross_ref, out_ref):
    tiles = 2 * cols
    weight = 2.0 * (level + 1) * coef_ref[level]
    for tile in range(tiles):
        row, col = divmod(tile, cols)
        place = pl.ds(col * rows, rows)
        probe = (probe_outer_ref, probe_inner_ref)[row][place, :]
        rim = (rim_outer_ref, rim_inner_ref)[row][place, :]
        same, cross = overlap_terms(probe, product(rim, sorted_ref[RIM * tiles + tile]))
        same = jnp.sum(terms_ref[tile] + weight * same, axis=0, keepdims=True)
        cross = jnp.sum(terms_ref[tiles + tile] + weight * cross, axis=0, keepdims=True)
        share = same_ref[pl.ds(tile, 1), :] * same + cross_ref[pl.ds(tile, 1), :] * cross
        for peer in range(out_ref.shape[0]):
            out_ref[peer, pl.ds(tile, 1), :] = share


def force_body(shares_ref, force_ref, largest_ref):
    force = shares_ref[0]
    for peer in range(1, shares_ref.shape[0]):
        force += shares_ref[peer]
    force_ref[...] = force
    largest_ref[...] = jnp.full(largest_ref.shape, jnp.max(jnp.abs(force)), jnp.float32)


def move_body(parity_ref, largest_ref, force_ref, angles_ref, noise_ref, next_ref, out_ref):
    parity = parity_ref[0]
    cols = out_ref.shape[1]
    largest = jnp.max(largest_ref[...])
    step_size = jnp.full((1, 1), STEP_MAX, jnp.float32) / (largest + 1e-06)
    kick = jnp.sqrt(TWO_TEMP * step_size)
    for row in range(2):
        origin = row + parity - 2 * row * parity
        force = force_ref[pl.ds(row * cols, cols), :]
        out_ref[origin] = force
        next_ref[origin] = angles_ref[origin] + step_size * force + kick * noise_ref[origin]


def exchange(outer, inner):
    count = lax.axis_size("site")
    across = [(i, (i + 1) % count if i % 2 else (i - 1) % count) for i in range(count)]
    within = [(i, i ^ 1) for i in range(count)]
    return lax.ppermute(outer, "site", across), lax.ppermute(inner, "site", within)


def local(angles, coupling, thermal_noise, coefficients, probes, hopping, offsets):
    cols, orbitals, share, width = probes.shape[1:]
    rows = orbitals * share
    tiles = 2 * cols
    steps = coefficients.shape[0] - 1
    f32, bf16 = jnp.float32, jnp.bfloat16
    side = ((cols * rows, width), bf16)
    whole = ((tiles, rows, width), f32)
    terms_like = ((2 * tiles, 8, width), f32)
    probe_total = lax.axis_size("probe") * share

    parity = (lax.axis_index("site") % 2).astype(jnp.int32).reshape(1)
    outer, inner = call(
        split_body, [side, side], [IN_SMEM, IN_HBM],
        (parity, held(probes.reshape(2, cols * rows, width), pltpu.HBM)),
        scratch=[pltpu.SemaphoreType.DMA((2,))],
    )
    probe_outer, probe_inner = outer, inner
    rims = exchange(outer, inner)

    def ordered(array):
        return jnp.where(parity[0] == 0, array, array[::-1]).reshape(tiles, width)

    cosines, sine_values = ordered(jnp.cos(angles)), ordered(jnp.sin(angles))
    strength = ordered(coupling)
    twice_cos = 2.0 * strength * cosines
    twice_sin = 2.0 * strength * sine_values
    scale = (-BAND / probe_total) * strength
    same_factor = -scale * sine_values
    cross_factor = scale * cosines

    sorted_hop, part, terms = call(
        functools.partial(first_body, cols, rows),
        [((4 * tiles, width, width), bf16), whole, terms_like],
        [IN_SMEM, IN_SMEM, IN_SMEM, IN_HBM] + [IN_VMEM] * 4,
        (parity, offsets.reshape(-1), coefficients,
         held(hopping.reshape(-1, width, width), pltpu.HBM),
         held(outer), held(inner), held(twice_cos), held(twice_sin)),
        scratch=[pltpu.VMEM((tiles, width, width), bf16), pltpu.SemaphoreType.DMA((4 * tiles,))],
        flops=2 * 3 * tiles * rows * width * width, moved=hopping.size * 2,
    )
    field = previous = None
    for level in range(1, steps):
        previous, (field, outer, inner) = field, call(
            functools.partial(rim_body, cols, rows),
            [whole, side, side],
            [IN_VMEM] * 4,
            tuple(held(x) for x in (*rims, sorted_hop, part)),
            flops=2 * tiles * rows * width * width,
        )
        rims = exchange(outer, inner)
        last = level == steps - 1
        args = [probe_outer, probe_inner, field, outer, inner]
        if level > 1:
            args.append(previous)
        args += [sorted_hop, twice_cos, twice_sin, terms]
        terms, *rest = call(
            functools.partial(local_body, cols, rows, level, last),
            [terms_like] if last else [terms_like, whole],
            [IN_SMEM] + [IN_VMEM] * len(args),
            (coefficients, *(held(x) for x in args)),
            flops=2 * 3 * tiles * rows * width * width, moved=hopping.size * 2,
        )
        if not last:
            part = rest[0]

    peers = lax.axis_size("probe")
    shares = call(
        functools.partial(last_body, cols, rows, steps),
        [((peers, tiles, width), f32)],
        [IN_SMEM] + [IN_VMEM] * 8,
        (coefficients, *(held(x) for x in (
            probe_outer, probe_inner, *rims, sorted_hop, terms, same_factor, cross_factor))),
        flops=2 * tiles * rows * width * width,
    )[0]
    shares = lax.all_to_all(shares, "probe", 0, 0)
    force, largest = call(
        force_body,
        [((tiles, width), f32), ((lax.axis_size("site"), 1, 128), f32)],
        [IN_VMEM], (held(shares),),
    )
    largest = lax.all_to_all(largest, "site", 0, 0)
    return pl.pallas_call(
        move_body,
        out_shape=[jax.ShapeDtypeStruct(angles.shape, f32)] * 2,
        in_specs=[IN_SMEM] + [IN_VMEM] * 4,
        out_specs=[IN_VMEM] * 2,
    )(parity, held(largest), held(force), held(angles), held(thermal_noise))


def solution(mesh):
    in_specs = (
        P("site", None, None),
        P("site", None, None),
        P("site", None, None),
        P(),
        P("site", None, None, "probe", None),
        P("site", None, None, None, None),
        P("site", None, None),
    )
    out_specs = (P("site", None, None), P("site", None, None))
    return jax.shard_map(local, mesh=mesh, in_specs=in_specs, out_specs=out_specs, check_vma=False)
```

```python
import functools
import jax
import jax.numpy as jnp
from jax import lax
from jax.experimental import pallas as pl
from jax.experimental.pallas import tpu as pltpu
from jax.sharding import PartitionSpec as P

BAND = 8.0
STEP_MAX = 0.3
TWO_TEMP = 0.1

VERT, LEFT, RIGHT, RIM, TURNED = range(5)
IN_VMEM = pl.BlockSpec(memory_space=pltpu.VMEM)
IN_SMEM = pl.BlockSpec(memory_space=pltpu.SMEM)
IN_HBM = pl.BlockSpec(memory_space=pltpu.HBM)


def held(array, space=pltpu.VMEM):
    return pltpu.with_memory_space_constraint(array, space)


def call(body, outs, in_specs, args, scratch=(), flops=0, moved=0):
    return pl.pallas_call(
        body,
        out_shape=[pltpu.VMEM(shape, dtype) for shape, dtype in outs],
        in_specs=in_specs,
        out_specs=[IN_VMEM] * len(outs),
        scratch_shapes=list(scratch),
        compiler_params=pltpu.CompilerParams(vmem_limit_bytes=16 * 1024 * 1024),
        cost_estimate=pl.CostEstimate(flops=flops, bytes_accessed=moved, transcendentals=0),
    )(*args)


def product(vectors, matrix):
    return jnp.dot(vectors, matrix, preferred_element_type=jnp.float32)


def folded(values):
    return jnp.sum(values.reshape(-1, 8, values.shape[-1]), axis=0)


def overlap_terms(probe, vectors):
    half = probe.shape[0] // 2
    upper_r = probe[:half].astype(jnp.float32)
    lower_r = probe[half:].astype(jnp.float32)
    upper_w, lower_w = vectors[:half], vectors[half:]
    same = folded(upper_r * upper_w - lower_r * lower_w)
    cross = folded(upper_r * lower_w + lower_r * upper_w)
    return same, cross


def split_body(parity_ref, probes_ref, outer_ref, inner_ref, sems):
    parity = parity_ref[0]
    copies = [
        pltpu.make_async_copy(probes_ref.at[parity], outer_ref, sems.at[0]),
        pltpu.make_async_copy(probes_ref.at[1 - parity], inner_ref, sems.at[1]),
    ]
    for copy in copies:
        copy.start()
    for copy in copies:
        copy.wait()


def local_hop(cols, rows, outer_ref, inner_ref, tile, matrix):
    refs = (outer_ref, inner_ref)
    row, col = divmod(tile, cols)

    def vectors(r, c):
        return refs[r][pl.ds(c * rows, rows), :]

    right, left = (col + 1) % cols, (col - 1) % cols
    total = product(vectors(1 - row, col), matrix(VERT, (1 - row) * cols + col))
    total += product(vectors(row, right), matrix(LEFT, row * cols + right))
    total += product(vectors(row, left), matrix(RIGHT, row * cols + left))
    return total


def kondo(vectors, twice_cos, twice_sin):
    half = vectors.shape[0] // 2
    upper, lower = vectors[:half], vectors[half:]
    return jnp.concatenate(
        [twice_cos * upper + twice_sin * lower, twice_sin * upper - twice_cos * lower], axis=0
    )


def first_body(cols, rows, probe_total, parity_ref, offsets_hbm, coef_hbm, hopping_hbm, angles_hbm,
               coupling_hbm, outer_ref, inner_ref, sorted_ref, part_ref, terms_ref, weights_ref,
               cos_ref, sin_ref, same_ref, cross_ref,
               offsets_ref, coef_ref, raw_ref, angles_ref, coupling_ref, sems):
    tiles = 2 * cols
    slots = offsets_ref.shape[2]
    steps = coef_ref.shape[0]
    parity = parity_ref[0]
    small = [
        pltpu.make_async_copy(source, target, sems.at[k])
        for k, (source, target) in enumerate((
            (offsets_hbm, offsets_ref), (coef_hbm, coef_ref),
            (angles_hbm, angles_ref), (coupling_hbm, coupling_ref),
        ))
    ]
    large = [
        pltpu.make_async_copy(
            hopping_hbm.at[pl.ds(tile * slots, slots)], raw_ref.at[pl.ds(tile * slots, slots)],
            sems.at[4 + tile],
        )
        for tile in range(tiles)
    ]
    for copy in small + large:
        copy.start()
    for copy in small:
        copy.wait()

    def tile_of(kind, tile):
        row, col = divmod(tile, cols)
        origin = row + parity - 2 * row * parity
        if kind == LEFT:
            code = 3
        elif kind == RIGHT:
            code = 5
        else:
            towards_high = (row == 0) == (kind == VERT)
            code = 7 - 6 * parity if towards_high else 1 + 6 * parity
        slot = jnp.int32(0)
        for k in range(1, slots):
            slot += jnp.where(offsets_ref[origin, col, k] == code, k, 0)
        return (origin * cols + col) * slots + slot

    for row in range(2):
        origin = row + parity - 2 * row * parity
        place = pl.ds(row * cols, cols)
        angles, strength = angles_ref[origin], coupling_ref[origin]
        cosines, sine_values = jnp.cos(angles), jnp.sin(angles)
        scale = (-BAND / probe_total) * strength
        cos_ref[place, :] = 2.0 * strength * cosines
        sin_ref[place, :] = 2.0 * strength * sine_values
        same_ref[place, :] = -scale * sine_values
        cross_ref[place, :] = scale * cosines
    for level in range(steps):
        weights_ref[pl.ds(level, 1), :] = jnp.full(
            (1, weights_ref.shape[1]), (level + 1) * coef_ref[level], jnp.float32
        )
    for tile in range(tiles):
        row, col = divmod(tile, cols)
        probe = (outer_ref, inner_ref)[row][pl.ds(col * rows, rows), :]
        same, cross = overlap_terms(probe, probe.astype(jnp.float32))
        terms_ref[tile] = coef_ref[0] * same
        terms_ref[tiles + tile] = coef_ref[0] * cross
    for copy in large:
        copy.wait()

    def matrix(kind, tile):
        found = raw_ref[tile_of(kind, tile)]
        sorted_ref[kind * tiles + tile] = found
        return found

    for tile in range(tiles):
        row, col = divmod(tile, cols)
        probe = (outer_ref, inner_ref)[row][pl.ds(col * rows, rows), :].astype(jnp.float32)
        total = local_hop(cols, rows, outer_ref, inner_ref, tile, matrix)
        part_ref[tile] = 2.0 * total + kondo(
            probe, cos_ref[pl.ds(tile, 1), :], sin_ref[pl.ds(tile, 1), :]
        )
    for tile in range(tiles):
        sorted_ref[TURNED * tiles + tile] = matrix(RIM, tile).T


def rim_body(cols, rows, rim_outer_ref, rim_inner_ref, sorted_ref, part_ref,
             field_ref, outer_ref, inner_ref):
    tiles = 2 * cols
    for tile in range(tiles):
        row, col = divmod(tile, cols)
        place = pl.ds(col * rows, rows)
        rim = (rim_outer_ref, rim_inner_ref)[row][place, :]
        field = part_ref[tile] + 2.0 * product(rim, sorted_ref[TURNED * tiles + tile])
        field_ref[tile] = field
        (outer_ref, inner_ref)[row][place, :] = field.astype(jnp.bfloat16)


def rim_sent_body(cols, rows, level, rim_outer_ref, rim_inner_ref, sorted_ref, part_ref,
                  probe_outer_ref, probe_inner_ref, weights_ref,
                  field_ref, outer_ref, inner_ref, sent_outer_ref, sent_inner_ref):
    tiles = 2 * cols
    rim_body(cols, rows, rim_outer_ref, rim_inner_ref, sorted_ref, part_ref,
             field_ref, outer_ref, inner_ref)
    weight = 2.0 * weights_ref[pl.ds(level + 1, 1), 0:1]
    for tile in range(tiles):
        row, col = divmod(tile, cols)
        place = pl.ds(col * rows, rows)
        field_low = (outer_ref, inner_ref)[row][place, :]
        probe = (probe_outer_ref, probe_inner_ref)[row][place, :]
        same, cross = overlap_terms(probe, product(field_low, sorted_ref[RIM * tiles + tile]))
        sent_ref = (sent_outer_ref, sent_inner_ref)[row]
        sent_ref[pl.ds(col, 1), :] = weight * jnp.sum(same, axis=0, keepdims=True)
        sent_ref[pl.ds(cols + col, 1), :] = weight * jnp.sum(cross, axis=0, keepdims=True)


def local_body(cols, rows, level, last, weights_ref, probe_outer_ref, probe_inner_ref, field_ref,
               outer_ref, inner_ref, *rest):
    tiles = 2 * cols
    previous_ref = None
    if level > 1:
        previous_ref, *rest = rest
    sorted_ref, cos_ref, sin_ref, terms_ref = rest[:4]
    rest = rest[4:]
    weight = weights_ref[pl.ds(level, 1), 0:1]
    weight_next = weights_ref[pl.ds(level + 1, 1), 0:1]

    def matrix(kind, source):
        return sorted_ref[kind * tiles + source]

    for tile in range(tiles):
        row, col = divmod(tile, cols)
        place = pl.ds(col * rows, rows)
        probe = (probe_outer_ref, probe_inner_ref)[row][place, :]
        field = field_ref[tile]
        total = local_hop(cols, rows, outer_ref, inner_ref, tile, matrix)
        following = 2.0 * total + kondo(
            field, cos_ref[pl.ds(tile, 1), :], sin_ref[pl.ds(tile, 1), :]
        )
        if previous_ref is None:
            following -= probe.astype(jnp.float32)
        else:
            following -= previous_ref[tile]
        if last:
            same_ref, cross_ref, share_ref = rest
            same, cross = overlap_terms(probe, weight * field + weight_next * following)
            same = jnp.sum(terms_ref[tile] + same, axis=0, keepdims=True)
            cross = jnp.sum(terms_ref[tiles + tile] + cross, axis=0, keepdims=True)
            one = pl.ds(tile, 1)
            share_ref[one, :] = same_ref[one, :] * same + cross_ref[one, :] * cross
        else:
            out_ref, following_ref = rest
            same, cross = overlap_terms(probe, field)
            out_ref[tile] = terms_ref[tile] + weight * same
            out_ref[tiles + tile] = terms_ref[tiles + tile] + weight * cross
            following_ref[tile] = following


def share_body(cols, parity_ref, share_ref, from_inner_ref, to_outer_ref, same_ref, cross_ref,
               out_ref):
    peers = out_ref.shape[0] // 2
    parity = parity_ref[0]
    same = same_ref[cols:, :] * from_inner_ref[:cols, :]
    cross = cross_ref[cols:, :] * from_inner_ref[cols:, :]
    share = jnp.concatenate([share_ref[:cols, :], share_ref[cols:, :] + same + cross], axis=0)
    for peer in range(peers):
        out_ref[(1 - parity) * peers + peer] = share
        out_ref[parity * peers + peer] = to_outer_ref[...]


def force_body(cols, parity_ref, shares_ref, same_ref, cross_ref, force_ref, largest_ref):
    peers = shares_ref.shape[0] // 2
    parity = parity_ref[0]
    own, across = shares_ref[(1 - parity) * peers], shares_ref[parity * peers]
    for peer in range(1, peers):
        own += shares_ref[(1 - parity) * peers + peer]
        across += shares_ref[parity * peers + peer]
    outer = same_ref[:cols, :] * across[:cols] + cross_ref[:cols, :] * across[cols:]
    force = jnp.concatenate([own[:cols] + outer, own[cols:]], axis=0)
    force_ref[...] = force
    largest_ref[...] = jnp.full(largest_ref.shape, jnp.max(jnp.abs(force)), jnp.float32)


def move_body(parity_ref, largest_ref, force_ref, angles_ref, noise_ref, next_ref, out_ref):
    parity = parity_ref[0]
    cols = out_ref.shape[1]
    largest = jnp.max(largest_ref[...])
    step_size = jnp.full((1, 1), STEP_MAX, jnp.float32) / (largest + 1e-06)
    kick = jnp.sqrt(TWO_TEMP * step_size)
    for row in range(2):
        origin = row + parity - 2 * row * parity
        force = force_ref[pl.ds(row * cols, cols), :]
        out_ref[origin] = force
        next_ref[origin] = angles_ref[origin] + step_size * force + kick * noise_ref[origin]


def exchange_outer(outer):
    count = lax.axis_size("site")
    pairs = [(i, (i + 1) % count if i % 2 else (i - 1) % count) for i in range(count)]
    return lax.ppermute(outer, "site", pairs)


def exchange_inner(inner):
    return lax.ppermute(inner, "site", [(i, i ^ 1) for i in range(lax.axis_size("site"))])


def local(angles, coupling, thermal_noise, coefficients, probes, hopping, offsets):
    cols, orbitals, share, width = probes.shape[1:]
    rows = orbitals * share
    tiles = 2 * cols
    steps = coefficients.shape[0] - 1
    f32, bf16 = jnp.float32, jnp.bfloat16
    side = ((cols * rows, width), bf16)
    whole = ((tiles, rows, width), f32)
    terms_like = ((2 * tiles, 8, width), f32)
    probe_total = lax.axis_size("probe") * share

    sites, peers = lax.axis_size("site"), lax.axis_size("probe")
    parity = (lax.axis_index("site") % 2).astype(jnp.int32).reshape(1)
    outer, inner = call(
        split_body, [side, side], [IN_SMEM, IN_HBM],
        (parity, held(probes.reshape(2, cols * rows, width), pltpu.HBM)),
        scratch=[pltpu.SemaphoreType.DMA((2,))],
    )
    probe_outer, probe_inner = outer, inner
    rims = rim_probes = exchange_outer(outer), exchange_inner(inner)

    local_flops = 2 * 3 * tiles * rows * width * width
    row_like = ((tiles, width), f32)
    sorted_hop, part, terms, weights, twice_cos, twice_sin, same_factor, cross_factor = call(
        functools.partial(first_body, cols, rows, probe_total),
        [((5 * tiles, width, width), bf16), whole, terms_like, ((8, 128), f32)] + [row_like] * 4,
        [IN_SMEM] + [IN_HBM] * 5 + [IN_VMEM] * 2,
        (parity, *(held(x, pltpu.HBM) for x in (
            offsets, coefficients, hopping.reshape(-1, width, width), angles, coupling)),
         held(outer), held(inner)),
        scratch=[
            pltpu.SMEM(offsets.shape, jnp.int32), pltpu.SMEM(coefficients.shape, f32),
            pltpu.VMEM((hopping.size // width**2, width, width), bf16),
            pltpu.VMEM(angles.shape, f32), pltpu.VMEM(coupling.shape, f32),
            pltpu.SemaphoreType.DMA((4 + tiles,)),
        ],
        flops=local_flops, moved=hopping.size * 2,
    )
    field = previous = None
    for level in range(1, steps):
        last = level == steps - 1
        previous = field
        args = [*rims, sorted_hop, part]
        if last:
            args += [*rim_probes, weights]
            field, outer, inner, to_outer, to_inner = call(
                functools.partial(rim_sent_body, cols, rows, level),
                [whole, side, side, row_like, row_like],
                [IN_VMEM] * len(args), tuple(held(x) for x in args), flops=local_flops,
            )
            from_inner = exchange_inner(to_inner)
        else:
            field, outer, inner = call(
                functools.partial(rim_body, cols, rows), [whole, side, side],
                [IN_VMEM] * len(args), tuple(held(x) for x in args), flops=local_flops // 3,
            )
            rims = exchange_outer(outer), exchange_inner(inner)
        args = [weights, probe_outer, probe_inner, field, outer, inner]
        if level > 1:
            args.append(previous)
        args += [sorted_hop, twice_cos, twice_sin, terms]
        if last:
            args += [same_factor, cross_factor]
        terms, *rest = call(
            functools.partial(local_body, cols, rows, level, last),
            [row_like] if last else [terms_like, whole],
            [IN_VMEM] * len(args), tuple(held(x) for x in args),
            flops=local_flops, moved=hopping.size * 2,
        )
        if not last:
            part = rest[0]

    pairs = [
        [site % sites * peers + peer for site in (2 * i - 1, 2 * i) for peer in range(peers)]
        for i in range(sites // 2)
    ]
    shares = call(
        functools.partial(share_body, cols), [((2 * peers, tiles, width), f32)],
        [IN_SMEM] + [IN_VMEM] * 5,
        (parity, *(held(x) for x in (terms, from_inner, to_outer, same_factor, cross_factor))),
    )[0]
    shares = lax.all_to_all(shares, ("site", "probe"), 0, 0, axis_index_groups=pairs)
    force, largest = call(
        functools.partial(force_body, cols), [row_like, ((sites, 1, 128), f32)],
        [IN_SMEM] + [IN_VMEM] * 3,
        (parity, *(held(x) for x in (shares, same_factor, cross_factor))),
    )
    largest = lax.all_to_all(largest, "site", 0, 0)
    return pl.pallas_call(
        move_body,
        out_shape=[jax.ShapeDtypeStruct(angles.shape, f32)] * 2,
        in_specs=[IN_SMEM] + [IN_VMEM] * 4,
        out_specs=[IN_VMEM] * 2,
    )(parity, held(largest), held(force), held(angles), held(thermal_noise))


def solution(mesh):
    in_specs = (
        P("site", None, None),
        P("site", None, None),
        P("site", None, None),
        P(),
        P("site", None, None, "probe", None),
        P("site", None, None, None, None),
        P("site", None, None),
    )
    out_specs = (P("site", None, None), P("site", None, None))
    return jax.shard_map(local, mesh=mesh, in_specs=in_specs, out_specs=out_specs, check_vma=False)
```

```python
import functools
import jax
import jax.numpy as jnp
from jax import lax
from jax.experimental import pallas as pl
from jax.experimental.pallas import tpu as pltpu
from jax.sharding import PartitionSpec as P

BAND = 8.0
STEP_MAX = 0.3
TWO_TEMP = 0.1

VERT, LEFT, RIGHT, RIM, TURNED = range(5)
IN_VMEM = pl.BlockSpec(memory_space=pltpu.VMEM)
IN_SMEM = pl.BlockSpec(memory_space=pltpu.SMEM)
IN_HBM = pl.BlockSpec(memory_space=pltpu.HBM)


def held(array, space=pltpu.VMEM):
    return pltpu.with_memory_space_constraint(array, space)


def call(body, outs, in_specs, args, scratch=(), flops=0, moved=0):
    return pl.pallas_call(
        body,
        out_shape=[pltpu.VMEM(shape, dtype) for shape, dtype in outs],
        in_specs=in_specs,
        out_specs=[IN_VMEM] * len(outs),
        scratch_shapes=list(scratch),
        compiler_params=pltpu.CompilerParams(vmem_limit_bytes=16 * 1024 * 1024),
        cost_estimate=pl.CostEstimate(flops=flops, bytes_accessed=moved, transcendentals=0),
    )(*args)


def product(vectors, matrix):
    return jnp.dot(vectors, matrix, preferred_element_type=jnp.float32)


def folded(values):
    return jnp.sum(values.reshape(-1, 8, values.shape[-1]), axis=0)


def overlap_terms(probe, vectors):
    half = probe.shape[0] // 2
    upper_r = probe[:half].astype(jnp.float32)
    lower_r = probe[half:].astype(jnp.float32)
    upper_w, lower_w = vectors[:half], vectors[half:]
    same = folded(upper_r * upper_w - lower_r * lower_w)
    cross = folded(upper_r * lower_w + lower_r * upper_w)
    return same, cross


def fetch_body(rows, parity_ref, probes_hbm, angles_hbm, coupling_hbm, hopping_hbm,
               outer_ref, inner_ref, angles_ref, coupling_ref, raw_ref, sems):
    parity = parity_ref[0]
    copies = [
        pltpu.make_async_copy(source, target, sems.at[k])
        for k, (source, target) in enumerate((
            (probes_hbm.at[parity], outer_ref),
            (probes_hbm.at[1 - parity], inner_ref),
            (angles_hbm, angles_ref),
            (coupling_hbm, coupling_ref),
            (hopping_hbm, raw_ref),
        ))
    ]
    for copy in copies:
        copy.start()
    for copy in copies:
        copy.wait()


def local_hop(cols, rows, outer_ref, inner_ref, tile, matrix):
    refs = (outer_ref, inner_ref)
    row, col = divmod(tile, cols)

    def vectors(r, c):
        return refs[r][pl.ds(c * rows, rows), :]

    right, left = (col + 1) % cols, (col - 1) % cols
    total = product(vectors(1 - row, col), matrix(VERT, (1 - row) * cols + col))
    total += product(vectors(row, right), matrix(LEFT, row * cols + right))
    total += product(vectors(row, left), matrix(RIGHT, row * cols + left))
    return total


def kondo(vectors, twice_cos, twice_sin):
    half = vectors.shape[0] // 2
    upper, lower = vectors[:half], vectors[half:]
    return jnp.concatenate(
        [twice_cos * upper + twice_sin * lower, twice_sin * upper - twice_cos * lower], axis=0
    )


def first_body(cols, rows, probe_total, parity_ref, offsets_hbm, coef_hbm, raw_ref, angles_ref,
               coupling_ref, outer_ref, inner_ref, sorted_ref, part_ref, send_ref, pair_ref,
               terms_ref, weights_ref, cos_ref, sin_ref, same_ref, cross_ref,
               offsets_ref, coef_ref, sems):
    tiles = 2 * cols
    slots = offsets_ref.shape[2]
    steps = coef_ref.shape[0]
    parity = parity_ref[0]
    small = [
        pltpu.make_async_copy(offsets_hbm, offsets_ref, sems.at[0]),
        pltpu.make_async_copy(coef_hbm, coef_ref, sems.at[1]),
    ]
    for copy in small:
        copy.start()

    def tile_of(kind, tile):
        row, col = divmod(tile, cols)
        origin = row + parity - 2 * row * parity
        if kind == LEFT:
            code = 3
        elif kind == RIGHT:
            code = 5
        else:
            towards_high = (row == 0) == (kind == VERT)
            code = 7 - 6 * parity if towards_high else 1 + 6 * parity
        slot = jnp.int32(0)
        for k in range(1, slots):
            slot += jnp.where(offsets_ref[origin, col, k] == code, k, 0)
        return (origin * cols + col) * slots + slot

    for row in range(2):
        origin = row + parity - 2 * row * parity
        place = pl.ds(row * cols, cols)
        angles, strength = angles_ref[origin], coupling_ref[origin]
        cosines, sine_values = jnp.cos(angles), jnp.sin(angles)
        scale = (-BAND / probe_total) * strength
        cos_ref[place, :] = 2.0 * strength * cosines
        sin_ref[place, :] = 2.0 * strength * sine_values
        same_ref[place, :] = -scale * sine_values
        cross_ref[place, :] = scale * cosines
    for tile in range(tiles):
        row, col = divmod(tile, cols)
        probe = (outer_ref, inner_ref)[row][pl.ds(col * rows, rows), :]
        terms_ref[tile], terms_ref[tiles + tile] = overlap_terms(
            probe, probe.astype(jnp.float32)
        )
    pair_ref[pl.ds(0, cols * rows), :] = inner_ref[...]
    for copy in small:
        copy.wait()
    for level in range(steps):
        weights_ref[pl.ds(level, 1), :] = jnp.full(
            (1, weights_ref.shape[1]), (level + 1) * coef_ref[level], jnp.float32
        )

    def matrix(kind, tile):
        found = raw_ref[tile_of(kind, tile)]
        sorted_ref[kind * tiles + tile] = found
        return found

    for tile in range(tiles):
        row, col = divmod(tile, cols)
        probe = (outer_ref, inner_ref)[row][pl.ds(col * rows, rows), :].astype(jnp.float32)
        total = local_hop(cols, rows, outer_ref, inner_ref, tile, matrix)
        part = 2.0 * total + kondo(
            probe, cos_ref[pl.ds(tile, 1), :], sin_ref[pl.ds(tile, 1), :]
        )
        part_ref[tile] = part
        low = part.astype(jnp.bfloat16)
        if row == 0:
            send_ref[pl.ds(col * rows, rows), :] = low
        else:
            pair_ref[pl.ds((cols + col) * rows, rows), :] = low
    for tile in range(tiles):
        sorted_ref[TURNED * tiles + tile] = matrix(RIM, tile).T


def rim_vectors(cols, rows, tile, got, half, low, sorted_ref):
    row, col = divmod(tile, cols)
    place = pl.ds(col * rows, rows)
    sent = got[row][pl.ds((half * row * cols + col) * rows, rows), :]
    if low is None:
        return sent
    share = product(low[row][place, :], sorted_ref[RIM * 2 * cols + tile])
    return (sent.astype(jnp.float32) + 2.0 * share).astype(jnp.bfloat16)


def completed(cols, rows, tile, got, half, low, sorted_ref, part_ref):
    rim = rim_vectors(cols, rows, tile, got, half, low, sorted_ref)
    return part_ref[tile] + 2.0 * product(rim, sorted_ref[TURNED * 2 * cols + tile])


def outer_body(cols, rows, level, *refs):
    refs = list(refs)
    got = refs.pop(0), None
    low_before = (refs.pop(0), None) if level > 1 else None
    sorted_ref, part_ref, field_ref, low_ref = refs
    for col in range(cols):
        field = completed(cols, rows, col, got, 0, low_before, sorted_ref, part_ref)
        field_ref[col] = field
        low_ref[pl.ds(col * rows, rows), :] = field.astype(jnp.bfloat16)


def step_body(cols, rows, level, last, *refs):
    tiles = 2 * cols
    refs = list(refs)

    def take(count):
        taken = refs[:count]
        del refs[:count]
        return taken

    probes = take(2)
    got = [None] + take(1)
    low_before, field_before = ([None] + take(1), take(2)) if level > 1 else (None, None)
    sorted_ref, part_ref, terms_ref, weights_ref, cos_ref, sin_ref = take(6)
    field_outer, low_outer = take(2)
    if last:
        same_ref, cross_ref, share_ref, field_inner, low_inner = refs
    else:
        field_inner, low_inner, next_ref, out_ref, send_ref, *pair = refs
    fields, low = (field_outer, field_inner), (low_outer, low_inner)

    for col in range(cols):
        field = completed(
            cols, rows, cols + col, got, (level - 1) % 2, low_before, sorted_ref, part_ref
        )
        field_inner[col] = field
        low_inner[pl.ds(col * rows, rows), :] = field.astype(jnp.bfloat16)

    weight = weights_ref[pl.ds(level, 1), 0:1]
    weight_next = weights_ref[pl.ds(level + 1, 1), 0:1]

    def matrix(kind, source):
        return sorted_ref[kind * tiles + source]

    for tile in range(tiles):
        row, col = divmod(tile, cols)
        place = pl.ds(col * rows, rows)
        probe = probes[row][place, :]
        field = fields[row][col]
        total = local_hop(cols, rows, *low, tile, matrix)
        following = 2.0 * total + kondo(
            field, cos_ref[pl.ds(tile, 1), :], sin_ref[pl.ds(tile, 1), :]
        )
        if field_before is None:
            following -= probe.astype(jnp.float32)
        else:
            following -= field_before[row][col]
        if last:
            same, cross = overlap_terms(probe, weight * field + weight_next * following)
            same = jnp.sum(terms_ref[tile] + same, axis=0, keepdims=True)
            cross = jnp.sum(terms_ref[tiles + tile] + cross, axis=0, keepdims=True)
            one = pl.ds(tile, 1)
            share_ref[one, :] = same_ref[one, :] * same + cross_ref[one, :] * cross
        else:
            next_ref[tile] = following
            if row == 0:
                send_ref[place, :] = following.astype(jnp.bfloat16)
            elif pair:
                pair[0][place, :] = part_ref[tile].astype(jnp.bfloat16)
                pair[0][pl.ds((cols + col) * rows, rows), :] = following.astype(jnp.bfloat16)
            same, cross = overlap_terms(probe, field)
            for at, term in ((tile, same), (tiles + tile, cross)):
                before = weights_ref[0:1, 0:1] * terms_ref[at] if level == 1 else terms_ref[at]
                out_ref[at] = before + weight * term


def last_body(cols, rows, level, probe_outer_ref, probe_inner_ref, got_outer_ref, got_inner_ref,
              low_outer_ref, low_inner_ref, sorted_ref, share_ref, weights_ref, same_ref,
              cross_ref, out_ref):
    tiles = 2 * cols
    weight = 2.0 * weights_ref[pl.ds(level, 1), 0:1]
    got, low = (got_outer_ref, got_inner_ref), (low_outer_ref, low_inner_ref)
    for tile in range(tiles):
        row, col = divmod(tile, cols)
        probe = (probe_outer_ref, probe_inner_ref)[row][pl.ds(col * rows, rows), :]
        rim = rim_vectors(cols, rows, tile, got, (level - 1) % 2, low, sorted_ref)
        same, cross = overlap_terms(probe, product(rim, sorted_ref[TURNED * tiles + tile]))
        same = weight * jnp.sum(same, axis=0, keepdims=True)
        cross = weight * jnp.sum(cross, axis=0, keepdims=True)
        one = pl.ds(tile, 1)
        share = share_ref[one, :] + same_ref[one, :] * same + cross_ref[one, :] * cross
        for peer in range(out_ref.shape[0]):
            out_ref[peer, one, :] = share


def force_body(upper_ref, shares_ref, force_ref, largest_ref):
    peers = shares_ref.shape[0] // 2
    strips = []
    for strip in range(2):
        total = shares_ref[strip * peers]
        for peer in range(1, peers):
            total += shares_ref[strip * peers + peer]
        strips.append(total)
    force_ref[...] = jnp.where(upper_ref[0] == 0, strips[0], strips[1])
    largest = jnp.max(jnp.maximum(jnp.abs(strips[0]), jnp.abs(strips[1])))
    largest_ref[...] = jnp.full(largest_ref.shape, largest, jnp.float32)


def move_body(parity_ref, largest_ref, force_ref, angles_ref, noise_ref, next_ref, out_ref):
    parity = parity_ref[0]
    cols = out_ref.shape[1]
    largest = jnp.max(largest_ref[...])
    step_size = jnp.full((1, 1), STEP_MAX, jnp.float32) / (largest + 1e-06)
    kick = jnp.sqrt(TWO_TEMP * step_size)
    for row in range(2):
        origin = row + parity - 2 * row * parity
        force = force_ref[pl.ds(row * cols, cols), :]
        out_ref[origin] = force
        next_ref[origin] = angles_ref[origin] + step_size * force + kick * noise_ref[origin]


def exchange_outer(outer):
    count = lax.axis_size("site")
    pairs = [(i, (i + 1) % count if i % 2 else (i - 1) % count) for i in range(count)]
    return lax.ppermute(outer, "site", pairs)


def exchange_inner(inner):
    return lax.ppermute(inner, "site", [(i, i ^ 1) for i in range(lax.axis_size("site"))])


def local(angles, coupling, thermal_noise, coefficients, probes, hopping, offsets):
    cols, orbitals, share, width = probes.shape[1:]
    rows = orbitals * share
    tiles = 2 * cols
    steps = coefficients.shape[0] - 1
    f32, bf16 = jnp.float32, jnp.bfloat16
    side = ((cols * rows, width), bf16)
    whole = ((tiles, rows, width), f32)
    terms_like = ((2 * tiles, 8, width), f32)
    probe_total = lax.axis_size("probe") * share

    pair = ((2 * cols * rows, width), bf16)
    row_like = ((tiles, width), f32)
    sites, peers = lax.axis_size("site"), lax.axis_size("probe")
    site = lax.axis_index("site")
    parity = (site % 2).astype(jnp.int32).reshape(1)
    upper = (site // (sites // 2)).astype(jnp.int32).reshape(1)
    raw = hopping.reshape(-1, width, width)
    outer, inner, angles_held, coupling_held, raw_held = call(
        functools.partial(fetch_body, rows),
        [side, side, (angles.shape, f32), (coupling.shape, f32), (raw.shape, bf16)],
        [IN_SMEM] + [IN_HBM] * 4,
        (parity, *(held(x, pltpu.HBM) for x in (
            probes.reshape(2, cols * rows, width), angles, coupling, raw))),
        scratch=[pltpu.SemaphoreType.DMA((5,))],
    )
    probe_rows = [outer, inner]
    from_outer = [exchange_outer(outer)]

    local_flops = 2 * 3 * tiles * rows * width * width
    (sorted_hop, part, send, send_pair, terms, weights, twice_cos, twice_sin, same_factor,
     cross_factor) = call(
        functools.partial(first_body, cols, rows, probe_total),
        [((5 * tiles, width, width), bf16), whole, side, pair, terms_like, ((8, 128), f32)]
        + [row_like] * 4,
        [IN_SMEM] + [IN_HBM] * 2 + [IN_VMEM] * 5,
        (parity, *(held(x, pltpu.HBM) for x in (offsets, coefficients)),
         *(held(x) for x in (raw_held, angles_held, coupling_held, outer, inner))),
        scratch=[
            pltpu.SMEM(offsets.shape, jnp.int32), pltpu.SMEM(coefficients.shape, f32),
            pltpu.SemaphoreType.DMA((2,)),
        ],
        flops=local_flops, moved=hopping.size * 2,
    )
    from_outer.append(exchange_outer(send))
    from_inner = exchange_inner(send_pair)
    rows_of, fields = [probe_rows], None
    row_whole = ((cols, rows, width), f32)
    for level in range(1, steps):
        last = level == steps - 1
        paired = level % 2 == 0
        before = level > 1
        args = [from_outer[level - 1]] + [rows_of[level - 2][0]] * before + [sorted_hop, part]
        field_outer, low_outer = call(
            functools.partial(outer_body, cols, rows, level), [row_whole, side],
            [IN_VMEM] * len(args), tuple(held(x) for x in args),
            flops=0 if paired else 20 * local_flops,
        )
        args = [*probe_rows, from_inner]
        if before:
            args += [rows_of[level - 2][1], *fields]
        args += [sorted_hop, part, terms, weights, twice_cos, twice_sin, field_outer, low_outer]
        if last:
            args += [same_factor, cross_factor]
        outs = call(
            functools.partial(step_body, cols, rows, level, last),
            [row_like] if last else [row_whole, side, whole, terms_like, side] + [pair] * paired,
            [IN_VMEM] * len(args), tuple(held(x) for x in args),
            scratch=[pltpu.VMEM(*row_whole), pltpu.VMEM(*side)] if last else (),
            flops=0 if paired else local_flops,
        )
        if last:
            share = outs[0]
        else:
            field_inner, low_inner, part, terms, send, *send_pair = outs
            fields = field_outer, field_inner
            rows_of.append((low_outer, low_inner))
            from_outer.append(exchange_outer(send))
            if paired:
                from_inner = exchange_inner(send_pair[0])

    args = [*probe_rows, from_outer[steps - 1], from_inner, *rows_of[steps - 2], sorted_hop,
            share, weights, same_factor, cross_factor]
    pairs = [
        [half * peers + peer for half in (i, i + sites // 2) for peer in range(peers)]
        for i in range(sites // 2)
    ]
    shares = call(
        functools.partial(last_body, cols, rows, steps), [((2 * peers, tiles, width), f32)],
        [IN_VMEM] * len(args), tuple(held(x) for x in args), flops=local_flops,
    )[0]
    shares = lax.all_to_all(shares, ("site", "probe"), 0, 0, axis_index_groups=pairs)
    force, largest = call(
        force_body, [row_like, ((sites // 2, 1, 128), f32)],
        [IN_SMEM, IN_VMEM], (upper, held(shares)),
    )
    halves = [list(range(sites // 2)), list(range(sites // 2, sites))]
    largest = lax.all_to_all(largest, "site", 0, 0, axis_index_groups=halves)
    return pl.pallas_call(
        move_body,
        out_shape=[jax.ShapeDtypeStruct(angles.shape, f32)] * 2,
        in_specs=[IN_SMEM] + [IN_VMEM] * 4,
        out_specs=[IN_VMEM] * 2,
    )(parity, held(largest), held(force), held(angles), held(thermal_noise))


def solution(mesh):
    in_specs = (
        P("site", None, None),
        P("site", None, None),
        P("site", None, None),
        P(),
        P("site", None, None, "probe", None),
        P("site", None, None, None, None),
        P("site", None, None),
    )
    out_specs = (P("site", None, None), P("site", None, None))
    return jax.shard_map(local, mesh=mesh, in_specs=in_specs, out_specs=out_specs, check_vma=False)
```

```python
import functools
import jax
import jax.numpy as jnp
from jax import lax
from jax.experimental import pallas as pl
from jax.experimental.pallas import tpu as pltpu
from jax.sharding import PartitionSpec as P

BAND = 8.0
STEP_MAX = 0.3
TWO_TEMP = 0.1

VERT, LEFT, RIGHT, RIM, TURNED = range(5)
IN_VMEM = pl.BlockSpec(memory_space=pltpu.VMEM)
IN_SMEM = pl.BlockSpec(memory_space=pltpu.SMEM)
IN_HBM = pl.BlockSpec(memory_space=pltpu.HBM)


def held(array, space=pltpu.VMEM):
    return pltpu.with_memory_space_constraint(array, space)


def call(body, outs, in_specs, args, scratch=(), flops=0, moved=0):
    return pl.pallas_call(
        body,
        out_shape=[pltpu.VMEM(shape, dtype) for shape, dtype in outs],
        in_specs=in_specs,
        out_specs=[IN_VMEM] * len(outs),
        scratch_shapes=list(scratch),
        compiler_params=pltpu.CompilerParams(vmem_limit_bytes=16 * 1024 * 1024),
        cost_estimate=pl.CostEstimate(flops=flops, bytes_accessed=moved, transcendentals=0),
    )(*args)


def product(vectors, matrix):
    return jnp.dot(vectors, matrix, preferred_element_type=jnp.float32)


def folded(values):
    return jnp.sum(values.reshape(-1, 8, values.shape[-1]), axis=0)


def overlap_terms(probe, vectors):
    half = probe.shape[0] // 2
    upper_r = probe[:half].astype(jnp.float32)
    lower_r = probe[half:].astype(jnp.float32)
    upper_w, lower_w = vectors[:half], vectors[half:]
    same = folded(upper_r * upper_w - lower_r * lower_w)
    cross = folded(upper_r * lower_w + lower_r * upper_w)
    return same, cross


def fetch_body(parity_ref, probes_hbm, angles_hbm, coupling_hbm,
               outer_ref, inner_ref, angles_ref, coupling_ref, sems):
    parity = parity_ref[0]
    copies = [
        pltpu.make_async_copy(source, target, sems.at[k])
        for k, (source, target) in enumerate((
            (probes_hbm.at[parity], outer_ref),
            (probes_hbm.at[1 - parity], inner_ref),
            (angles_hbm, angles_ref),
            (coupling_hbm, coupling_ref),
        ))
    ]
    for copy in copies:
        copy.start()
    for copy in copies:
        copy.wait()


def beside(cols, rows, low_ref, tile, matrix):
    row, col = divmod(tile, cols)
    right, left = (col + 1) % cols, (col - 1) % cols
    return product(
        low_ref[pl.ds(right * rows, rows), :], matrix(LEFT, row * cols + right)
    ) + product(low_ref[pl.ds(left * rows, rows), :], matrix(RIGHT, row * cols + left))


def local_hop(cols, rows, outer_ref, inner_ref, tile, matrix):
    refs = (outer_ref, inner_ref)
    row, col = divmod(tile, cols)
    total = product(
        refs[1 - row][pl.ds(col * rows, rows), :], matrix(VERT, (1 - row) * cols + col)
    )
    return total + beside(cols, rows, refs[row], tile, matrix)


def kondo(vectors, twice_cos, twice_sin):
    half = vectors.shape[0] // 2
    upper, lower = vectors[:half], vectors[half:]
    return jnp.concatenate(
        [twice_cos * upper + twice_sin * lower, twice_sin * upper - twice_cos * lower], axis=0
    )


def first_body(cols, rows, probe_total, parity_ref, offsets_hbm, coef_hbm, raw_ref, angles_ref,
               coupling_ref, outer_ref, inner_ref, sorted_ref, part_ref, send_ref, pair_ref,
               terms_ref, weights_ref, cos_ref, sin_ref, same_ref, cross_ref,
               offsets_ref, coef_ref, sems):
    tiles = 2 * cols
    slots = offsets_ref.shape[2]
    steps = coef_ref.shape[0]
    parity = parity_ref[0]
    small = [
        pltpu.make_async_copy(offsets_hbm, offsets_ref, sems.at[0]),
        pltpu.make_async_copy(coef_hbm, coef_ref, sems.at[1]),
    ]
    for copy in small:
        copy.start()

    def tile_of(kind, tile):
        row, col = divmod(tile, cols)
        origin = row + parity - 2 * row * parity
        if kind == LEFT:
            code = 3
        elif kind == RIGHT:
            code = 5
        else:
            towards_high = (row == 0) == (kind == VERT)
            code = 7 - 6 * parity if towards_high else 1 + 6 * parity
        slot = jnp.int32(0)
        for k in range(1, slots):
            slot += jnp.where(offsets_ref[origin, col, k] == code, k, 0)
        return (origin * cols + col) * slots + slot

    for row in range(2):
        origin = row + parity - 2 * row * parity
        place = pl.ds(row * cols, cols)
        angles, strength = angles_ref[origin], coupling_ref[origin]
        cosines, sine_values = jnp.cos(angles), jnp.sin(angles)
        scale = (-BAND / probe_total) * strength
        cos_ref[place, :] = 2.0 * strength * cosines
        sin_ref[place, :] = 2.0 * strength * sine_values
        same_ref[place, :] = -scale * sine_values
        cross_ref[place, :] = scale * cosines
    for tile in range(tiles):
        row, col = divmod(tile, cols)
        probe = (outer_ref, inner_ref)[row][pl.ds(col * rows, rows), :]
        terms_ref[tile], terms_ref[tiles + tile] = overlap_terms(
            probe, probe.astype(jnp.float32)
        )
    pair_ref[pl.ds(0, cols * rows), :] = inner_ref[...]
    for copy in small:
        copy.wait()
    for level in range(steps):
        weights_ref[pl.ds(level, 1), :] = jnp.full(
            (1, weights_ref.shape[1]), (level + 1) * coef_ref[level], jnp.float32
        )

    def matrix(kind, tile):
        found = raw_ref[tile_of(kind, tile)]
        sorted_ref[kind * tiles + tile] = found
        return found

    for tile in range(tiles):
        row, col = divmod(tile, cols)
        probe = (outer_ref, inner_ref)[row][pl.ds(col * rows, rows), :].astype(jnp.float32)
        total = local_hop(cols, rows, outer_ref, inner_ref, tile, matrix)
        part = 2.0 * total + kondo(
            probe, cos_ref[pl.ds(tile, 1), :], sin_ref[pl.ds(tile, 1), :]
        )
        part_ref[tile] = part
        low = part.astype(jnp.bfloat16)
        if row == 0:
            send_ref[pl.ds(col * rows, rows), :] = low
        else:
            pair_ref[pl.ds((cols + col) * rows, rows), :] = low
    for tile in range(tiles):
        sorted_ref[TURNED * tiles + tile] = matrix(RIM, tile).T


def rim_vectors(cols, rows, tile, got, half, low, sorted_ref):
    row, col = divmod(tile, cols)
    place = pl.ds(col * rows, rows)
    sent = got[row][pl.ds((half * row * cols + col) * rows, rows), :]
    if low is None:
        return sent
    share = product(low[row][place, :], sorted_ref[RIM * 2 * cols + tile])
    return (sent.astype(jnp.float32) + 2.0 * share).astype(jnp.bfloat16)


def completed(cols, rows, tile, got, half, low, sorted_ref, part_ref):
    rim = rim_vectors(cols, rows, tile, got, half, low, sorted_ref)
    return part_ref[tile] + 2.0 * product(rim, sorted_ref[TURNED * 2 * cols + tile])


def outer_body(cols, rows, level, *refs):
    refs = list(refs)
    got = refs.pop(0), None
    low_before = (refs.pop(0), None) if level > 1 else None
    sorted_ref, part_ref, field_ref, low_ref = refs
    for col in range(cols):
        field = completed(cols, rows, col, got, 0, low_before, sorted_ref, part_ref)
        field_ref[col] = field
        low_ref[pl.ds(col * rows, rows), :] = field.astype(jnp.bfloat16)


def step_body(cols, rows, level, *refs):
    tiles = 2 * cols
    refs = list(refs)

    def take(count):
        taken = refs[:count]
        del refs[:count]
        return taken

    probes = take(2)
    got = [None] + take(1)
    low_before, field_before = ([None] + take(1), take(2)) if level > 1 else (None, None)
    sorted_ref, part_ref, terms_ref, weights_ref, cos_ref, sin_ref = take(6)
    field_outer, low_outer, field_inner, low_inner, next_ref, out_ref, send_inner, *pair = refs
    fields, low = (field_outer, field_inner), (low_outer, low_inner)

    for col in range(cols):
        field = completed(
            cols, rows, cols + col, got, (level - 1) % 2, low_before, sorted_ref, part_ref
        )
        field_inner[col] = field
        low_inner[pl.ds(col * rows, rows), :] = field.astype(jnp.bfloat16)

    weight = weights_ref[pl.ds(level, 1), 0:1]

    def matrix(kind, source):
        return sorted_ref[kind * tiles + source]

    for tile in range(tiles):
        row, col = divmod(tile, cols)
        place = pl.ds(col * rows, rows)
        probe = probes[row][place, :]
        field = fields[row][col]
        total = local_hop(cols, rows, *low, tile, matrix)
        following = 2.0 * total + kondo(
            field, cos_ref[pl.ds(tile, 1), :], sin_ref[pl.ds(tile, 1), :]
        )
        if field_before is None:
            following -= probe.astype(jnp.float32)
        else:
            following -= field_before[row][col]
        next_ref[tile] = following
        if row == 1:
            send_inner[place, :] = following.astype(jnp.bfloat16)
        elif pair:
            pair[0][place, :] = part_ref[tile].astype(jnp.bfloat16)
            pair[0][pl.ds((cols + col) * rows, rows), :] = following.astype(jnp.bfloat16)
        same, cross = overlap_terms(probe, field)
        for at, term in ((tile, same), (tiles + tile, cross)):
            before = weights_ref[0:1, 0:1] * terms_ref[at] if level == 1 else terms_ref[at]
            out_ref[at] = before + weight * term


def inner_last_body(cols, rows, level, probe_outer, probe_inner, got_2, got_1, low_2_outer,
                    low_2_inner, low_1_outer, low_1_inner, field_outer, field_inner,
                    sorted_ref, part_ref, terms_ref, weights_ref, cos_ref, sin_ref,
                    out_ref, halo_2_ref, halo_1_ref, low_ref):
    tiles = 2 * cols
    weight = weights_ref[pl.ds(level, 1), 0:1]
    weight_next = weights_ref[pl.ds(level + 1, 1), 0:1]

    def matrix(kind, tile):
        return sorted_ref[kind * tiles + tile]

    fields = []
    for col in range(cols):
        field = completed(
            cols, rows, cols + col, (None, got_2), 0, (None, low_2_inner), sorted_ref, part_ref
        )
        fields.append(field)
        low_ref[pl.ds(col * rows, rows), :] = field.astype(jnp.bfloat16)
    for tile in range(tiles):
        row, col = divmod(tile, cols)
        place = pl.ds(col * rows, rows)
        if row == 0:
            following = 2.0 * product(low_ref[place, :], matrix(VERT, cols + col))
            vectors = weight_next * (following - field_outer[col])
            probe = probe_outer[place, :]
        else:
            rim = rim_vectors(
                cols, rows, tile, (None, got_1), 0, (None, low_1_inner), sorted_ref
            )
            total = beside(cols, rows, low_ref, tile, matrix) + product(rim, matrix(TURNED, tile))
            following = 2.0 * total - field_inner[col] + kondo(
                fields[col], cos_ref[pl.ds(tile, 1), :], sin_ref[pl.ds(tile, 1), :]
            )
            vectors = weight * fields[col] + weight_next * following
            probe = probe_inner[place, :]
        same, cross = overlap_terms(probe, vectors)
        out_ref[tile] = terms_ref[tile] + same
        out_ref[tiles + tile] = terms_ref[tiles + tile] + cross
    for col in range(cols):
        place = pl.ds(col * rows, rows)
        halo_2_ref[col] = 2.0 * product(low_2_outer[place, :], matrix(RIM, col))
        halo_1_ref[col] = 2.0 * product(low_1_outer[place, :], matrix(RIM, col))


def outer_last_body(cols, rows, level, probe_outer, probe_inner, got_ref, halo_2_ref, halo_1_ref,
                    sorted_ref, part_ref, terms_ref, weights_ref, cos_ref, sin_ref, same_ref,
                    cross_ref, out_ref, low_ref, share_ref):
    tiles = 2 * cols
    weight = weights_ref[pl.ds(level, 1), 0:1]
    weight_next = weights_ref[pl.ds(level + 1, 1), 0:1]

    def matrix(kind, tile):
        return sorted_ref[kind * tiles + tile]

    def halo(half, share_ref, col):
        sent = got_ref[pl.ds((half * cols + col) * rows, rows), :].astype(jnp.float32)
        return (sent + share_ref[col]).astype(jnp.bfloat16)

    fields = []
    for col in range(cols):
        field = part_ref[col] + 2.0 * product(halo(0, halo_2_ref, col), matrix(TURNED, col))
        fields.append(field)
        low_ref[pl.ds(col * rows, rows), :] = field.astype(jnp.bfloat16)
    for tile in range(tiles):
        row, col = divmod(tile, cols)
        place = pl.ds(col * rows, rows)
        one = pl.ds(tile, 1)
        if row == 0:
            total = beside(cols, rows, low_ref, tile, matrix)
            total += product(halo(1, halo_1_ref, col), matrix(TURNED, tile))
            following = 2.0 * total + kondo(fields[col], cos_ref[one, :], sin_ref[one, :])
            vectors = weight * fields[col] + weight_next * following
            probe = probe_outer[place, :]
        else:
            vectors = (2.0 * weight_next) * product(low_ref[place, :], matrix(VERT, col))
            probe = probe_inner[place, :]
        same, cross = overlap_terms(probe, vectors)
        same = jnp.sum(terms_ref[tile] + same, axis=0, keepdims=True)
        cross = jnp.sum(terms_ref[tiles + tile] + cross, axis=0, keepdims=True)
        share_ref[one, :] = same_ref[one, :] * same + cross_ref[one, :] * cross
    share = share_ref[...]
    for peer in range(out_ref.shape[0]):
        out_ref[peer] = share


def force_body(upper_ref, shares_ref, force_ref, largest_ref):
    peers = shares_ref.shape[0] // 2
    strips = []
    for strip in range(2):
        total = shares_ref[strip * peers]
        for peer in range(1, peers):
            total += shares_ref[strip * peers + peer]
        strips.append(total)
    force_ref[...] = jnp.where(upper_ref[0] == 0, strips[0], strips[1])
    largest = jnp.max(jnp.maximum(jnp.abs(strips[0]), jnp.abs(strips[1])))
    largest_ref[...] = jnp.full(largest_ref.shape, largest, jnp.float32)


def move_body(parity_ref, largest_ref, force_ref, angles_ref, noise_ref, next_ref, out_ref):
    parity = parity_ref[0]
    cols = out_ref.shape[1]
    largest = jnp.max(largest_ref[...])
    step_size = jnp.full((1, 1), STEP_MAX, jnp.float32) / (largest + 1e-06)
    kick = jnp.sqrt(TWO_TEMP * step_size)
    for row in range(2):
        origin = row + parity - 2 * row * parity
        force = force_ref[pl.ds(row * cols, cols), :]
        out_ref[origin] = force
        next_ref[origin] = angles_ref[origin] + step_size * force + kick * noise_ref[origin]


def exchange_outer(outer):
    count = lax.axis_size("site")
    pairs = [(i, (i + 1) % count if i % 2 else (i - 1) % count) for i in range(count)]
    return lax.ppermute(outer, "site", pairs)


def exchange_inner(inner):
    return lax.ppermute(inner, "site", [(i, i ^ 1) for i in range(lax.axis_size("site"))])


def local(angles, coupling, thermal_noise, coefficients, probes, hopping, offsets):
    cols, orbitals, share, width = probes.shape[1:]
    rows = orbitals * share
    tiles = 2 * cols
    steps = coefficients.shape[0] - 1
    f32, bf16 = jnp.float32, jnp.bfloat16
    side = ((cols * rows, width), bf16)
    whole = ((tiles, rows, width), f32)
    terms_like = ((2 * tiles, 8, width), f32)
    probe_total = lax.axis_size("probe") * share

    pair = ((2 * cols * rows, width), bf16)
    row_like = ((tiles, width), f32)
    sites, peers = lax.axis_size("site"), lax.axis_size("probe")
    site = lax.axis_index("site")
    parity = (site % 2).astype(jnp.int32).reshape(1)
    upper = (site // (sites // 2)).astype(jnp.int32).reshape(1)
    local_flops = 2 * 3 * tiles * rows * width * width
    outer, inner, angles_held, coupling_held = call(
        fetch_body, [side, side, (angles.shape, f32), (coupling.shape, f32)],
        [IN_SMEM] + [IN_HBM] * 3,
        (parity, *(held(x, pltpu.HBM) for x in (
            probes.reshape(2, cols * rows, width), angles, coupling))),
        scratch=[pltpu.SemaphoreType.DMA((4,))], flops=20 * local_flops,
    )
    probe_rows = [outer, inner]
    from_outer = [exchange_outer(outer)]

    (sorted_hop, part, send, send_pair, terms, weights, twice_cos, twice_sin, same_factor,
     cross_factor) = call(
        functools.partial(first_body, cols, rows, probe_total),
        [((5 * tiles, width, width), bf16), whole, side, pair, terms_like, ((8, 128), f32)]
        + [row_like] * 4,
        [IN_SMEM] + [IN_HBM] * 2 + [IN_VMEM] * 5,
        (parity, *(held(x, pltpu.HBM) for x in (offsets, coefficients)),
         *(held(x) for x in (hopping.reshape(-1, width, width), angles_held, coupling_held, outer, inner))),
        scratch=[
            pltpu.SMEM(offsets.shape, jnp.int32), pltpu.SMEM(coefficients.shape, f32),
            pltpu.SemaphoreType.DMA((2,)),
        ],
        flops=local_flops, moved=hopping.size * 2,
    )
    from_outer.append(exchange_outer(send))
    from_inner = exchange_inner(send_pair)
    rows_of, fields, later_inner = [probe_rows], None, []
    row_whole = ((cols, rows, width), f32)
    for level in range(1, steps - 1):
        paired = level % 2 == 0
        before = level > 1
        args = [from_outer[level - 1]] + [rows_of[level - 2][0]] * before + [sorted_hop, part]
        field_outer, low_outer = call(
            functools.partial(outer_body, cols, rows, level), [row_whole, side],
            [IN_VMEM] * len(args), tuple(held(x) for x in args),
            flops=0 if paired else 20 * local_flops,
        )
        args = [*probe_rows, from_inner]
        if before:
            args += [rows_of[level - 2][1], *fields]
        args += [sorted_hop, part, terms, weights, twice_cos, twice_sin, field_outer, low_outer]
        field_inner, low_inner, part, terms, send_inner, *send_pair = call(
            functools.partial(step_body, cols, rows, level),
            [row_whole, side, whole, terms_like, side] + [pair] * paired,
            [IN_VMEM] * len(args), tuple(held(x) for x in args), flops=local_flops,
        )
        fields = field_outer, field_inner
        rows_of.append((low_outer, low_inner))
        if paired:
            from_outer.append(exchange_outer(send_pair[0]))
        later_inner.append(exchange_inner(send_inner))

    level = steps - 1
    args = [*probe_rows, *later_inner, *rows_of[level - 2], *rows_of[level - 1], *fields,
            sorted_hop, part, terms, weights, twice_cos, twice_sin]
    terms, halo_2, halo_1 = call(
        functools.partial(inner_last_body, cols, rows, level), [terms_like, row_whole, row_whole],
        [IN_VMEM] * len(args), tuple(held(x) for x in args),
        scratch=[pltpu.VMEM(*side)],
    )
    args = [*probe_rows, from_outer[-1], halo_2, halo_1, sorted_hop, part, terms, weights,
            twice_cos, twice_sin, same_factor, cross_factor]
    shares = call(
        functools.partial(outer_last_body, cols, rows, level), [((2 * peers, tiles, width), f32)],
        [IN_VMEM] * len(args), tuple(held(x) for x in args),
        scratch=[pltpu.VMEM(*side), pltpu.VMEM(*row_like)], flops=local_flops,
    )[0]
    pairs = [
        [half * peers + peer for half in (i, i + sites // 2) for peer in range(peers)]
        for i in range(sites // 2)
    ]
    shares = lax.all_to_all(shares, ("site", "probe"), 0, 0, axis_index_groups=pairs)
    force, largest = call(
        force_body, [row_like, ((sites // 2, 1, 128), f32)],
        [IN_SMEM, IN_VMEM], (upper, held(shares)),
    )
    halves = [list(range(sites // 2)), list(range(sites // 2, sites))]
    largest = lax.all_to_all(largest, "site", 0, 0, axis_index_groups=halves)
    return pl.pallas_call(
        move_body,
        out_shape=[jax.ShapeDtypeStruct(angles.shape, f32)] * 2,
        in_specs=[IN_SMEM] + [IN_VMEM] * 4,
        out_specs=[IN_VMEM] * 2,
    )(parity, held(largest), held(force), held(angles), held(thermal_noise))


def solution(mesh):
    in_specs = (
        P("site", None, None),
        P("site", None, None),
        P("site", None, None),
        P(),
        P("site", None, None, "probe", None),
        P("site", None, None, None, None),
        P("site", None, None),
    )
    out_specs = (P("site", None, None), P("site", None, None))
    return jax.shard_map(local, mesh=mesh, in_specs=in_specs, out_specs=out_specs, check_vma=False)
```

```python
import functools
import jax
import jax.numpy as jnp
from jax import lax
from jax.experimental import pallas as pl
from jax.experimental.pallas import tpu as pltpu
from jax.sharding import PartitionSpec as P

BAND = 8.0
STEP_MAX = 0.3
TWO_TEMP = 0.1

VERT, LEFT, RIGHT, RIM = range(4)
IN_VMEM = pl.BlockSpec(memory_space=pltpu.VMEM)
IN_SMEM = pl.BlockSpec(memory_space=pltpu.SMEM)
IN_HBM = pl.BlockSpec(memory_space=pltpu.HBM)


def held(array, space=pltpu.VMEM):
    return pltpu.with_memory_space_constraint(array, space)


def call(body, outs, in_specs, args, scratch=(), flops=0, moved=0):
    return pl.pallas_call(
        body,
        out_shape=[pltpu.VMEM(shape, dtype) for shape, dtype in outs],
        in_specs=in_specs,
        out_specs=[IN_VMEM] * len(outs),
        scratch_shapes=list(scratch),
        compiler_params=pltpu.CompilerParams(vmem_limit_bytes=16 * 1024 * 1024),
        cost_estimate=pl.CostEstimate(flops=flops, bytes_accessed=moved, transcendentals=0),
    )(*args)


def product(vectors, matrix):
    return jnp.dot(vectors, matrix, preferred_element_type=jnp.float32)


def folded(values):
    return jnp.sum(values.reshape(-1, 8, values.shape[-1]), axis=0)


def overlap_terms(probe, vectors):
    half = probe.shape[0] // 2
    upper_r = probe[:half].astype(jnp.float32)
    lower_r = probe[half:].astype(jnp.float32)
    upper_w, lower_w = vectors[:half], vectors[half:]
    same = folded(upper_r * upper_w - lower_r * lower_w)
    cross = folded(upper_r * lower_w + lower_r * upper_w)
    return same, cross


def fetch_body(parity_ref, probes_hbm, offsets_hbm, coef_hbm, angles_hbm, coupling_hbm,
               outer_ref, inner_ref, offsets_ref, coef_ref, angles_ref, coupling_ref, sems):
    parity = parity_ref[0]
    copies = [
        pltpu.make_async_copy(source, target, sems.at[k])
        for k, (source, target) in enumerate((
            (probes_hbm.at[parity], outer_ref),
            (probes_hbm.at[1 - parity], inner_ref),
            (offsets_hbm, offsets_ref),
            (coef_hbm, coef_ref),
            (angles_hbm, angles_ref),
            (coupling_hbm, coupling_ref),
        ))
    ]
    for copy in copies:
        copy.start()
    for copy in copies:
        copy.wait()


def beside(cols, rows, low_ref, tile, matrix):
    row, col = divmod(tile, cols)
    right, left = (col + 1) % cols, (col - 1) % cols
    return product(
        low_ref[pl.ds(right * rows, rows), :], matrix(LEFT, row * cols + right)
    ) + product(low_ref[pl.ds(left * rows, rows), :], matrix(RIGHT, row * cols + left))


def local_hop(cols, rows, outer_ref, inner_ref, tile, matrix):
    refs = (outer_ref, inner_ref)
    row, col = divmod(tile, cols)
    total = product(
        refs[1 - row][pl.ds(col * rows, rows), :], matrix(VERT, (1 - row) * cols + col)
    )
    return total + beside(cols, rows, refs[row], tile, matrix)


def kondo(vectors, twice_cos, twice_sin):
    half = vectors.shape[0] // 2
    upper, lower = vectors[:half], vectors[half:]
    return jnp.concatenate(
        [twice_cos * upper + twice_sin * lower, twice_sin * upper - twice_cos * lower], axis=0
    )


def first_body(cols, rows, probe_total, parity_ref, offsets_ref, coef_ref, raw_ref, angles_ref,
               coupling_ref, outer_ref, inner_ref, sorted_ref, part_outer, part_inner, send_ref,
               pair_ref, weights_ref, cos_ref, sin_ref, same_ref, cross_ref):
    tiles = 2 * cols
    slots = offsets_ref.shape[2]
    parity = parity_ref[0]

    def tile_of(kind, tile):
        row, col = divmod(tile, cols)
        origin = row + parity - 2 * row * parity
        if kind == LEFT:
            code = 3
        elif kind == RIGHT:
            code = 5
        else:
            towards_high = (row == 0) == (kind == VERT)
            code = 7 - 6 * parity if towards_high else 1 + 6 * parity
        slot = jnp.int32(0)
        for k in range(1, slots):
            slot += jnp.where(offsets_ref[origin, col, k] == code, k, 0)
        return (origin * cols + col) * slots + slot

    def matrix(kind, tile):
        found = raw_ref[tile_of(kind, tile)]
        sorted_ref[kind * tiles + tile] = found
        return found

    for row in range(2):
        origin = row + parity - 2 * row * parity
        place = pl.ds(row * cols, cols)
        angles, strength = angles_ref[origin], coupling_ref[origin]
        cosines, sine_values = jnp.cos(angles), jnp.sin(angles)
        scale = (-BAND / probe_total) * strength
        cos_ref[place, :] = 2.0 * strength * cosines
        sin_ref[place, :] = 2.0 * strength * sine_values
        same_ref[place, :] = -scale * sine_values
        cross_ref[place, :] = scale * cosines
    for level in range(coef_ref.shape[0]):
        weights_ref[pl.ds(level, 1), :] = jnp.full(
            (1, weights_ref.shape[1]), (level + 1) * coef_ref[level], jnp.float32
        )
    for tile in range(tiles):
        row, col = divmod(tile, cols)
        place = pl.ds(col * rows, rows)
        probe = (outer_ref, inner_ref)[row][place, :]
        total = local_hop(cols, rows, outer_ref, inner_ref, tile, matrix)
        part = 2.0 * total + kondo(
            probe.astype(jnp.float32), cos_ref[pl.ds(tile, 1), :], sin_ref[pl.ds(tile, 1), :]
        )
        (part_outer, part_inner)[row][col] = part
        if row == 0:
            send_ref[place, :] = part.astype(jnp.bfloat16)
        else:
            pair_ref[place, :] = probe
            pair_ref[pl.ds((cols + col) * rows, rows), :] = part.astype(jnp.bfloat16)
    for tile in range(tiles):
        matrix(RIM, tile)


def first_outer_body(cols, rows, got_ref, sorted_ref, part_ref, field_ref, low_ref, turned_ref):
    for col in range(cols):
        place = pl.ds(col * rows, rows)
        turned = sorted_ref[RIM * 2 * cols + col].T
        turned_ref[col] = turned
        field = part_ref[col] + 2.0 * product(got_ref[place, :], turned)
        field_ref[col] = field
        low_ref[place, :] = field.astype(jnp.bfloat16)


def first_inner_body(cols, rows, probe_outer, probe_inner, got_ref, sorted_ref, part_ref,
                     weights_ref, cos_ref, sin_ref, field_outer, low_outer,
                     field_inner, low_inner, part_outer, part_inner, send_ref, terms_ref,
                     turned_ref):
    tiles = 2 * cols
    fields, low, probes = (field_outer, field_inner), (low_outer, low_inner), (probe_outer, probe_inner)
    for col in range(cols):
        place = pl.ds(col * rows, rows)
        turned = sorted_ref[RIM * tiles + cols + col].T
        turned_ref[col] = turned
        field = part_ref[col] + 2.0 * product(got_ref[place, :], turned)
        field_inner[col] = field
        low_inner[place, :] = field.astype(jnp.bfloat16)

    def matrix(kind, source):
        return sorted_ref[kind * tiles + source]

    for tile in range(tiles):
        row, col = divmod(tile, cols)
        place = pl.ds(col * rows, rows)
        probe_low = probes[row][place, :]
        probe = probe_low.astype(jnp.float32)
        field = fields[row][col]
        total = local_hop(cols, rows, *low, tile, matrix)
        following = 2.0 * total - probe + kondo(
            field, cos_ref[pl.ds(tile, 1), :], sin_ref[pl.ds(tile, 1), :]
        )
        (part_outer, part_inner)[row][col] = following
        if row == 1:
            send_ref[place, :] = following.astype(jnp.bfloat16)
        terms_ref[tile], terms_ref[tiles + tile] = overlap_terms(
            probe_low, weights_ref[0:1, 0:1] * probe + weights_ref[1:2, 0:1] * field
        )


def second_inner_body(cols, rows, probe_outer, probe_inner, got_ref, sorted_ref, turned_ref,
                      part_ref, field_ref, low_ref, share_ref, vert_ref):
    tiles = 2 * cols
    for col in range(cols):
        place = pl.ds(col * rows, rows)
        own = 2.0 * product(probe_inner[place, :], sorted_ref[RIM * tiles + cols + col])
        sent = got_ref[pl.ds((cols + col) * rows, rows), :].astype(jnp.float32)
        rim = (sent + own).astype(jnp.bfloat16)
        field = part_ref[col] + 2.0 * product(rim, turned_ref[col])
        field_ref[col] = field
        low = field.astype(jnp.bfloat16)
        low_ref[place, :] = low
        vert_ref[col] = 2.0 * product(low, sorted_ref[VERT * tiles + cols + col])
        share_ref[col] = 2.0 * product(probe_outer[place, :], sorted_ref[RIM * tiles + col])


def second_outer_body(cols, rows, got_ref, share_ref, vert_ref, sorted_ref, turned_ref, part_ref,
                      field_before, cos_ref, sin_ref, field_ref, low_ref, next_ref, pair_ref):
    tiles = 2 * cols
    for col in range(cols):
        place = pl.ds(col * rows, rows)
        rim = (got_ref[place, :].astype(jnp.float32) + share_ref[col]).astype(jnp.bfloat16)
        field = part_ref[col] + 2.0 * product(rim, turned_ref[col])
        field_ref[col] = field
        low_ref[place, :] = field.astype(jnp.bfloat16)

    def matrix(kind, source):
        return sorted_ref[kind * tiles + source]

    for col in range(cols):
        following = 2.0 * beside(cols, rows, low_ref, col, matrix) + vert_ref[col] + kondo(
            field_ref[col], cos_ref[pl.ds(col, 1), :], sin_ref[pl.ds(col, 1), :]
        ) - field_before[col]
        next_ref[col] = following
        pair_ref[pl.ds(col * rows, rows), :] = part_ref[col].astype(jnp.bfloat16)
        pair_ref[pl.ds((cols + col) * rows, rows), :] = following.astype(jnp.bfloat16)


def second_rest_body(cols, rows, probe_outer, probe_inner, sorted_ref, terms_ref, weights_ref,
                     cos_ref, sin_ref, field_outer, field_inner, low_outer, low_inner,
                     field_before, next_ref, send_ref, out_ref):
    tiles = 2 * cols

    def matrix(kind, source):
        return sorted_ref[kind * tiles + source]

    for col in range(cols):
        tile = cols + col
        place = pl.ds(col * rows, rows)
        total = local_hop(cols, rows, low_outer, low_inner, tile, matrix)
        following = 2.0 * total - field_before[col] + kondo(
            field_inner[col], cos_ref[pl.ds(tile, 1), :], sin_ref[pl.ds(tile, 1), :]
        )
        next_ref[col] = following
        send_ref[place, :] = following.astype(jnp.bfloat16)
    weight = weights_ref[2:3, 0:1]
    for tile in range(tiles):
        row, col = divmod(tile, cols)
        probe = (probe_outer, probe_inner)[row][pl.ds(col * rows, rows), :]
        same, cross = overlap_terms(probe, (field_outer, field_inner)[row][col])
        out_ref[tile] = terms_ref[tile] + weight * same
        out_ref[tiles + tile] = terms_ref[tiles + tile] + weight * cross


def last_inner_body(cols, rows, probe_outer, probe_inner, got_2, got_3, low_1_outer, low_1_inner,
                    low_2_outer, low_2_inner, field_outer, field_inner, sorted_ref, turned_ref,
                    part_ref, terms_ref, weights_ref, cos_ref, sin_ref,
                    out_ref, halo_2_ref, halo_3_ref, low_ref):
    tiles = 2 * cols
    weight, weight_next = weights_ref[3:4, 0:1], weights_ref[4:5, 0:1]

    def matrix(kind, tile):
        return sorted_ref[kind * tiles + tile]

    def rim(got_ref, low_before, col):
        place = pl.ds(col * rows, rows)
        own = 2.0 * product(low_before[place, :], matrix(RIM, cols + col))
        return (got_ref[place, :].astype(jnp.float32) + own).astype(jnp.bfloat16)

    fields = []
    for col in range(cols):
        field = part_ref[col] + 2.0 * product(rim(got_2, low_1_inner, col), turned_ref[col])
        fields.append(field)
        low_ref[pl.ds(col * rows, rows), :] = field.astype(jnp.bfloat16)
    for tile in range(tiles):
        row, col = divmod(tile, cols)
        place = pl.ds(col * rows, rows)
        if row == 0:
            following = 2.0 * product(low_ref[place, :], matrix(VERT, cols + col))
            vectors = weight_next * (following - field_outer[col])
            probe = probe_outer[place, :]
        else:
            total = beside(cols, rows, low_ref, tile, matrix)
            total += product(rim(got_3, low_2_inner, col), turned_ref[col])
            following = 2.0 * total - field_inner[col] + kondo(
                fields[col], cos_ref[pl.ds(tile, 1), :], sin_ref[pl.ds(tile, 1), :]
            )
            vectors = weight * fields[col] + weight_next * following
            probe = probe_inner[place, :]
        same, cross = overlap_terms(probe, vectors)
        out_ref[tile] = terms_ref[tile] + same
        out_ref[tiles + tile] = terms_ref[tiles + tile] + cross
    for col in range(cols):
        place = pl.ds(col * rows, rows)
        halo_2_ref[col] = 2.0 * product(low_1_outer[place, :], matrix(RIM, col))
        halo_3_ref[col] = 2.0 * product(low_2_outer[place, :], matrix(RIM, col))


def row_sums(blocks):
    index = lax.broadcasted_iota(jnp.int32, blocks[0].shape, 0)
    shift = 4
    while shift:
        low = (index & shift) == 0
        half = len(blocks) // 2
        joined = []
        for first, second in zip(blocks[:half], blocks[half:]):
            kept, moved = jnp.where(low, first, second), jnp.where(low, second, first)
            down = pltpu.roll(moved, shift, 0)
            if shift == 4:
                joined.append(kept + down)
            else:
                joined.append(kept + jnp.where(low, pltpu.roll(moved, 8 - shift, 0), down))
        blocks = joined
        shift //= 2
    return blocks[0]


def last_outer_body(cols, rows, probe_outer, probe_inner, got_ref, halo_2_ref, halo_3_ref,
                    sorted_ref, turned_ref, part_ref, terms_ref, weights_ref, cos_ref, sin_ref,
                    same_ref, cross_ref, out_ref, low_ref):
    tiles = 2 * cols
    weight, weight_next = weights_ref[3:4, 0:1], weights_ref[4:5, 0:1]

    def matrix(kind, tile):
        return sorted_ref[kind * tiles + tile]

    def halo(half, share_ref, col):
        sent = got_ref[pl.ds((half * cols + col) * rows, rows), :].astype(jnp.float32)
        return (sent + share_ref[col]).astype(jnp.bfloat16)

    fields = []
    for col in range(cols):
        field = part_ref[col] + 2.0 * product(halo(0, halo_2_ref, col), turned_ref[col])
        fields.append(field)
        low_ref[pl.ds(col * rows, rows), :] = field.astype(jnp.bfloat16)
    shares = []
    for tile in range(tiles):
        row, col = divmod(tile, cols)
        place = pl.ds(col * rows, rows)
        one = pl.ds(tile, 1)
        if row == 0:
            total = beside(cols, rows, low_ref, tile, matrix)
            total += product(halo(1, halo_3_ref, col), turned_ref[col])
            following = 2.0 * total + kondo(fields[col], cos_ref[one, :], sin_ref[one, :])
            vectors = weight * fields[col] + weight_next * following
            probe = probe_outer[place, :]
        else:
            vectors = (2.0 * weight_next) * product(low_ref[place, :], matrix(VERT, col))
            probe = probe_inner[place, :]
        same, cross = overlap_terms(probe, vectors)
        shares.append(
            same_ref[one, :] * (terms_ref[tile] + same)
            + cross_ref[one, :] * (terms_ref[tiles + tile] + cross)
        )
    share = row_sums(shares)
    for peer in range(out_ref.shape[0]):
        out_ref[peer] = share


def force_body(upper_ref, shares_ref, force_ref, largest_ref):
    peers = shares_ref.shape[0] // 2
    strips = []
    for strip in range(2):
        total = shares_ref[strip * peers]
        for peer in range(1, peers):
            total += shares_ref[strip * peers + peer]
        strips.append(total)
    force_ref[...] = jnp.where(upper_ref[0] == 0, strips[0], strips[1])
    largest = jnp.max(jnp.maximum(jnp.abs(strips[0]), jnp.abs(strips[1])))
    largest_ref[...] = jnp.full(largest_ref.shape, largest, jnp.float32)


def move_body(parity_ref, largest_ref, force_ref, angles_ref, noise_ref, next_ref, out_ref):
    parity = parity_ref[0]
    cols = out_ref.shape[1]
    largest = jnp.max(largest_ref[...])
    step_size = jnp.full((1, 1), STEP_MAX, jnp.float32) / (largest + 1e-06)
    kick = jnp.sqrt(TWO_TEMP * step_size)
    for row in range(2):
        origin = row + parity - 2 * row * parity
        force = force_ref[pl.ds(row * cols, cols), :]
        out_ref[origin] = force
        next_ref[origin] = angles_ref[origin] + step_size * force + kick * noise_ref[origin]


def exchange_outer(outer):
    count = lax.axis_size("site")
    pairs = [(i, (i + 1) % count if i % 2 else (i - 1) % count) for i in range(count)]
    return lax.ppermute(outer, "site", pairs)


def exchange_inner(inner):
    return lax.ppermute(inner, "site", [(i, i ^ 1) for i in range(lax.axis_size("site"))])


def local(angles, coupling, thermal_noise, coefficients, probes, hopping, offsets):
    cols, orbitals, share, width = probes.shape[1:]
    rows = orbitals * share
    tiles = 2 * cols
    f32, bf16 = jnp.float32, jnp.bfloat16
    side = ((cols * rows, width), bf16)
    pair = ((2 * cols * rows, width), bf16)
    row = ((cols, rows, width), f32)
    matrices = ((cols, width, width), bf16)
    terms_like = ((2 * tiles, 8, width), f32)
    row_like = ((tiles, width), f32)
    sites, peers = lax.axis_size("site"), lax.axis_size("probe")
    probe_total = peers * share
    local_flops = 2 * 3 * tiles * rows * width * width
    site = lax.axis_index("site")
    parity = (site % 2).astype(jnp.int32).reshape(1)
    upper = (site // (sites // 2)).astype(jnp.int32).reshape(1)

    def run(body, outs, args, scratch=(), flops=0):
        return call(
            functools.partial(body, cols, rows), outs, [IN_VMEM] * len(args),
            tuple(held(x) for x in args), scratch=scratch, flops=flops,
        )

    fetched = pl.pallas_call(
        fetch_body,
        out_shape=[
            pltpu.VMEM(*side), pltpu.VMEM(*side), pltpu.SMEM(offsets.shape, jnp.int32),
            pltpu.SMEM(coefficients.shape, f32), pltpu.VMEM(angles.shape, f32),
            pltpu.VMEM(coupling.shape, f32),
        ],
        in_specs=[IN_SMEM] + [IN_HBM] * 5,
        out_specs=[IN_VMEM, IN_VMEM, IN_SMEM, IN_SMEM, IN_VMEM, IN_VMEM],
        scratch_shapes=[pltpu.SemaphoreType.DMA((6,))],
        compiler_params=pltpu.CompilerParams(vmem_limit_bytes=16 * 1024 * 1024),
        cost_estimate=pl.CostEstimate(flops=20 * local_flops, bytes_accessed=0, transcendentals=0),
    )(parity, *(held(x, pltpu.HBM) for x in (
        probes.reshape(2, cols * rows, width), offsets, coefficients, angles, coupling)))
    outer, inner, offsets_held, coef_held, angles_held, coupling_held = fetched
    probe_rows = [outer, inner]
    got_0 = exchange_outer(outer)

    (sorted_hop, part_outer, part_inner, send, send_pair, weights, twice_cos, twice_sin,
     same_factor, cross_factor) = call(
        functools.partial(first_body, cols, rows, probe_total),
        [((4 * tiles, width, width), bf16), row, row, side, pair, ((8, 128), f32)]
        + [row_like] * 4,
        [IN_SMEM] * 3 + [IN_VMEM] * 5,
        (parity, held(offsets_held, pltpu.SMEM), held(coef_held, pltpu.SMEM),
         *(held(x) for x in (hopping.reshape(-1, width, width), angles_held, coupling_held,
                             outer, inner))),
        flops=local_flops, moved=hopping.size * 2,
    )
    got_1 = exchange_outer(send)
    from_inner = exchange_inner(send_pair)
    trig = [twice_cos, twice_sin]

    field_1_outer, low_1_outer, turned_outer = run(
        first_outer_body, [row, side, matrices], [got_0, sorted_hop, part_outer],
        flops=20 * local_flops,
    )
    (field_1_inner, low_1_inner, part_outer, part_inner, send, terms, turned_inner) = run(
        first_inner_body, [row, side, row, row, side, terms_like, matrices],
        [*probe_rows, from_inner, sorted_hop, part_inner, weights, *trig,
         field_1_outer, low_1_outer],
        flops=local_flops,
    )
    inner_2 = exchange_inner(send)
    field_2_inner, low_2_inner, rim_share, vert = run(
        second_inner_body, [row, side, row, row],
        [*probe_rows, from_inner, sorted_hop, turned_inner, part_inner],
    )
    field_2_outer, low_2_outer, part_outer, send_pair = run(
        second_outer_body, [row, side, row, pair],
        [got_1, rim_share, vert, sorted_hop, turned_outer, part_outer, field_1_outer, *trig],
    )
    got_pair = exchange_outer(send_pair)
    part_inner, send, terms = run(
        second_rest_body, [row, side, terms_like],
        [*probe_rows, sorted_hop, terms, weights, *trig, field_2_outer, field_2_inner,
         low_2_outer, low_2_inner, field_1_inner],
    )
    inner_3 = exchange_inner(send)
    terms, halo_2, halo_3 = run(
        last_inner_body, [terms_like, row, row],
        [*probe_rows, inner_2, inner_3, low_1_outer, low_1_inner, low_2_outer, low_2_inner,
         field_2_outer, field_2_inner, sorted_hop, turned_inner, part_inner, terms, weights,
         *trig],
        scratch=[pltpu.VMEM(*side)],
    )
    shares = run(
        last_outer_body, [((2 * peers, tiles, width), f32)],
        [*probe_rows, got_pair, halo_2, halo_3, sorted_hop, turned_outer, part_outer, terms,
         weights, *trig, same_factor, cross_factor],
        scratch=[pltpu.VMEM(*side)], flops=local_flops,
    )[0]
    pairs = [
        [half * peers + peer for half in (i, i + sites // 2) for peer in range(peers)]
        for i in range(sites // 2)
    ]
    shares = lax.all_to_all(shares, ("site", "probe"), 0, 0, axis_index_groups=pairs)
    force, largest = call(
        force_body, [row_like, ((sites // 2, 1, 128), f32)],
        [IN_SMEM, IN_VMEM], (upper, held(shares)),
    )
    halves = [list(range(sites // 2)), list(range(sites // 2, sites))]
    largest = lax.all_to_all(largest, "site", 0, 0, axis_index_groups=halves)
    return pl.pallas_call(
        move_body,
        out_shape=[jax.ShapeDtypeStruct(angles.shape, f32)] * 2,
        in_specs=[IN_SMEM] + [IN_VMEM] * 4,
        out_specs=[IN_VMEM] * 2,
    )(parity, held(largest), held(force), held(angles), held(thermal_noise))


def solution(mesh):
    in_specs = (
        P("site", None, None),
        P("site", None, None),
        P("site", None, None),
        P(),
        P("site", None, None, "probe", None),
        P("site", None, None, None, None),
        P("site", None, None),
    )
    out_specs = (P("site", None, None), P("site", None, None))
    return jax.shard_map(local, mesh=mesh, in_specs=in_specs, out_specs=out_specs, check_vma=False)
```

```python
import functools
import jax
import jax.numpy as jnp
from jax import lax
from jax.experimental import pallas as pl
from jax.experimental.pallas import tpu as pltpu
from jax.sharding import PartitionSpec as P

BAND = 8.0
STEP_MAX = 0.3
TWO_TEMP = 0.1

VERT, LEFT, RIGHT, RIM = range(4)
IN_VMEM = pl.BlockSpec(memory_space=pltpu.VMEM)
IN_SMEM = pl.BlockSpec(memory_space=pltpu.SMEM)
IN_HBM = pl.BlockSpec(memory_space=pltpu.HBM)


def held(array, space=pltpu.VMEM):
    return pltpu.with_memory_space_constraint(array, space)


def call(body, outs, in_specs, args, scratch=(), flops=0, moved=0):
    return pl.pallas_call(
        body,
        out_shape=[pltpu.VMEM(shape, dtype) for shape, dtype in outs],
        in_specs=in_specs,
        out_specs=[IN_VMEM] * len(outs),
        scratch_shapes=list(scratch),
        compiler_params=pltpu.CompilerParams(vmem_limit_bytes=16 * 1024 * 1024),
        cost_estimate=pl.CostEstimate(flops=flops, bytes_accessed=moved, transcendentals=0),
    )(*args)


def product(vectors, matrix):
    return jnp.dot(vectors, matrix, preferred_element_type=jnp.float32)


def folded(values):
    return jnp.sum(values.reshape(-1, 8, values.shape[-1]), axis=0)


def overlap_terms(probe, vectors):
    half = probe.shape[0] // 2
    upper_r = probe[:half].astype(jnp.float32)
    lower_r = probe[half:].astype(jnp.float32)
    upper_w, lower_w = vectors[:half], vectors[half:]
    same = folded(upper_r * upper_w - lower_r * lower_w)
    cross = folded(upper_r * lower_w + lower_r * upper_w)
    return same, cross


def fetch_body(parity_ref, probes_hbm, offsets_hbm, coef_hbm, angles_hbm, coupling_hbm,
               outer_ref, inner_ref, offsets_ref, coef_ref, angles_ref, coupling_ref, sems):
    parity = parity_ref[0]
    copies = [
        pltpu.make_async_copy(source, target, sems.at[k])
        for k, (source, target) in enumerate((
            (probes_hbm.at[parity], outer_ref),
            (probes_hbm.at[1 - parity], inner_ref),
            (offsets_hbm, offsets_ref),
            (coef_hbm, coef_ref),
            (angles_hbm, angles_ref),
            (coupling_hbm, coupling_ref),
        ))
    ]
    for copy in copies:
        copy.start()
    for copy in copies:
        copy.wait()


def beside(cols, rows, low_ref, tile, matrix):
    row, col = divmod(tile, cols)
    right, left = (col + 1) % cols, (col - 1) % cols
    return product(
        low_ref[pl.ds(right * rows, rows), :], matrix(LEFT, row * cols + right)
    ) + product(low_ref[pl.ds(left * rows, rows), :], matrix(RIGHT, row * cols + left))


def local_hop(cols, rows, outer_ref, inner_ref, tile, matrix):
    refs = (outer_ref, inner_ref)
    row, col = divmod(tile, cols)
    total = product(
        refs[1 - row][pl.ds(col * rows, rows), :], matrix(VERT, (1 - row) * cols + col)
    )
    return total + beside(cols, rows, refs[row], tile, matrix)


def kondo(vectors, twice_cos, twice_sin):
    half = vectors.shape[0] // 2
    upper, lower = vectors[:half], vectors[half:]
    return jnp.concatenate(
        [twice_cos * upper + twice_sin * lower, twice_sin * upper - twice_cos * lower], axis=0
    )


def first_body(cols, rows, probe_total, parity_ref, offsets_ref, coef_ref, raw_ref, angles_ref,
               coupling_ref, outer_ref, inner_ref, sorted_ref, part_outer, part_inner, send_ref,
               pair_ref, weights_ref, cos_ref, sin_ref, same_ref, cross_ref):
    tiles = 2 * cols
    slots = offsets_ref.shape[2]
    parity = parity_ref[0]

    def tile_of(kind, tile):
        row, col = divmod(tile, cols)
        origin = row + parity - 2 * row * parity
        if kind == LEFT:
            code = 3
        elif kind == RIGHT:
            code = 5
        else:
            towards_high = (row == 0) == (kind == VERT)
            code = 7 - 6 * parity if towards_high else 1 + 6 * parity
        slot = jnp.int32(0)
        for k in range(1, slots):
            slot += jnp.where(offsets_ref[origin, col, k] == code, k, 0)
        return (origin * cols + col) * slots + slot

    def matrix(kind, tile):
        found = raw_ref[tile_of(kind, tile)]
        sorted_ref[kind * tiles + tile] = found
        return found

    for row in range(2):
        origin = row + parity - 2 * row * parity
        place = pl.ds(row * cols, cols)
        angles, strength = angles_ref[origin], coupling_ref[origin]
        cosines, sine_values = jnp.cos(angles), jnp.sin(angles)
        scale = (-BAND / probe_total) * strength
        cos_ref[place, :] = 2.0 * strength * cosines
        sin_ref[place, :] = 2.0 * strength * sine_values
        same_ref[place, :] = -scale * sine_values
        cross_ref[place, :] = scale * cosines
    for level in range(coef_ref.shape[0]):
        weights_ref[pl.ds(level, 1), :] = jnp.full(
            (1, weights_ref.shape[1]), (level + 1) * coef_ref[level], jnp.float32
        )
    for tile in range(tiles):
        row, col = divmod(tile, cols)
        place = pl.ds(col * rows, rows)
        probe = (outer_ref, inner_ref)[row][place, :]
        total = local_hop(cols, rows, outer_ref, inner_ref, tile, matrix)
        part = 2.0 * total + kondo(
            probe.astype(jnp.float32), cos_ref[pl.ds(tile, 1), :], sin_ref[pl.ds(tile, 1), :]
        )
        (part_outer, part_inner)[row][col] = part
        if row == 0:
            send_ref[place, :] = part.astype(jnp.bfloat16)
        else:
            pair_ref[place, :] = probe
            pair_ref[pl.ds((cols + col) * rows, rows), :] = part.astype(jnp.bfloat16)
    for tile in range(tiles):
        matrix(RIM, tile)


def first_outer_body(cols, rows, got_ref, sorted_ref, part_ref, field_ref, low_ref, turned_ref):
    for col in range(cols):
        place = pl.ds(col * rows, rows)
        turned = sorted_ref[RIM * 2 * cols + col].T
        turned_ref[col] = turned
        field = part_ref[col] + 2.0 * product(got_ref[place, :], turned)
        field_ref[col] = field
        low_ref[place, :] = field.astype(jnp.bfloat16)


def first_inner_body(cols, rows, probe_outer, probe_inner, got_ref, sorted_ref, part_ref,
                     weights_ref, cos_ref, sin_ref, field_outer, low_outer,
                     field_inner, low_inner, part_outer, part_inner, send_ref, terms_ref,
                     turned_ref):
    tiles = 2 * cols
    fields, low, probes = (field_outer, field_inner), (low_outer, low_inner), (probe_outer, probe_inner)
    for col in range(cols):
        place = pl.ds(col * rows, rows)
        turned = sorted_ref[RIM * tiles + cols + col].T
        turned_ref[col] = turned
        field = part_ref[col] + 2.0 * product(got_ref[place, :], turned)
        field_inner[col] = field
        low_inner[place, :] = field.astype(jnp.bfloat16)

    def matrix(kind, source):
        return sorted_ref[kind * tiles + source]

    for tile in range(tiles):
        row, col = divmod(tile, cols)
        place = pl.ds(col * rows, rows)
        probe_low = probes[row][place, :]
        probe = probe_low.astype(jnp.float32)
        field = fields[row][col]
        total = local_hop(cols, rows, *low, tile, matrix)
        following = 2.0 * total - probe + kondo(
            field, cos_ref[pl.ds(tile, 1), :], sin_ref[pl.ds(tile, 1), :]
        )
        (part_outer, part_inner)[row][col] = following
        if row == 1:
            send_ref[place, :] = following.astype(jnp.bfloat16)
        terms_ref[tile], terms_ref[tiles + tile] = overlap_terms(
            probe_low, weights_ref[0:1, 0:1] * probe + weights_ref[1:2, 0:1] * field
        )


def second_inner_body(cols, rows, probe_outer, probe_inner, got_ref, sorted_ref, turned_ref,
                      part_ref, field_ref, low_ref, share_ref, vert_ref):
    tiles = 2 * cols
    places = [pl.ds(col * rows, rows) for col in range(cols)]
    own = [
        2.0 * product(probe_inner[places[col], :], sorted_ref[RIM * tiles + cols + col])
        for col in range(cols)
    ]
    for col in range(cols):
        share_ref[col] = 2.0 * product(probe_outer[places[col], :], sorted_ref[RIM * tiles + col])
    sent = [
        got_ref[pl.ds((cols + col) * rows, rows), :].astype(jnp.float32) for col in range(cols)
    ]
    rims = [(sent[col] + own[col]).astype(jnp.bfloat16) for col in range(cols)]
    fields = [
        part_ref[col] + 2.0 * product(rims[col], turned_ref[col]) for col in range(cols)
    ]
    lows = [field.astype(jnp.bfloat16) for field in fields]
    verts = [product(lows[col], sorted_ref[VERT * tiles + cols + col]) for col in range(cols)]
    for col in range(cols):
        field_ref[col] = fields[col]
        low_ref[places[col], :] = lows[col]
        vert_ref[col] = 2.0 * verts[col]


def row_sums(blocks):
    index = lax.broadcasted_iota(jnp.int32, blocks[0].shape, 0)
    shift = 4
    while shift:
        low = (index & shift) == 0
        half = len(blocks) // 2
        joined = []
        for first, second in zip(blocks[:half], blocks[half:]):
            kept, moved = jnp.where(low, first, second), jnp.where(low, second, first)
            down = pltpu.roll(moved, shift, 0)
            if shift == 4:
                joined.append(kept + down)
            else:
                joined.append(kept + jnp.where(low, pltpu.roll(moved, 8 - shift, 0), down))
        blocks = joined
        shift //= 2
    return blocks[0]


def second_outer_body(cols, rows, got_ref, share_ref, vert_ref, sorted_ref, turned_ref, part_ref,
                      field_before, cos_ref, sin_ref, rim_probe, weights_ref,
                      field_ref, low_ref, next_ref, send_ref):
    tiles = 2 * cols
    places = [pl.ds(col * rows, rows) for col in range(cols)]
    rims = [
        (got_ref[places[col], :].astype(jnp.float32) + share_ref[col]).astype(jnp.bfloat16)
        for col in range(cols)
    ]
    fields = [
        part_ref[col] + 2.0 * product(rims[col], turned_ref[col]) for col in range(cols)
    ]
    for col in range(cols):
        field_ref[col] = fields[col]
        low_ref[places[col], :] = fields[col].astype(jnp.bfloat16)

    def matrix(kind, source):
        return sorted_ref[kind * tiles + source]

    totals = [beside(cols, rows, low_ref, col, matrix) for col in range(cols)]
    following = [
        2.0 * totals[col] + vert_ref[col] + kondo(
            fields[col], cos_ref[pl.ds(col, 1), :], sin_ref[pl.ds(col, 1), :]
        ) - field_before[col]
        for col in range(cols)
    ]
    crossed = [
        product(following[col].astype(jnp.bfloat16), matrix(RIM, col)) for col in range(cols)
    ]
    terms = [overlap_terms(rim_probe[places[col], :], crossed[col]) for col in range(cols)]
    sums = (2.0 * weights_ref[4:5, 0:1]) * row_sums(
        [same for same, _ in terms] + [cross for _, cross in terms]
    )
    rest = sums - sums.astype(jnp.bfloat16).astype(jnp.float32)
    for col in range(cols):
        next_ref[col] = following[col]
        send_ref[places[col], :] = part_ref[col].astype(jnp.bfloat16)
    send_ref[pl.ds(cols * rows, 16), :] = jnp.concatenate([sums, rest], axis=0).astype(jnp.bfloat16)


def second_rest_body(cols, rows, probe_outer, probe_inner, sorted_ref, terms_ref, weights_ref,
                     cos_ref, sin_ref, field_outer, field_inner, low_outer, low_inner,
                     field_before, next_ref, send_ref, out_ref):
    tiles = 2 * cols

    def matrix(kind, source):
        return sorted_ref[kind * tiles + source]

    for col in range(cols):
        tile = cols + col
        place = pl.ds(col * rows, rows)
        total = local_hop(cols, rows, low_outer, low_inner, tile, matrix)
        following = 2.0 * total - field_before[col] + kondo(
            field_inner[col], cos_ref[pl.ds(tile, 1), :], sin_ref[pl.ds(tile, 1), :]
        )
        next_ref[col] = following
        send_ref[place, :] = following.astype(jnp.bfloat16)
    weight = weights_ref[2:3, 0:1]
    for tile in range(tiles):
        row, col = divmod(tile, cols)
        probe = (probe_outer, probe_inner)[row][pl.ds(col * rows, rows), :]
        same, cross = overlap_terms(probe, (field_outer, field_inner)[row][col])
        out_ref[tile] = terms_ref[tile] + weight * same
        out_ref[tiles + tile] = terms_ref[tiles + tile] + weight * cross


def last_inner_body(cols, rows, probe_outer, probe_inner, got_2, got_3, low_1_outer, low_1_inner,
                    low_2_outer, low_2_inner, field_outer, field_inner, sorted_ref, turned_outer,
                    turned_inner, part_ref, terms_ref, weights_ref, cos_ref, sin_ref,
                    out_ref, halo_2_ref, low_ref):
    tiles = 2 * cols
    weight, weight_next = weights_ref[3:4, 0:1], weights_ref[4:5, 0:1]
    places = [pl.ds(col * rows, rows) for col in range(cols)]

    def matrix(kind, tile):
        return sorted_ref[kind * tiles + tile]

    def rims(got_ref, low_before):
        own = [
            2.0 * product(low_before[places[col], :], matrix(RIM, cols + col))
            for col in range(cols)
        ]
        return [
            (got_ref[places[col], :].astype(jnp.float32) + own[col]).astype(jnp.bfloat16)
            for col in range(cols)
        ]

    rim_2, rim_3 = rims(got_2, low_1_inner), rims(got_3, low_2_inner)
    crossed = [
        (2.0 * product(low_2_outer[places[col], :], matrix(RIM, col))).astype(jnp.bfloat16)
        for col in range(cols)
    ]
    fields = [
        part_ref[col] + 2.0 * product(rim_2[col], turned_inner[col]) for col in range(cols)
    ]
    for col in range(cols):
        low_ref[places[col], :] = fields[col].astype(jnp.bfloat16)
        halo_2_ref[col] = 2.0 * product(low_1_outer[places[col], :], matrix(RIM, col))
    for tile in range(tiles):
        row, col = divmod(tile, cols)
        if row == 0:
            total = product(low_ref[places[col], :], matrix(VERT, cols + col))
            total += product(crossed[col], turned_outer[col])
            vectors = weight_next * (2.0 * total - field_outer[col])
            probe = probe_outer[places[col], :]
        else:
            total = beside(cols, rows, low_ref, tile, matrix)
            total += product(rim_3[col], turned_inner[col])
            following = 2.0 * total - field_inner[col] + kondo(
                fields[col], cos_ref[pl.ds(tile, 1), :], sin_ref[pl.ds(tile, 1), :]
            )
            vectors = weight * fields[col] + weight_next * following
            probe = probe_inner[places[col], :]
        same, cross = overlap_terms(probe, vectors)
        out_ref[tile] = terms_ref[tile] + same
        out_ref[tiles + tile] = terms_ref[tiles + tile] + cross


def last_outer_body(cols, rows, probe_outer, probe_inner, got_ref, halo_2_ref, sorted_ref,
                    turned_ref, part_ref, terms_ref, weights_ref, cos_ref, sin_ref, same_ref,
                    cross_ref, out_ref, low_ref):
    tiles = 2 * cols
    weight, weight_next = weights_ref[3:4, 0:1], weights_ref[4:5, 0:1]
    places = [pl.ds(col * rows, rows) for col in range(cols)]

    def matrix(kind, tile):
        return sorted_ref[kind * tiles + tile]

    rims = [
        (got_ref[places[col], :].astype(jnp.float32) + halo_2_ref[col]).astype(jnp.bfloat16)
        for col in range(cols)
    ]
    fields = [
        part_ref[col] + 2.0 * product(rims[col], turned_ref[col]) for col in range(cols)
    ]
    for col in range(cols):
        low_ref[places[col], :] = fields[col].astype(jnp.bfloat16)
    totals = [beside(cols, rows, low_ref, col, matrix) for col in range(cols)]
    verts = [product(low_ref[places[col], :], matrix(VERT, col)) for col in range(cols)]
    shares = []
    for tile in range(tiles):
        row, col = divmod(tile, cols)
        one = pl.ds(tile, 1)
        if row == 0:
            following = 2.0 * totals[col] + kondo(fields[col], cos_ref[one, :], sin_ref[one, :])
            vectors = weight * fields[col] + weight_next * following
            probe = probe_outer[places[col], :]
        else:
            vectors = (2.0 * weight_next) * verts[col]
            probe = probe_inner[places[col], :]
        same, cross = overlap_terms(probe, vectors)
        shares.append(
            same_ref[one, :] * (terms_ref[tile] + same)
            + cross_ref[one, :] * (terms_ref[tiles + tile] + cross)
        )
    sent = got_ref[pl.ds(cols * rows, 16), :].astype(jnp.float32)
    sent = sent[:tiles] + sent[tiles:]
    across = same_ref[:cols, :] * sent[:cols] + cross_ref[:cols, :] * sent[cols:]
    share = row_sums(shares) + jnp.concatenate([across, jnp.zeros_like(across)], axis=0)
    for peer in range(out_ref.shape[0]):
        out_ref[peer] = share


def force_body(upper_ref, shares_ref, force_ref, largest_ref):
    peers = shares_ref.shape[0] // 2
    strips = []
    for strip in range(2):
        total = shares_ref[strip * peers]
        for peer in range(1, peers):
            total += shares_ref[strip * peers + peer]
        strips.append(total)
    force_ref[...] = jnp.where(upper_ref[0] == 0, strips[0], strips[1])
    largest = jnp.max(jnp.maximum(jnp.abs(strips[0]), jnp.abs(strips[1])))
    largest_ref[...] = jnp.full(largest_ref.shape, largest, jnp.float32)


def move_body(parity_ref, largest_ref, force_ref, angles_ref, noise_ref, next_ref, out_ref):
    parity = parity_ref[0]
    cols = out_ref.shape[1]
    largest = jnp.max(largest_ref[...])
    step_size = jnp.full((1, 1), STEP_MAX, jnp.float32) / (largest + 1e-06)
    kick = jnp.sqrt(TWO_TEMP * step_size)
    for row in range(2):
        origin = row + parity - 2 * row * parity
        force = force_ref[pl.ds(row * cols, cols), :]
        out_ref[origin] = force
        next_ref[origin] = angles_ref[origin] + step_size * force + kick * noise_ref[origin]


def exchange_outer(outer):
    count = lax.axis_size("site")
    pairs = [(i, (i + 1) % count if i % 2 else (i - 1) % count) for i in range(count)]
    return lax.ppermute(outer, "site", pairs)


def exchange_inner(inner):
    return lax.ppermute(inner, "site", [(i, i ^ 1) for i in range(lax.axis_size("site"))])


def local(angles, coupling, thermal_noise, coefficients, probes, hopping, offsets):
    cols, orbitals, share, width = probes.shape[1:]
    rows = orbitals * share
    tiles = 2 * cols
    f32, bf16 = jnp.float32, jnp.bfloat16
    side = ((cols * rows, width), bf16)
    pair = ((2 * cols * rows, width), bf16)
    row = ((cols, rows, width), f32)
    matrices = ((cols, width, width), bf16)
    terms_like = ((2 * tiles, 8, width), f32)
    row_like = ((tiles, width), f32)
    sites, peers = lax.axis_size("site"), lax.axis_size("probe")
    probe_total = peers * share
    local_flops = 2 * 3 * tiles * rows * width * width
    site = lax.axis_index("site")
    parity = (site % 2).astype(jnp.int32).reshape(1)
    upper = (site // (sites // 2)).astype(jnp.int32).reshape(1)

    def run(body, outs, args, scratch=(), flops=0):
        return call(
            functools.partial(body, cols, rows), outs, [IN_VMEM] * len(args),
            tuple(held(x) for x in args), scratch=scratch, flops=flops,
        )

    fetched = pl.pallas_call(
        fetch_body,
        out_shape=[
            pltpu.VMEM(*side), pltpu.VMEM(*side), pltpu.SMEM(offsets.shape, jnp.int32),
            pltpu.SMEM(coefficients.shape, f32), pltpu.VMEM(angles.shape, f32),
            pltpu.VMEM(coupling.shape, f32),
        ],
        in_specs=[IN_SMEM] + [IN_HBM] * 5,
        out_specs=[IN_VMEM, IN_VMEM, IN_SMEM, IN_SMEM, IN_VMEM, IN_VMEM],
        scratch_shapes=[pltpu.SemaphoreType.DMA((6,))],
        compiler_params=pltpu.CompilerParams(vmem_limit_bytes=16 * 1024 * 1024),
        cost_estimate=pl.CostEstimate(flops=20 * local_flops, bytes_accessed=0, transcendentals=0),
    )(parity, *(held(x, pltpu.HBM) for x in (
        probes.reshape(2, cols * rows, width), offsets, coefficients, angles, coupling)))
    outer, inner, offsets_held, coef_held, angles_held, coupling_held = fetched
    probe_rows = [outer, inner]
    got_0 = exchange_outer(outer)

    (sorted_hop, part_outer, part_inner, send, send_pair, weights, twice_cos, twice_sin,
     same_factor, cross_factor) = call(
        functools.partial(first_body, cols, rows, probe_total),
        [((4 * tiles, width, width), bf16), row, row, side, pair, ((8, 128), f32)]
        + [row_like] * 4,
        [IN_SMEM] * 3 + [IN_VMEM] * 5,
        (parity, held(offsets_held, pltpu.SMEM), held(coef_held, pltpu.SMEM),
         *(held(x) for x in (hopping.reshape(-1, width, width), angles_held, coupling_held,
                             outer, inner))),
        flops=local_flops, moved=hopping.size * 2,
    )
    got_1 = exchange_outer(send)
    from_inner = exchange_inner(send_pair)
    trig = [twice_cos, twice_sin]

    field_1_outer, low_1_outer, turned_outer = run(
        first_outer_body, [row, side, matrices], [got_0, sorted_hop, part_outer],
        flops=20 * local_flops,
    )
    (field_1_inner, low_1_inner, part_outer, part_inner, send, terms, turned_inner) = run(
        first_inner_body, [row, side, row, row, side, terms_like, matrices],
        [*probe_rows, from_inner, sorted_hop, part_inner, weights, *trig,
         field_1_outer, low_1_outer],
        flops=local_flops,
    )
    inner_2 = exchange_inner(send)
    field_2_inner, low_2_inner, rim_share, vert = run(
        second_inner_body, [row, side, row, row],
        [*probe_rows, from_inner, sorted_hop, turned_inner, part_inner],
    )
    field_2_outer, low_2_outer, part_outer, send = run(
        second_outer_body, [row, side, row, ((cols * rows + 16, width), bf16)],
        [got_1, rim_share, vert, sorted_hop, turned_outer, part_outer, field_1_outer, *trig,
         got_0, weights],
    )
    got_2 = exchange_outer(send)
    part_inner, send, terms = run(
        second_rest_body, [row, side, terms_like],
        [*probe_rows, sorted_hop, terms, weights, *trig, field_2_outer, field_2_inner,
         low_2_outer, low_2_inner, field_1_inner],
    )
    inner_3 = exchange_inner(send)
    terms, halo_2 = run(
        last_inner_body, [terms_like, row],
        [*probe_rows, inner_2, inner_3, low_1_outer, low_1_inner, low_2_outer, low_2_inner,
         field_2_outer, field_2_inner, sorted_hop, turned_outer, turned_inner, part_inner,
         terms, weights, *trig],
        scratch=[pltpu.VMEM(*side)],
    )
    shares = run(
        last_outer_body, [((2 * peers, tiles, width), f32)],
        [*probe_rows, got_2, halo_2, sorted_hop, turned_outer, part_outer, terms,
         weights, *trig, same_factor, cross_factor],
        scratch=[pltpu.VMEM(*side)], flops=local_flops,
    )[0]
    pairs = [
        [half * peers + peer for half in (i, i + sites // 2) for peer in range(peers)]
        for i in range(sites // 2)
    ]
    shares = lax.all_to_all(shares, ("site", "probe"), 0, 0, axis_index_groups=pairs)
    force, largest = call(
        force_body, [row_like, ((sites // 2, 1, 128), f32)],
        [IN_SMEM, IN_VMEM], (upper, held(shares)),
    )
    halves = [list(range(sites // 2)), list(range(sites // 2, sites))]
    largest = lax.all_to_all(largest, "site", 0, 0, axis_index_groups=halves)
    return pl.pallas_call(
        move_body,
        out_shape=[jax.ShapeDtypeStruct(angles.shape, f32)] * 2,
        in_specs=[IN_SMEM] + [IN_VMEM] * 4,
        out_specs=[IN_VMEM] * 2,
    )(parity, held(largest), held(force), held(angles), held(thermal_noise))


def solution(mesh):
    in_specs = (
        P("site", None, None),
        P("site", None, None),
        P("site", None, None),
        P(),
        P("site", None, None, "probe", None),
        P("site", None, None, None, None),
        P("site", None, None),
    )
    out_specs = (P("site", None, None), P("site", None, None))
    return jax.shard_map(local, mesh=mesh, in_specs=in_specs, out_specs=out_specs, check_vma=False)
```

```python
import functools
import jax
import jax.numpy as jnp
from jax import lax
from jax.experimental import pallas as pl
from jax.experimental.pallas import tpu as pltpu
from jax.sharding import PartitionSpec as P

BAND = 8.0
STEP_MAX = 0.3
TWO_TEMP = 0.1

VERT, LEFT, RIGHT, RIM = range(4)
IN_VMEM = pl.BlockSpec(memory_space=pltpu.VMEM)
IN_SMEM = pl.BlockSpec(memory_space=pltpu.SMEM)
IN_HBM = pl.BlockSpec(memory_space=pltpu.HBM)


def held(array, space=pltpu.VMEM):
    return pltpu.with_memory_space_constraint(array, space)


def call(body, outs, in_specs, args, scratch=(), flops=0, moved=0):
    return pl.pallas_call(
        body,
        out_shape=[pltpu.VMEM(shape, dtype) for shape, dtype in outs],
        in_specs=in_specs,
        out_specs=[IN_VMEM] * len(outs),
        scratch_shapes=list(scratch),
        compiler_params=pltpu.CompilerParams(vmem_limit_bytes=16 * 1024 * 1024),
        cost_estimate=pl.CostEstimate(flops=flops, bytes_accessed=moved, transcendentals=0),
    )(*args)


def product(vectors, matrix):
    return jnp.dot(vectors, matrix, preferred_element_type=jnp.float32)


def folded(values):
    return jnp.sum(values.reshape(-1, 8, values.shape[-1]), axis=0)


def overlap_terms(probe, vectors):
    half = probe.shape[0] // 2
    upper_r = probe[:half].astype(jnp.float32)
    lower_r = probe[half:].astype(jnp.float32)
    upper_w, lower_w = vectors[:half], vectors[half:]
    same = folded(upper_r * upper_w - lower_r * lower_w)
    cross = folded(upper_r * lower_w + lower_r * upper_w)
    return same, cross


def fetch_body(parity_ref, probes_hbm, offsets_hbm, coef_hbm, angles_hbm, coupling_hbm,
               outer_ref, inner_ref, offsets_ref, coef_ref, angles_ref, coupling_ref, sems):
    parity = parity_ref[0]
    copies = [
        pltpu.make_async_copy(source, target, sems.at[k])
        for k, (source, target) in enumerate((
            (probes_hbm.at[parity], outer_ref),
            (probes_hbm.at[1 - parity], inner_ref),
            (offsets_hbm, offsets_ref),
            (coef_hbm, coef_ref),
            (angles_hbm, angles_ref),
            (coupling_hbm, coupling_ref),
        ))
    ]
    for copy in copies:
        copy.start()
    for copy in copies:
        copy.wait()


def beside(cols, rows, low_ref, tile, matrix):
    row, col = divmod(tile, cols)
    right, left = (col + 1) % cols, (col - 1) % cols
    return product(
        low_ref[pl.ds(right * rows, rows), :], matrix(LEFT, row * cols + right)
    ) + product(low_ref[pl.ds(left * rows, rows), :], matrix(RIGHT, row * cols + left))


def local_hop(cols, rows, outer_ref, inner_ref, tile, matrix):
    refs = (outer_ref, inner_ref)
    row, col = divmod(tile, cols)
    total = product(
        refs[1 - row][pl.ds(col * rows, rows), :], matrix(VERT, (1 - row) * cols + col)
    )
    return total + beside(cols, rows, refs[row], tile, matrix)


def kondo(vectors, twice_cos, twice_sin):
    half = vectors.shape[0] // 2
    upper, lower = vectors[:half], vectors[half:]
    return jnp.concatenate(
        [twice_cos * upper + twice_sin * lower, twice_sin * upper - twice_cos * lower], axis=0
    )


def first_body(cols, rows, probe_total, parity_ref, offsets_ref, coef_ref, raw_ref, angles_ref,
               coupling_ref, outer_ref, inner_ref, sorted_ref, part_outer, part_inner, send_ref,
               pair_ref, weights_ref, cos_ref, sin_ref, same_ref, cross_ref):
    tiles = 2 * cols
    slots = offsets_ref.shape[2]
    parity = parity_ref[0]

    def tile_of(kind, tile):
        row, col = divmod(tile, cols)
        origin = row + parity - 2 * row * parity
        if kind == LEFT:
            code = 3
        elif kind == RIGHT:
            code = 5
        else:
            towards_high = (row == 0) == (kind == VERT)
            code = 7 - 6 * parity if towards_high else 1 + 6 * parity
        slot = jnp.int32(0)
        for k in range(1, slots):
            slot += jnp.where(offsets_ref[origin, col, k] == code, k, 0)
        return (origin * cols + col) * slots + slot

    def matrix(kind, tile):
        found = raw_ref[tile_of(kind, tile)]
        sorted_ref[kind * tiles + tile] = found
        return found

    for row in range(2):
        origin = row + parity - 2 * row * parity
        place = pl.ds(row * cols, cols)
        angles, strength = angles_ref[origin], coupling_ref[origin]
        cosines, sine_values = jnp.cos(angles), jnp.sin(angles)
        scale = (-BAND / probe_total) * strength
        cos_ref[place, :] = 2.0 * strength * cosines
        sin_ref[place, :] = 2.0 * strength * sine_values
        same_ref[place, :] = -scale * sine_values
        cross_ref[place, :] = scale * cosines
    for level in range(coef_ref.shape[0]):
        weights_ref[pl.ds(level, 1), :] = jnp.full(
            (1, weights_ref.shape[1]), (level + 1) * coef_ref[level], jnp.float32
        )
    for tile in range(tiles):
        row, col = divmod(tile, cols)
        place = pl.ds(col * rows, rows)
        probe = (outer_ref, inner_ref)[row][place, :]
        total = local_hop(cols, rows, outer_ref, inner_ref, tile, matrix)
        part = 2.0 * total + kondo(
            probe.astype(jnp.float32), cos_ref[pl.ds(tile, 1), :], sin_ref[pl.ds(tile, 1), :]
        )
        (part_outer, part_inner)[row][col] = part
        if row == 0:
            send_ref[place, :] = part.astype(jnp.bfloat16)
        else:
            pair_ref[place, :] = probe
            pair_ref[pl.ds((cols + col) * rows, rows), :] = part.astype(jnp.bfloat16)
    for tile in range(tiles):
        matrix(RIM, tile)


def first_outer_body(cols, rows, got_ref, sorted_ref, part_ref, field_ref, low_ref, turned_ref):
    for col in range(cols):
        place = pl.ds(col * rows, rows)
        turned = sorted_ref[RIM * 2 * cols + col].T
        turned_ref[col] = turned
        field = part_ref[col] + 2.0 * product(got_ref[place, :], turned)
        field_ref[col] = field
        low_ref[place, :] = field.astype(jnp.bfloat16)


def first_inner_body(cols, rows, probe_outer, probe_inner, got_ref, sorted_ref, part_ref,
                     weights_ref, cos_ref, sin_ref, field_outer, low_outer,
                     field_inner, low_inner, part_outer, part_inner, send_ref, terms_ref,
                     turned_ref):
    tiles = 2 * cols
    fields, low, probes = (field_outer, field_inner), (low_outer, low_inner), (probe_outer, probe_inner)
    for col in range(cols):
        place = pl.ds(col * rows, rows)
        turned = sorted_ref[RIM * tiles + cols + col].T
        turned_ref[col] = turned
        field = part_ref[col] + 2.0 * product(got_ref[place, :], turned)
        field_inner[col] = field
        low_inner[place, :] = field.astype(jnp.bfloat16)

    def matrix(kind, source):
        return sorted_ref[kind * tiles + source]

    for tile in range(tiles):
        row, col = divmod(tile, cols)
        place = pl.ds(col * rows, rows)
        probe_low = probes[row][place, :]
        probe = probe_low.astype(jnp.float32)
        field = fields[row][col]
        total = local_hop(cols, rows, *low, tile, matrix)
        following = 2.0 * total - probe + kondo(
            field, cos_ref[pl.ds(tile, 1), :], sin_ref[pl.ds(tile, 1), :]
        )
        (part_outer, part_inner)[row][col] = following
        if row == 1:
            send_ref[place, :] = following.astype(jnp.bfloat16)
        terms_ref[tile], terms_ref[tiles + tile] = overlap_terms(
            probe_low, weights_ref[0:1, 0:1] * probe + weights_ref[1:2, 0:1] * field
        )


def second_inner_body(cols, rows, probe_outer, probe_inner, got_ref, sorted_ref, turned_ref,
                      part_ref, field_ref, low_ref, share_ref, vert_ref):
    tiles = 2 * cols
    places = [pl.ds(col * rows, rows) for col in range(cols)]
    own = [
        2.0 * product(probe_inner[places[col], :], sorted_ref[RIM * tiles + cols + col])
        for col in range(cols)
    ]
    for col in range(cols):
        share_ref[col] = 2.0 * product(probe_outer[places[col], :], sorted_ref[RIM * tiles + col])
    sent = [
        got_ref[pl.ds((cols + col) * rows, rows), :].astype(jnp.float32) for col in range(cols)
    ]
    rims = [(sent[col] + own[col]).astype(jnp.bfloat16) for col in range(cols)]
    fields = [
        part_ref[col] + 2.0 * product(rims[col], turned_ref[col]) for col in range(cols)
    ]
    lows = [field.astype(jnp.bfloat16) for field in fields]
    verts = [product(lows[col], sorted_ref[VERT * tiles + cols + col]) for col in range(cols)]
    for col in range(cols):
        field_ref[col] = fields[col]
        low_ref[places[col], :] = lows[col]
        vert_ref[col] = 2.0 * verts[col]


def row_sums(blocks):
    index = lax.broadcasted_iota(jnp.int32, blocks[0].shape, 0)
    shift = 4
    while shift:
        low = (index & shift) == 0
        half = len(blocks) // 2
        joined = []
        for first, second in zip(blocks[:half], blocks[half:]):
            kept, moved = jnp.where(low, first, second), jnp.where(low, second, first)
            down = pltpu.roll(moved, shift, 0)
            if shift == 4:
                joined.append(kept + down)
            else:
                joined.append(kept + jnp.where(low, pltpu.roll(moved, 8 - shift, 0), down))
        blocks = joined
        shift //= 2
    return blocks[0]


def second_outer_body(cols, rows, got_ref, share_ref, vert_ref, sorted_ref, turned_ref, part_ref,
                      field_before, cos_ref, sin_ref, rim_probe, weights_ref,
                      field_ref, low_ref, next_ref, send_ref):
    tiles = 2 * cols
    places = [pl.ds(col * rows, rows) for col in range(cols)]
    rims = [
        (got_ref[places[col], :].astype(jnp.float32) + share_ref[col]).astype(jnp.bfloat16)
        for col in range(cols)
    ]
    fields = [
        part_ref[col] + 2.0 * product(rims[col], turned_ref[col]) for col in range(cols)
    ]
    for col in range(cols):
        field_ref[col] = fields[col]
        low_ref[places[col], :] = fields[col].astype(jnp.bfloat16)

    def matrix(kind, source):
        return sorted_ref[kind * tiles + source]

    totals = [beside(cols, rows, low_ref, col, matrix) for col in range(cols)]
    following = [
        2.0 * totals[col] + vert_ref[col] + kondo(
            fields[col], cos_ref[pl.ds(col, 1), :], sin_ref[pl.ds(col, 1), :]
        ) - field_before[col]
        for col in range(cols)
    ]
    crossed = [
        product(following[col].astype(jnp.bfloat16), matrix(RIM, col)) for col in range(cols)
    ]
    terms = [overlap_terms(rim_probe[places[col], :], crossed[col]) for col in range(cols)]
    sums = (2.0 * weights_ref[4:5, 0:1]) * row_sums(
        [same for same, _ in terms] + [cross for _, cross in terms]
    )
    rest = sums - sums.astype(jnp.bfloat16).astype(jnp.float32)
    for col in range(cols):
        next_ref[col] = following[col]
        send_ref[places[col], :] = part_ref[col].astype(jnp.bfloat16)
    send_ref[pl.ds(cols * rows, 16), :] = jnp.concatenate([sums, rest], axis=0).astype(jnp.bfloat16)


def second_rest_body(cols, rows, probe_outer, probe_inner, sorted_ref, terms_ref, weights_ref,
                     cos_ref, sin_ref, field_outer, field_inner, low_outer, low_inner,
                     field_before, next_ref, send_ref, out_ref):
    tiles = 2 * cols

    def matrix(kind, source):
        return sorted_ref[kind * tiles + source]

    for col in range(cols):
        tile = cols + col
        place = pl.ds(col * rows, rows)
        total = local_hop(cols, rows, low_outer, low_inner, tile, matrix)
        following = 2.0 * total - field_before[col] + kondo(
            field_inner[col], cos_ref[pl.ds(tile, 1), :], sin_ref[pl.ds(tile, 1), :]
        )
        next_ref[col] = following
        send_ref[place, :] = following.astype(jnp.bfloat16)
    weight = weights_ref[2:3, 0:1]
    for tile in range(tiles):
        row, col = divmod(tile, cols)
        probe = (probe_outer, probe_inner)[row][pl.ds(col * rows, rows), :]
        same, cross = overlap_terms(probe, (field_outer, field_inner)[row][col])
        out_ref[tile] = terms_ref[tile] + weight * same
        out_ref[tiles + tile] = terms_ref[tiles + tile] + weight * cross


def last_inner_body(cols, rows, probe_outer, probe_inner, got_2, got_3, low_1_outer, low_1_inner,
                    low_2_outer, low_2_inner, field_outer, field_inner, sorted_ref, turned_outer,
                    turned_inner, part_ref, terms_ref, weights_ref, cos_ref, sin_ref,
                    out_ref, halo_2_ref, low_ref):
    tiles = 2 * cols
    weight, weight_next = weights_ref[3:4, 0:1], weights_ref[4:5, 0:1]
    places = [pl.ds(col * rows, rows) for col in range(cols)]

    def matrix(kind, tile):
        return sorted_ref[kind * tiles + tile]

    def rims(got_ref, low_before):
        own = [
            2.0 * product(low_before[places[col], :], matrix(RIM, cols + col))
            for col in range(cols)
        ]
        return [
            (got_ref[places[col], :].astype(jnp.float32) + own[col]).astype(jnp.bfloat16)
            for col in range(cols)
        ]

    rim_2, rim_3 = rims(got_2, low_1_inner), rims(got_3, low_2_inner)
    crossed = [
        (2.0 * product(low_2_outer[places[col], :], matrix(RIM, col))).astype(jnp.bfloat16)
        for col in range(cols)
    ]
    fields = [
        part_ref[col] + 2.0 * product(rim_2[col], turned_inner[col]) for col in range(cols)
    ]
    for col in range(cols):
        low_ref[places[col], :] = fields[col].astype(jnp.bfloat16)
        halo_2_ref[col] = 2.0 * product(low_1_outer[places[col], :], matrix(RIM, col))
    for tile in range(tiles):
        row, col = divmod(tile, cols)
        if row == 0:
            total = product(low_ref[places[col], :], matrix(VERT, cols + col))
            total += product(crossed[col], turned_outer[col])
            vectors = weight_next * (2.0 * total - field_outer[col])
            probe = probe_outer[places[col], :]
        else:
            total = beside(cols, rows, low_ref, tile, matrix)
            total += product(rim_3[col], turned_inner[col])
            following = 2.0 * total - field_inner[col] + kondo(
                fields[col], cos_ref[pl.ds(tile, 1), :], sin_ref[pl.ds(tile, 1), :]
            )
            vectors = weight * fields[col] + weight_next * following
            probe = probe_inner[places[col], :]
        same, cross = overlap_terms(probe, vectors)
        out_ref[tile] = terms_ref[tile] + same
        out_ref[tiles + tile] = terms_ref[tiles + tile] + cross


def last_outer_body(cols, rows, probe_outer, probe_inner, got_ref, halo_2_ref, sorted_ref,
                    turned_ref, part_ref, terms_ref, weights_ref, cos_ref, sin_ref, same_ref,
                    cross_ref, out_ref, low_ref):
    tiles = 2 * cols
    weight, weight_next = weights_ref[3:4, 0:1], weights_ref[4:5, 0:1]
    places = [pl.ds(col * rows, rows) for col in range(cols)]

    def matrix(kind, tile):
        return sorted_ref[kind * tiles + tile]

    rims = [
        (got_ref[places[col], :].astype(jnp.float32) + halo_2_ref[col]).astype(jnp.bfloat16)
        for col in range(cols)
    ]
    fields = [
        part_ref[col] + 2.0 * product(rims[col], turned_ref[col]) for col in range(cols)
    ]
    for col in range(cols):
        low_ref[places[col], :] = fields[col].astype(jnp.bfloat16)
    totals = [beside(cols, rows, low_ref, col, matrix) for col in range(cols)]
    verts = [product(low_ref[places[col], :], matrix(VERT, col)) for col in range(cols)]
    shares = []
    for tile in range(tiles):
        row, col = divmod(tile, cols)
        one = pl.ds(tile, 1)
        if row == 0:
            following = 2.0 * totals[col] + kondo(fields[col], cos_ref[one, :], sin_ref[one, :])
            vectors = weight * fields[col] + weight_next * following
            probe = probe_outer[places[col], :]
        else:
            vectors = (2.0 * weight_next) * verts[col]
            probe = probe_inner[places[col], :]
        same, cross = overlap_terms(probe, vectors)
        shares.append(
            same_ref[one, :] * (terms_ref[tile] + same)
            + cross_ref[one, :] * (terms_ref[tiles + tile] + cross)
        )
    sent = got_ref[pl.ds(cols * rows, 16), :].astype(jnp.float32)
    sent = sent[:tiles] + sent[tiles:]
    across = same_ref[:cols, :] * sent[:cols] + cross_ref[:cols, :] * sent[cols:]
    share = row_sums(shares) + jnp.concatenate([across, jnp.zeros_like(across)], axis=0)
    for peer in range(out_ref.shape[0]):
        out_ref[peer] = share


def force_body(upper_ref, shares_ref, force_ref, largest_ref):
    peers = shares_ref.shape[0] // 2
    strips = []
    for strip in range(2):
        total = shares_ref[strip * peers]
        for peer in range(1, peers):
            total += shares_ref[strip * peers + peer]
        strips.append(total)
    force_ref[...] = jnp.where(upper_ref[0] == 0, strips[0], strips[1])
    largest = jnp.max(jnp.maximum(jnp.abs(strips[0]), jnp.abs(strips[1])))
    largest_ref[...] = jnp.full(largest_ref.shape, largest, jnp.float32)


def move_body(parity_ref, largest_ref, force_ref, angles_ref, noise_ref, next_ref, out_ref):
    parity = parity_ref[0]
    cols = out_ref.shape[1]
    largest = jnp.max(largest_ref[...])
    step_size = jnp.full((1, 1), STEP_MAX, jnp.float32) / (largest + 1e-06)
    kick = jnp.sqrt(TWO_TEMP * step_size)
    for row in range(2):
        origin = row + parity - 2 * row * parity
        force = force_ref[pl.ds(row * cols, cols), :]
        out_ref[origin] = force
        next_ref[origin] = angles_ref[origin] + step_size * force + kick * noise_ref[origin]


def exchange_outer(outer):
    count = lax.axis_size("site")
    pairs = [(i, (i + 1) % count if i % 2 else (i - 1) % count) for i in range(count)]
    return lax.ppermute(outer, "site", pairs)


def exchange_inner(inner):
    return lax.ppermute(inner, "site", [(i, i ^ 1) for i in range(lax.axis_size("site"))])


def local(angles, coupling, thermal_noise, coefficients, probes, hopping, offsets):
    cols, orbitals, share, width = probes.shape[1:]
    rows = orbitals * share
    tiles = 2 * cols
    f32, bf16 = jnp.float32, jnp.bfloat16
    side = ((cols * rows, width), bf16)
    pair = ((2 * cols * rows, width), bf16)
    row = ((cols, rows, width), f32)
    matrices = ((cols, width, width), bf16)
    terms_like = ((2 * tiles, 8, width), f32)
    row_like = ((tiles, width), f32)
    sites, peers = lax.axis_size("site"), lax.axis_size("probe")
    probe_total = peers * share
    local_flops = 2 * 3 * tiles * rows * width * width
    site = lax.axis_index("site")
    parity = (site % 2).astype(jnp.int32).reshape(1)
    upper = (site // (sites // 2)).astype(jnp.int32).reshape(1)

    def run(body, outs, args, scratch=(), flops=0):
        return call(
            functools.partial(body, cols, rows), outs, [IN_VMEM] * len(args),
            tuple(held(x) for x in args), scratch=scratch, flops=flops,
        )

    fetched = pl.pallas_call(
        fetch_body,
        out_shape=[
            pltpu.VMEM(*side), pltpu.VMEM(*side), pltpu.SMEM(offsets.shape, jnp.int32),
            pltpu.SMEM(coefficients.shape, f32), pltpu.VMEM(angles.shape, f32),
            pltpu.VMEM(coupling.shape, f32),
        ],
        in_specs=[IN_SMEM] + [IN_HBM] * 5,
        out_specs=[IN_VMEM, IN_VMEM, IN_SMEM, IN_SMEM, IN_VMEM, IN_VMEM],
        scratch_shapes=[pltpu.SemaphoreType.DMA((6,))],
        compiler_params=pltpu.CompilerParams(vmem_limit_bytes=16 * 1024 * 1024),
        cost_estimate=pl.CostEstimate(flops=20 * local_flops, bytes_accessed=0, transcendentals=0),
    )(parity, *(held(x, pltpu.HBM) for x in (
        probes.reshape(2, cols * rows, width), offsets, coefficients, angles, coupling)))
    outer, inner, offsets_held, coef_held, angles_held, coupling_held = fetched
    probe_rows = [outer, inner]
    got_0 = exchange_outer(outer)

    (sorted_hop, part_outer, part_inner, send, send_pair, weights, twice_cos, twice_sin,
     same_factor, cross_factor) = call(
        functools.partial(first_body, cols, rows, probe_total),
        [((4 * tiles, width, width), bf16), row, row, side, pair, ((8, 128), f32)]
        + [row_like] * 4,
        [IN_SMEM] * 3 + [IN_VMEM] * 5,
        (parity, held(offsets_held, pltpu.SMEM), held(coef_held, pltpu.SMEM),
         *(held(x) for x in (hopping.reshape(-1, width, width), angles_held, coupling_held,
                             outer, inner))),
        flops=local_flops, moved=hopping.size * 2,
    )
    got_1 = exchange_outer(send)
    from_inner = exchange_inner(send_pair)
    trig = [twice_cos, twice_sin]

    field_1_outer, low_1_outer, turned_outer = run(
        first_outer_body, [row, side, matrices], [got_0, sorted_hop, part_outer],
        flops=20 * local_flops,
    )
    (field_1_inner, low_1_inner, part_outer, part_inner, send, terms, turned_inner) = run(
        first_inner_body, [row, side, row, row, side, terms_like, matrices],
        [*probe_rows, from_inner, sorted_hop, part_inner, weights, *trig,
         field_1_outer, low_1_outer],
        flops=local_flops,
    )
    inner_2 = exchange_inner(send)
    field_2_inner, low_2_inner, rim_share, vert = run(
        second_inner_body, [row, side, row, row],
        [*probe_rows, from_inner, sorted_hop, turned_inner, part_inner],
    )
    field_2_outer, low_2_outer, part_outer, send = run(
        second_outer_body, [row, side, row, ((cols * rows + 16, width), bf16)],
        [got_1, rim_share, vert, sorted_hop, turned_outer, part_outer, field_1_outer, *trig,
         got_0, weights],
    )
    got_2 = exchange_outer(send)
    part_inner, send, terms = run(
        second_rest_body, [row, side, terms_like],
        [*probe_rows, sorted_hop, terms, weights, *trig, field_2_outer, field_2_inner,
         low_2_outer, low_2_inner, field_1_inner],
    )
    inner_3 = exchange_inner(send)
    terms, halo_2 = run(
        last_inner_body, [terms_like, row],
        [*probe_rows, inner_2, inner_3, low_1_outer, low_1_inner, low_2_outer, low_2_inner,
         field_2_outer, field_2_inner, sorted_hop, turned_outer, turned_inner, part_inner,
         terms, weights, *trig],
        scratch=[pltpu.VMEM(*side)],
    )
    shares = run(
        last_outer_body, [((2 * peers, tiles, width), f32)],
        [*probe_rows, got_2, halo_2, sorted_hop, turned_outer, part_outer, terms,
         weights, *trig, same_factor, cross_factor],
        scratch=[pltpu.VMEM(*side)], flops=local_flops,
    )[0]
    half = sites // 2
    pairs = [
        [strip * peers + peer for strip in (i, half + (i ^ 1)) for peer in range(peers)]
        for i in range(half)
    ]
    shares = lax.all_to_all(shares, ("site", "probe"), 0, 0, axis_index_groups=pairs)
    force, largest = call(
        force_body, [row_like, ((sites // 2, 1, 128), f32)],
        [IN_SMEM, IN_VMEM], (upper, held(shares)),
    )
    halves = [list(range(half)), list(range(half, sites))]
    largest = lax.all_to_all(largest, "site", 0, 0, axis_index_groups=halves)
    return pl.pallas_call(
        move_body,
        out_shape=[jax.ShapeDtypeStruct(angles.shape, f32)] * 2,
        in_specs=[IN_SMEM] + [IN_VMEM] * 4,
        out_specs=[IN_VMEM] * 2,
    )(parity, held(largest), held(force), held(angles), held(thermal_noise))


def solution(mesh):
    in_specs = (
        P("site", None, None),
        P("site", None, None),
        P("site", None, None),
        P(),
        P("site", None, None, "probe", None),
        P("site", None, None, None, None),
        P("site", None, None),
    )
    out_specs = (P("site", None, None), P("site", None, None))
    return jax.shard_map(local, mesh=mesh, in_specs=in_specs, out_specs=out_specs, check_vma=False)
```

```python
import functools
import jax
import jax.numpy as jnp
from jax import lax
from jax.experimental import pallas as pl
from jax.experimental.pallas import tpu as pltpu
from jax.sharding import PartitionSpec as P

BAND = 8.0
STEP_MAX = 0.3
TWO_TEMP = 0.1

VERT, LEFT, RIGHT, RIM = range(4)
IN_VMEM = pl.BlockSpec(memory_space=pltpu.VMEM)
IN_SMEM = pl.BlockSpec(memory_space=pltpu.SMEM)
IN_HBM = pl.BlockSpec(memory_space=pltpu.HBM)


def held(array, space=pltpu.VMEM):
    return pltpu.with_memory_space_constraint(array, space)


def call(body, outs, in_specs, args, scratch=(), flops=0, moved=0):
    return pl.pallas_call(
        body,
        out_shape=[pltpu.VMEM(shape, dtype) for shape, dtype in outs],
        in_specs=in_specs,
        out_specs=[IN_VMEM] * len(outs),
        scratch_shapes=list(scratch),
        compiler_params=pltpu.CompilerParams(vmem_limit_bytes=16 * 1024 * 1024),
        cost_estimate=pl.CostEstimate(flops=flops, bytes_accessed=moved, transcendentals=0),
    )(*args)


def product(vectors, matrix):
    return jnp.dot(vectors, matrix, preferred_element_type=jnp.float32)


def folded(values):
    return jnp.sum(values.reshape(-1, 8, values.shape[-1]), axis=0)


def overlap_terms(probe, vectors):
    half = probe.shape[0] // 2
    upper_r = probe[:half].astype(jnp.float32)
    lower_r = probe[half:].astype(jnp.float32)
    upper_w, lower_w = vectors[:half], vectors[half:]
    same = folded(upper_r * upper_w - lower_r * lower_w)
    cross = folded(upper_r * lower_w + lower_r * upper_w)
    return same, cross


def fetch_body(parity_ref, probes_hbm, offsets_hbm, coef_hbm, angles_hbm, coupling_hbm,
               outer_ref, inner_ref, offsets_ref, coef_ref, angles_ref, coupling_ref, sems):
    parity = parity_ref[0]
    copies = [
        pltpu.make_async_copy(source, target, sems.at[k])
        for k, (source, target) in enumerate((
            (probes_hbm.at[parity], outer_ref),
            (probes_hbm.at[1 - parity], inner_ref),
            (offsets_hbm, offsets_ref),
            (coef_hbm, coef_ref),
            (angles_hbm, angles_ref),
            (coupling_hbm, coupling_ref),
        ))
    ]
    for copy in copies:
        copy.start()
    for copy in copies:
        copy.wait()


def beside(cols, rows, low_ref, tile, matrix):
    row, col = divmod(tile, cols)
    right, left = (col + 1) % cols, (col - 1) % cols
    return product(
        low_ref[pl.ds(right * rows, rows), :], matrix(LEFT, row * cols + right)
    ) + product(low_ref[pl.ds(left * rows, rows), :], matrix(RIGHT, row * cols + left))


def local_hop(cols, rows, outer_ref, inner_ref, tile, matrix):
    refs = (outer_ref, inner_ref)
    row, col = divmod(tile, cols)
    total = product(
        refs[1 - row][pl.ds(col * rows, rows), :], matrix(VERT, (1 - row) * cols + col)
    )
    return total + beside(cols, rows, refs[row], tile, matrix)


def kondo(vectors, twice_cos, twice_sin):
    half = vectors.shape[0] // 2
    upper, lower = vectors[:half], vectors[half:]
    return jnp.concatenate(
        [twice_cos * upper + twice_sin * lower, twice_sin * upper - twice_cos * lower], axis=0
    )


def first_body(cols, rows, probe_total, parity_ref, offsets_ref, coef_ref, raw_ref, angles_ref,
               coupling_ref, outer_ref, inner_ref, sorted_ref, part_outer, part_inner, send_ref,
               pair_ref, weights_ref, cos_ref, sin_ref, same_ref, cross_ref):
    tiles = 2 * cols
    slots = offsets_ref.shape[2]
    parity = parity_ref[0]

    def tile_of(kind, tile):
        row, col = divmod(tile, cols)
        origin = row + parity - 2 * row * parity
        if kind == LEFT:
            code = 3
        elif kind == RIGHT:
            code = 5
        else:
            towards_high = (row == 0) == (kind == VERT)
            code = 7 - 6 * parity if towards_high else 1 + 6 * parity
        slot = jnp.int32(0)
        for k in range(1, slots):
            slot += jnp.where(offsets_ref[origin, col, k] == code, k, 0)
        return (origin * cols + col) * slots + slot

    def matrix(kind, tile):
        found = raw_ref[tile_of(kind, tile)]
        sorted_ref[kind * tiles + tile] = found
        return found

    for row in range(2):
        origin = row + parity - 2 * row * parity
        place = pl.ds(row * cols, cols)
        angles, strength = angles_ref[origin], coupling_ref[origin]
        cosines, sine_values = jnp.cos(angles), jnp.sin(angles)
        scale = (-BAND / probe_total) * strength
        cos_ref[place, :] = 2.0 * strength * cosines
        sin_ref[place, :] = 2.0 * strength * sine_values
        same_ref[place, :] = -scale * sine_values
        cross_ref[place, :] = scale * cosines
    for level in range(coef_ref.shape[0]):
        weights_ref[pl.ds(level, 1), :] = jnp.full(
            (1, weights_ref.shape[1]), (level + 1) * coef_ref[level], jnp.float32
        )
    for tile in range(tiles):
        row, col = divmod(tile, cols)
        place = pl.ds(col * rows, rows)
        probe = (outer_ref, inner_ref)[row][place, :]
        total = local_hop(cols, rows, outer_ref, inner_ref, tile, matrix)
        part = 2.0 * total + kondo(
            probe.astype(jnp.float32), cos_ref[pl.ds(tile, 1), :], sin_ref[pl.ds(tile, 1), :]
        )
        (part_outer, part_inner)[row][col] = part
        if row == 0:
            send_ref[place, :] = part.astype(jnp.bfloat16)
        else:
            pair_ref[place, :] = probe
            pair_ref[pl.ds((cols + col) * rows, rows), :] = part.astype(jnp.bfloat16)
    for tile in range(tiles):
        matrix(RIM, tile)


def first_outer_body(cols, rows, got_ref, sorted_ref, part_ref, field_ref, low_ref, turned_ref):
    for col in range(cols):
        place = pl.ds(col * rows, rows)
        turned = sorted_ref[RIM * 2 * cols + col].T
        turned_ref[col] = turned
        field = part_ref[col] + 2.0 * product(got_ref[place, :], turned)
        field_ref[col] = field
        low_ref[place, :] = field.astype(jnp.bfloat16)


def first_inner_body(cols, rows, probe_outer, probe_inner, got_ref, sorted_ref, part_ref,
                     weights_ref, cos_ref, sin_ref, field_outer, low_outer,
                     field_inner, low_inner, part_outer, part_inner, send_ref, terms_ref,
                     turned_ref):
    tiles = 2 * cols
    fields, low, probes = (field_outer, field_inner), (low_outer, low_inner), (probe_outer, probe_inner)
    for col in range(cols):
        place = pl.ds(col * rows, rows)
        turned = sorted_ref[RIM * tiles + cols + col].T
        turned_ref[col] = turned
        field = part_ref[col] + 2.0 * product(got_ref[place, :], turned)
        field_inner[col] = field
        low_inner[place, :] = field.astype(jnp.bfloat16)

    def matrix(kind, source):
        return sorted_ref[kind * tiles + source]

    for tile in range(tiles):
        row, col = divmod(tile, cols)
        place = pl.ds(col * rows, rows)
        probe_low = probes[row][place, :]
        probe = probe_low.astype(jnp.float32)
        field = fields[row][col]
        total = local_hop(cols, rows, *low, tile, matrix)
        following = 2.0 * total - probe + kondo(
            field, cos_ref[pl.ds(tile, 1), :], sin_ref[pl.ds(tile, 1), :]
        )
        (part_outer, part_inner)[row][col] = following
        if row == 1:
            send_ref[place, :] = following.astype(jnp.bfloat16)
        terms_ref[tile], terms_ref[tiles + tile] = overlap_terms(
            probe_low, weights_ref[0:1, 0:1] * probe + weights_ref[1:2, 0:1] * field
        )


def second_inner_body(cols, rows, probe_outer, probe_inner, got_ref, sorted_ref, turned_ref,
                      part_ref, field_ref, low_ref, share_ref, vert_ref):
    tiles = 2 * cols
    places = [pl.ds(col * rows, rows) for col in range(cols)]
    own = [
        2.0 * product(probe_inner[places[col], :], sorted_ref[RIM * tiles + cols + col])
        for col in range(cols)
    ]
    for col in range(cols):
        share_ref[col] = 2.0 * product(probe_outer[places[col], :], sorted_ref[RIM * tiles + col])
    sent = [
        got_ref[pl.ds((cols + col) * rows, rows), :].astype(jnp.float32) for col in range(cols)
    ]
    rims = [(sent[col] + own[col]).astype(jnp.bfloat16) for col in range(cols)]
    fields = [
        part_ref[col] + 2.0 * product(rims[col], turned_ref[col]) for col in range(cols)
    ]
    lows = [field.astype(jnp.bfloat16) for field in fields]
    verts = [product(lows[col], sorted_ref[VERT * tiles + cols + col]) for col in range(cols)]
    for col in range(cols):
        field_ref[col] = fields[col]
        low_ref[places[col], :] = lows[col]
        vert_ref[col] = 2.0 * verts[col]


def row_sums(blocks):
    index = lax.broadcasted_iota(jnp.int32, blocks[0].shape, 0)
    shift = 4
    while shift:
        low = (index & shift) == 0
        half = len(blocks) // 2
        joined = []
        for first, second in zip(blocks[:half], blocks[half:]):
            kept, moved = jnp.where(low, first, second), jnp.where(low, second, first)
            down = pltpu.roll(moved, shift, 0)
            if shift == 4:
                joined.append(kept + down)
            else:
                joined.append(kept + jnp.where(low, pltpu.roll(moved, 8 - shift, 0), down))
        blocks = joined
        shift //= 2
    return blocks[0]


def second_outer_body(cols, rows, got_ref, share_ref, vert_ref, sorted_ref, turned_ref, part_ref,
                      field_before, cos_ref, sin_ref, rim_probe, weights_ref,
                      field_ref, low_ref, next_ref, send_ref):
    tiles = 2 * cols
    places = [pl.ds(col * rows, rows) for col in range(cols)]
    rims = [
        (got_ref[places[col], :].astype(jnp.float32) + share_ref[col]).astype(jnp.bfloat16)
        for col in range(cols)
    ]
    fields = [
        part_ref[col] + 2.0 * product(rims[col], turned_ref[col]) for col in range(cols)
    ]
    for col in range(cols):
        field_ref[col] = fields[col]
        low_ref[places[col], :] = fields[col].astype(jnp.bfloat16)

    def matrix(kind, source):
        return sorted_ref[kind * tiles + source]

    totals = [beside(cols, rows, low_ref, col, matrix) for col in range(cols)]
    following = [
        2.0 * totals[col] + vert_ref[col] + kondo(
            fields[col], cos_ref[pl.ds(col, 1), :], sin_ref[pl.ds(col, 1), :]
        ) - field_before[col]
        for col in range(cols)
    ]
    crossed = [
        product(following[col].astype(jnp.bfloat16), matrix(RIM, col)) for col in range(cols)
    ]
    terms = [overlap_terms(rim_probe[places[col], :], crossed[col]) for col in range(cols)]
    sums = (2.0 * weights_ref[4:5, 0:1]) * row_sums(
        [same for same, _ in terms] + [cross for _, cross in terms]
    )
    rest = sums - sums.astype(jnp.bfloat16).astype(jnp.float32)
    for col in range(cols):
        next_ref[col] = following[col]
        send_ref[places[col], :] = part_ref[col].astype(jnp.bfloat16)
    send_ref[pl.ds(cols * rows, 16), :] = jnp.concatenate([sums, rest], axis=0).astype(jnp.bfloat16)


def second_rest_body(cols, rows, probe_outer, probe_inner, sorted_ref, terms_ref, weights_ref,
                     cos_ref, sin_ref, field_outer, field_inner, low_outer, low_inner,
                     field_before, next_ref, send_ref, out_ref):
    tiles = 2 * cols

    def matrix(kind, source):
        return sorted_ref[kind * tiles + source]

    for col in range(cols):
        tile = cols + col
        place = pl.ds(col * rows, rows)
        total = local_hop(cols, rows, low_outer, low_inner, tile, matrix)
        following = 2.0 * total - field_before[col] + kondo(
            field_inner[col], cos_ref[pl.ds(tile, 1), :], sin_ref[pl.ds(tile, 1), :]
        )
        next_ref[col] = following
        send_ref[place, :] = following.astype(jnp.bfloat16)
    weight = weights_ref[2:3, 0:1]
    for tile in range(tiles):
        row, col = divmod(tile, cols)
        probe = (probe_outer, probe_inner)[row][pl.ds(col * rows, rows), :]
        same, cross = overlap_terms(probe, (field_outer, field_inner)[row][col])
        out_ref[tile] = terms_ref[tile] + weight * same
        out_ref[tiles + tile] = terms_ref[tiles + tile] + weight * cross


def last_inner_body(cols, rows, probe_outer, probe_inner, got_2, got_3, low_1_outer, low_1_inner,
                    low_2_outer, low_2_inner, field_outer, field_inner, sorted_ref, turned_outer,
                    turned_inner, part_ref, terms_ref, weights_ref, cos_ref, sin_ref,
                    out_ref, halo_2_ref, low_ref):
    tiles = 2 * cols
    weight, weight_next = weights_ref[3:4, 0:1], weights_ref[4:5, 0:1]
    places = [pl.ds(col * rows, rows) for col in range(cols)]

    def matrix(kind, tile):
        return sorted_ref[kind * tiles + tile]

    def rims(got_ref, low_before):
        own = [
            2.0 * product(low_before[places[col], :], matrix(RIM, cols + col))
            for col in range(cols)
        ]
        return [
            (got_ref[places[col], :].astype(jnp.float32) + own[col]).astype(jnp.bfloat16)
            for col in range(cols)
        ]

    rim_2, rim_3 = rims(got_2, low_1_inner), rims(got_3, low_2_inner)
    crossed = [
        (2.0 * product(low_2_outer[places[col], :], matrix(RIM, col))).astype(jnp.bfloat16)
        for col in range(cols)
    ]
    fields = [
        part_ref[col] + 2.0 * product(rim_2[col], turned_inner[col]) for col in range(cols)
    ]
    for col in range(cols):
        low_ref[places[col], :] = fields[col].astype(jnp.bfloat16)
        halo_2_ref[col] = 2.0 * product(low_1_outer[places[col], :], matrix(RIM, col))
    for tile in range(tiles):
        row, col = divmod(tile, cols)
        if row == 0:
            total = product(low_ref[places[col], :], matrix(VERT, cols + col))
            total += product(crossed[col], turned_outer[col])
            vectors = weight_next * (2.0 * total - field_outer[col])
            probe = probe_outer[places[col], :]
        else:
            total = beside(cols, rows, low_ref, tile, matrix)
            total += product(rim_3[col], turned_inner[col])
            following = 2.0 * total - field_inner[col] + kondo(
                fields[col], cos_ref[pl.ds(tile, 1), :], sin_ref[pl.ds(tile, 1), :]
            )
            vectors = weight * fields[col] + weight_next * following
            probe = probe_inner[places[col], :]
        same, cross = overlap_terms(probe, vectors)
        out_ref[tile] = terms_ref[tile] + same
        out_ref[tiles + tile] = terms_ref[tiles + tile] + cross


def last_outer_body(cols, rows, probe_outer, probe_inner, got_ref, halo_2_ref, sorted_ref,
                    turned_ref, part_ref, terms_ref, weights_ref, cos_ref, sin_ref, same_ref,
                    cross_ref, out_ref, low_ref):
    tiles = 2 * cols
    weight, weight_next = weights_ref[3:4, 0:1], weights_ref[4:5, 0:1]
    places = [pl.ds(col * rows, rows) for col in range(cols)]

    def matrix(kind, tile):
        return sorted_ref[kind * tiles + tile]

    rims = [
        (got_ref[places[col], :].astype(jnp.float32) + halo_2_ref[col]).astype(jnp.bfloat16)
        for col in range(cols)
    ]
    fields = [
        part_ref[col] + 2.0 * product(rims[col], turned_ref[col]) for col in range(cols)
    ]
    for col in range(cols):
        low_ref[places[col], :] = fields[col].astype(jnp.bfloat16)
    totals = [beside(cols, rows, low_ref, col, matrix) for col in range(cols)]
    verts = [product(low_ref[places[col], :], matrix(VERT, col)) for col in range(cols)]
    shares = []
    for tile in range(tiles):
        row, col = divmod(tile, cols)
        one = pl.ds(tile, 1)
        if row == 0:
            following = 2.0 * totals[col] + kondo(fields[col], cos_ref[one, :], sin_ref[one, :])
            vectors = weight * fields[col] + weight_next * following
            probe = probe_outer[places[col], :]
        else:
            vectors = (2.0 * weight_next) * verts[col]
            probe = probe_inner[places[col], :]
        same, cross = overlap_terms(probe, vectors)
        shares.append(
            same_ref[one, :] * (terms_ref[tile] + same)
            + cross_ref[one, :] * (terms_ref[tiles + tile] + cross)
        )
    sent = got_ref[pl.ds(cols * rows, 16), :].astype(jnp.float32)
    sent = sent[:tiles] + sent[tiles:]
    across = same_ref[:cols, :] * sent[:cols] + cross_ref[:cols, :] * sent[cols:]
    share = row_sums(shares) + jnp.concatenate([across, jnp.zeros_like(across)], axis=0)
    for peer in range(out_ref.shape[0]):
        out_ref[peer] = share


def force_body(shares_ref, force_ref, largest_ref):
    force = shares_ref[0]
    for peer in range(1, shares_ref.shape[0]):
        force += shares_ref[peer]
    force_ref[...] = force
    largest_ref[...] = jnp.full(largest_ref.shape, jnp.max(jnp.abs(force)), jnp.float32)


def move_body(parity_ref, largest_ref, force_ref, angles_ref, noise_ref, next_ref, out_ref):
    parity = parity_ref[0]
    cols = out_ref.shape[1]
    largest = jnp.max(largest_ref[...])
    step_size = jnp.full((1, 1), STEP_MAX, jnp.float32) / (largest + 1e-06)
    kick = jnp.sqrt(TWO_TEMP * step_size)
    for row in range(2):
        origin = row + parity - 2 * row * parity
        force = force_ref[pl.ds(row * cols, cols), :]
        out_ref[origin] = force
        next_ref[origin] = angles_ref[origin] + step_size * force + kick * noise_ref[origin]


def exchange_outer(outer):
    count = lax.axis_size("site")
    pairs = [(i, (i + 1) % count if i % 2 else (i - 1) % count) for i in range(count)]
    return lax.ppermute(outer, "site", pairs)


def exchange_inner(inner):
    return lax.ppermute(inner, "site", [(i, i ^ 1) for i in range(lax.axis_size("site"))])


def local(angles, coupling, thermal_noise, coefficients, probes, hopping, offsets):
    cols, orbitals, share, width = probes.shape[1:]
    rows = orbitals * share
    tiles = 2 * cols
    f32, bf16 = jnp.float32, jnp.bfloat16
    side = ((cols * rows, width), bf16)
    pair = ((2 * cols * rows, width), bf16)
    row = ((cols, rows, width), f32)
    matrices = ((cols, width, width), bf16)
    terms_like = ((2 * tiles, 8, width), f32)
    row_like = ((tiles, width), f32)
    sites, peers = lax.axis_size("site"), lax.axis_size("probe")
    probe_total = peers * share
    local_flops = 2 * 3 * tiles * rows * width * width
    parity = (lax.axis_index("site") % 2).astype(jnp.int32).reshape(1)

    def run(body, outs, args, scratch=(), flops=0):
        return call(
            functools.partial(body, cols, rows), outs, [IN_VMEM] * len(args),
            tuple(held(x) for x in args), scratch=scratch, flops=flops,
        )

    fetched = pl.pallas_call(
        fetch_body,
        out_shape=[
            pltpu.VMEM(*side), pltpu.VMEM(*side), pltpu.SMEM(offsets.shape, jnp.int32),
            pltpu.SMEM(coefficients.shape, f32), pltpu.VMEM(angles.shape, f32),
            pltpu.VMEM(coupling.shape, f32),
        ],
        in_specs=[IN_SMEM] + [IN_HBM] * 5,
        out_specs=[IN_VMEM, IN_VMEM, IN_SMEM, IN_SMEM, IN_VMEM, IN_VMEM],
        scratch_shapes=[pltpu.SemaphoreType.DMA((6,))],
        compiler_params=pltpu.CompilerParams(vmem_limit_bytes=16 * 1024 * 1024),
        cost_estimate=pl.CostEstimate(flops=20 * local_flops, bytes_accessed=0, transcendentals=0),
    )(parity, *(held(x, pltpu.HBM) for x in (
        probes.reshape(2, cols * rows, width), offsets, coefficients, angles, coupling)))
    outer, inner, offsets_held, coef_held, angles_held, coupling_held = fetched
    probe_rows = [outer, inner]
    got_0 = exchange_outer(outer)

    (sorted_hop, part_outer, part_inner, send, send_pair, weights, twice_cos, twice_sin,
     same_factor, cross_factor) = call(
        functools.partial(first_body, cols, rows, probe_total),
        [((4 * tiles, width, width), bf16), row, row, side, pair, ((8, 128), f32)]
        + [row_like] * 4,
        [IN_SMEM] * 3 + [IN_VMEM] * 5,
        (parity, held(offsets_held, pltpu.SMEM), held(coef_held, pltpu.SMEM),
         *(held(x) for x in (hopping.reshape(-1, width, width), angles_held, coupling_held,
                             outer, inner))),
        flops=local_flops, moved=hopping.size * 2,
    )
    got_1 = exchange_outer(send)
    from_inner = exchange_inner(send_pair)
    trig = [twice_cos, twice_sin]

    field_1_outer, low_1_outer, turned_outer = run(
        first_outer_body, [row, side, matrices], [got_0, sorted_hop, part_outer],
        flops=20 * local_flops,
    )
    (field_1_inner, low_1_inner, part_outer, part_inner, send, terms, turned_inner) = run(
        first_inner_body, [row, side, row, row, side, terms_like, matrices],
        [*probe_rows, from_inner, sorted_hop, part_inner, weights, *trig,
         field_1_outer, low_1_outer],
        flops=local_flops,
    )
    inner_2 = exchange_inner(send)
    field_2_inner, low_2_inner, rim_share, vert = run(
        second_inner_body, [row, side, row, row],
        [*probe_rows, from_inner, sorted_hop, turned_inner, part_inner],
    )
    field_2_outer, low_2_outer, part_outer, send = run(
        second_outer_body, [row, side, row, ((cols * rows + 16, width), bf16)],
        [got_1, rim_share, vert, sorted_hop, turned_outer, part_outer, field_1_outer, *trig,
         got_0, weights],
    )
    got_2 = exchange_outer(send)
    part_inner, send, terms = run(
        second_rest_body, [row, side, terms_like],
        [*probe_rows, sorted_hop, terms, weights, *trig, field_2_outer, field_2_inner,
         low_2_outer, low_2_inner, field_1_inner],
    )
    inner_3 = exchange_inner(send)
    terms, halo_2 = run(
        last_inner_body, [terms_like, row],
        [*probe_rows, inner_2, inner_3, low_1_outer, low_1_inner, low_2_outer, low_2_inner,
         field_2_outer, field_2_inner, sorted_hop, turned_outer, turned_inner, part_inner,
         terms, weights, *trig],
        scratch=[pltpu.VMEM(*side)],
    )
    shares = run(
        last_outer_body, [((peers, tiles, width), f32)],
        [*probe_rows, got_2, halo_2, sorted_hop, turned_outer, part_outer, terms,
         weights, *trig, same_factor, cross_factor],
        scratch=[pltpu.VMEM(*side)], flops=local_flops,
    )[0]
    shares = lax.all_to_all(shares, "probe", 0, 0)
    force, largest = call(
        force_body, [row_like, ((sites, 1, 128), f32)], [IN_VMEM], (held(shares),)
    )
    largest = lax.all_to_all(largest, "site", 0, 0)
    return pl.pallas_call(
        move_body,
        out_shape=[jax.ShapeDtypeStruct(angles.shape, f32)] * 2,
        in_specs=[IN_SMEM] + [IN_VMEM] * 4,
        out_specs=[IN_VMEM] * 2,
    )(parity, held(largest), held(force), held(angles), held(thermal_noise))


def solution(mesh):
    in_specs = (
        P("site", None, None),
        P("site", None, None),
        P("site", None, None),
        P(),
        P("site", None, None, "probe", None),
        P("site", None, None, None, None),
        P("site", None, None),
    )
    out_specs = (P("site", None, None), P("site", None, None))
    return jax.shard_map(local, mesh=mesh, in_specs=in_specs, out_specs=out_specs, check_vma=False)
```

```python
import functools
import jax
import jax.numpy as jnp
from jax import lax
from jax.experimental import pallas as pl
from jax.experimental.pallas import tpu as pltpu
from jax.sharding import PartitionSpec as P

BAND = 8.0
STEP_MAX = 0.3
TWO_TEMP = 0.1

VERT, LEFT, RIGHT, RIM = range(4)
IN_VMEM = pl.BlockSpec(memory_space=pltpu.VMEM)
IN_SMEM = pl.BlockSpec(memory_space=pltpu.SMEM)
IN_HBM = pl.BlockSpec(memory_space=pltpu.HBM)


def held(array, space=pltpu.VMEM):
    return pltpu.with_memory_space_constraint(array, space)


def call(body, outs, in_specs, args, scratch=(), flops=0, moved=0):
    return pl.pallas_call(
        body,
        out_shape=[pltpu.VMEM(shape, dtype) for shape, dtype in outs],
        in_specs=in_specs,
        out_specs=[IN_VMEM] * len(outs),
        scratch_shapes=list(scratch),
        compiler_params=pltpu.CompilerParams(vmem_limit_bytes=16 * 1024 * 1024),
        cost_estimate=pl.CostEstimate(flops=flops, bytes_accessed=moved, transcendentals=0),
    )(*args)


def product(vectors, matrix):
    return jnp.dot(vectors, matrix, preferred_element_type=jnp.float32)


def folded(values):
    return jnp.sum(values.reshape(-1, 8, values.shape[-1]), axis=0)


def overlap_terms(probe, vectors):
    half = probe.shape[0] // 2
    upper_r = probe[:half].astype(jnp.float32)
    lower_r = probe[half:].astype(jnp.float32)
    upper_w, lower_w = vectors[:half], vectors[half:]
    same = folded(upper_r * upper_w - lower_r * lower_w)
    cross = folded(upper_r * lower_w + lower_r * upper_w)
    return same, cross


def fetch_body(parity_ref, probes_hbm, offsets_hbm, coef_hbm, angles_hbm, coupling_hbm,
               outer_ref, inner_ref, offsets_ref, coef_ref, angles_ref, coupling_ref, sems):
    parity = parity_ref[0]
    copies = [
        pltpu.make_async_copy(source, target, sems.at[k])
        for k, (source, target) in enumerate((
            (probes_hbm.at[parity], outer_ref),
            (probes_hbm.at[1 - parity], inner_ref),
            (offsets_hbm, offsets_ref),
            (coef_hbm, coef_ref),
            (angles_hbm, angles_ref),
            (coupling_hbm, coupling_ref),
        ))
    ]
    for copy in copies:
        copy.start()
    for copy in copies:
        copy.wait()


def beside(cols, rows, low_ref, tile, matrix):
    row, col = divmod(tile, cols)
    right, left = (col + 1) % cols, (col - 1) % cols
    return product(
        low_ref[pl.ds(right * rows, rows), :], matrix(LEFT, row * cols + right)
    ) + product(low_ref[pl.ds(left * rows, rows), :], matrix(RIGHT, row * cols + left))


def local_hop(cols, rows, outer_ref, inner_ref, tile, matrix):
    refs = (outer_ref, inner_ref)
    row, col = divmod(tile, cols)
    total = product(
        refs[1 - row][pl.ds(col * rows, rows), :], matrix(VERT, (1 - row) * cols + col)
    )
    return total + beside(cols, rows, refs[row], tile, matrix)


def kondo(vectors, twice_cos, twice_sin):
    half = vectors.shape[0] // 2
    upper, lower = vectors[:half], vectors[half:]
    return jnp.concatenate(
        [twice_cos * upper + twice_sin * lower, twice_sin * upper - twice_cos * lower], axis=0
    )


def first_body(cols, rows, probe_total, parity_ref, offsets_ref, coef_ref, raw_ref, angles_ref,
               coupling_ref, outer_ref, inner_ref, sorted_ref, part_outer, part_inner, send_ref,
               pair_ref, weights_ref, cos_ref, sin_ref, same_ref, cross_ref):
    tiles = 2 * cols
    slots = offsets_ref.shape[2]
    parity = parity_ref[0]

    def tile_of(kind, tile):
        row, col = divmod(tile, cols)
        origin = row + parity - 2 * row * parity
        if kind == LEFT:
            code = 3
        elif kind == RIGHT:
            code = 5
        else:
            towards_high = (row == 0) == (kind == VERT)
            code = 7 - 6 * parity if towards_high else 1 + 6 * parity
        slot = jnp.int32(0)
        for k in range(1, slots):
            slot += jnp.where(offsets_ref[origin, col, k] == code, k, 0)
        return (origin * cols + col) * slots + slot

    def matrix(kind, tile):
        found = raw_ref[tile_of(kind, tile)]
        sorted_ref[kind * tiles + tile] = found
        return found

    for row in range(2):
        origin = row + parity - 2 * row * parity
        place = pl.ds(row * cols, cols)
        angles, strength = angles_ref[origin], coupling_ref[origin]
        cosines, sine_values = jnp.cos(angles), jnp.sin(angles)
        scale = (-BAND / probe_total) * strength
        cos_ref[place, :] = 2.0 * strength * cosines
        sin_ref[place, :] = 2.0 * strength * sine_values
        same_ref[place, :] = -scale * sine_values
        cross_ref[place, :] = scale * cosines
    for level in range(coef_ref.shape[0]):
        weights_ref[pl.ds(level, 1), :] = jnp.full(
            (1, weights_ref.shape[1]), (level + 1) * coef_ref[level], jnp.float32
        )
    for tile in range(tiles):
        row, col = divmod(tile, cols)
        place = pl.ds(col * rows, rows)
        probe = (outer_ref, inner_ref)[row][place, :]
        total = local_hop(cols, rows, outer_ref, inner_ref, tile, matrix)
        part = 2.0 * total + kondo(
            probe.astype(jnp.float32), cos_ref[pl.ds(tile, 1), :], sin_ref[pl.ds(tile, 1), :]
        )
        (part_outer, part_inner)[row][col] = part
        if row == 0:
            send_ref[place, :] = part.astype(jnp.bfloat16)
        else:
            pair_ref[place, :] = probe
            pair_ref[pl.ds((cols + col) * rows, rows), :] = part.astype(jnp.bfloat16)
    for tile in range(tiles):
        matrix(RIM, tile)


def first_outer_body(cols, rows, got_ref, sorted_ref, part_ref, field_ref, low_ref, turned_ref):
    for col in range(cols):
        place = pl.ds(col * rows, rows)
        turned = sorted_ref[RIM * 2 * cols + col].T
        turned_ref[col] = turned
        field = part_ref[col] + 2.0 * product(got_ref[place, :], turned)
        field_ref[col] = field
        low_ref[place, :] = field.astype(jnp.bfloat16)


def first_inner_body(cols, rows, probe_outer, probe_inner, got_ref, sorted_ref, part_ref,
                     weights_ref, cos_ref, sin_ref, field_outer, low_outer,
                     field_inner, low_inner, part_outer, part_inner, send_ref, terms_ref,
                     turned_ref):
    tiles = 2 * cols
    fields, low, probes = (field_outer, field_inner), (low_outer, low_inner), (probe_outer, probe_inner)
    for col in range(cols):
        place = pl.ds(col * rows, rows)
        turned = sorted_ref[RIM * tiles + cols + col].T
        turned_ref[col] = turned
        field = part_ref[col] + 2.0 * product(got_ref[place, :], turned)
        field_inner[col] = field
        low_inner[place, :] = field.astype(jnp.bfloat16)

    def matrix(kind, source):
        return sorted_ref[kind * tiles + source]

    for tile in range(tiles):
        row, col = divmod(tile, cols)
        place = pl.ds(col * rows, rows)
        probe_low = probes[row][place, :]
        probe = probe_low.astype(jnp.float32)
        field = fields[row][col]
        total = local_hop(cols, rows, *low, tile, matrix)
        following = 2.0 * total - probe + kondo(
            field, cos_ref[pl.ds(tile, 1), :], sin_ref[pl.ds(tile, 1), :]
        )
        (part_outer, part_inner)[row][col] = following
        if row == 1:
            send_ref[place, :] = following.astype(jnp.bfloat16)
        terms_ref[tile], terms_ref[tiles + tile] = overlap_terms(
            probe_low, weights_ref[0:1, 0:1] * probe + weights_ref[1:2, 0:1] * field
        )


def second_inner_body(cols, rows, probe_outer, probe_inner, got_ref, sorted_ref, turned_ref,
                      part_ref, field_ref, low_ref, share_ref, vert_ref):
    tiles = 2 * cols
    places = [pl.ds(col * rows, rows) for col in range(cols)]
    own = [
        2.0 * product(probe_inner[places[col], :], sorted_ref[RIM * tiles + cols + col])
        for col in range(cols)
    ]
    for col in range(cols):
        share_ref[col] = 2.0 * product(probe_outer[places[col], :], sorted_ref[RIM * tiles + col])
    sent = [
        got_ref[pl.ds((cols + col) * rows, rows), :].astype(jnp.float32) for col in range(cols)
    ]
    rims = [(sent[col] + own[col]).astype(jnp.bfloat16) for col in range(cols)]
    fields = [
        part_ref[col] + 2.0 * product(rims[col], turned_ref[col]) for col in range(cols)
    ]
    lows = [field.astype(jnp.bfloat16) for field in fields]
    verts = [product(lows[col], sorted_ref[VERT * tiles + cols + col]) for col in range(cols)]
    for col in range(cols):
        field_ref[col] = fields[col]
        low_ref[places[col], :] = lows[col]
        vert_ref[col] = 2.0 * verts[col]


def row_sums(blocks):
    index = lax.broadcasted_iota(jnp.int32, blocks[0].shape, 0)
    shift = 4
    while shift:
        low = (index & shift) == 0
        half = len(blocks) // 2
        joined = []
        for first, second in zip(blocks[:half], blocks[half:]):
            kept, moved = jnp.where(low, first, second), jnp.where(low, second, first)
            down = pltpu.roll(moved, shift, 0)
            if shift == 4:
                joined.append(kept + down)
            else:
                joined.append(kept + jnp.where(low, pltpu.roll(moved, 8 - shift, 0), down))
        blocks = joined
        shift //= 2
    return blocks[0]


def second_outer_body(cols, rows, got_ref, share_ref, vert_ref, sorted_ref, turned_ref, part_ref,
                      field_before, cos_ref, sin_ref, rim_probe, weights_ref,
                      field_ref, low_ref, next_ref, send_ref):
    tiles = 2 * cols
    places = [pl.ds(col * rows, rows) for col in range(cols)]
    rims = [
        (got_ref[places[col], :].astype(jnp.float32) + share_ref[col]).astype(jnp.bfloat16)
        for col in range(cols)
    ]
    fields = [
        part_ref[col] + 2.0 * product(rims[col], turned_ref[col]) for col in range(cols)
    ]
    for col in range(cols):
        field_ref[col] = fields[col]
        low_ref[places[col], :] = fields[col].astype(jnp.bfloat16)

    def matrix(kind, source):
        return sorted_ref[kind * tiles + source]

    totals = [beside(cols, rows, low_ref, col, matrix) for col in range(cols)]
    following = [
        2.0 * totals[col] + vert_ref[col] + kondo(
            fields[col], cos_ref[pl.ds(col, 1), :], sin_ref[pl.ds(col, 1), :]
        ) - field_before[col]
        for col in range(cols)
    ]
    crossed = [
        product(following[col].astype(jnp.bfloat16), matrix(RIM, col)) for col in range(cols)
    ]
    terms = [overlap_terms(rim_probe[places[col], :], crossed[col]) for col in range(cols)]
    sums = (2.0 * weights_ref[4:5, 0:1]) * row_sums(
        [same for same, _ in terms] + [cross for _, cross in terms]
    )
    rest = sums - sums.astype(jnp.bfloat16).astype(jnp.float32)
    for col in range(cols):
        next_ref[col] = following[col]
        send_ref[places[col], :] = part_ref[col].astype(jnp.bfloat16)
    send_ref[pl.ds(cols * rows, 16), :] = jnp.concatenate([sums, rest], axis=0).astype(jnp.bfloat16)


def second_rest_body(cols, rows, probe_outer, probe_inner, sorted_ref, terms_ref, weights_ref,
                     cos_ref, sin_ref, field_outer, field_inner, low_outer, low_inner,
                     field_before, next_ref, send_ref, out_ref):
    tiles = 2 * cols

    def matrix(kind, source):
        return sorted_ref[kind * tiles + source]

    for col in range(cols):
        tile = cols + col
        place = pl.ds(col * rows, rows)
        total = local_hop(cols, rows, low_outer, low_inner, tile, matrix)
        following = 2.0 * total - field_before[col] + kondo(
            field_inner[col], cos_ref[pl.ds(tile, 1), :], sin_ref[pl.ds(tile, 1), :]
        )
        next_ref[col] = following
        send_ref[place, :] = following.astype(jnp.bfloat16)
    weight = weights_ref[2:3, 0:1]
    for tile in range(tiles):
        row, col = divmod(tile, cols)
        probe = (probe_outer, probe_inner)[row][pl.ds(col * rows, rows), :]
        same, cross = overlap_terms(probe, (field_outer, field_inner)[row][col])
        out_ref[tile] = terms_ref[tile] + weight * same
        out_ref[tiles + tile] = terms_ref[tiles + tile] + weight * cross


def last_inner_body(cols, rows, probe_outer, probe_inner, got_2, got_3, low_1_outer, low_1_inner,
                    low_2_outer, low_2_inner, field_outer, field_inner, sorted_ref, turned_outer,
                    turned_inner, part_ref, terms_ref, weights_ref, cos_ref, sin_ref,
                    out_ref, halo_2_ref, low_ref):
    tiles = 2 * cols
    weight, weight_next = weights_ref[3:4, 0:1], weights_ref[4:5, 0:1]
    places = [pl.ds(col * rows, rows) for col in range(cols)]

    def matrix(kind, tile):
        return sorted_ref[kind * tiles + tile]

    def rims(got_ref, low_before):
        own = [
            2.0 * product(low_before[places[col], :], matrix(RIM, cols + col))
            for col in range(cols)
        ]
        return [
            (got_ref[places[col], :].astype(jnp.float32) + own[col]).astype(jnp.bfloat16)
            for col in range(cols)
        ]

    rim_2, rim_3 = rims(got_2, low_1_inner), rims(got_3, low_2_inner)
    crossed = [
        (2.0 * product(low_2_outer[places[col], :], matrix(RIM, col))).astype(jnp.bfloat16)
        for col in range(cols)
    ]
    fields = [
        part_ref[col] + 2.0 * product(rim_2[col], turned_inner[col]) for col in range(cols)
    ]
    for col in range(cols):
        low_ref[places[col], :] = fields[col].astype(jnp.bfloat16)
        halo_2_ref[col] = 2.0 * product(low_1_outer[places[col], :], matrix(RIM, col))
    for tile in range(tiles):
        row, col = divmod(tile, cols)
        if row == 0:
            total = product(low_ref[places[col], :], matrix(VERT, cols + col))
            total += product(crossed[col], turned_outer[col])
            vectors = weight_next * (2.0 * total - field_outer[col])
            probe = probe_outer[places[col], :]
        else:
            total = beside(cols, rows, low_ref, tile, matrix)
            total += product(rim_3[col], turned_inner[col])
            following = 2.0 * total - field_inner[col] + kondo(
                fields[col], cos_ref[pl.ds(tile, 1), :], sin_ref[pl.ds(tile, 1), :]
            )
            vectors = weight * fields[col] + weight_next * following
            probe = probe_inner[places[col], :]
        same, cross = overlap_terms(probe, vectors)
        out_ref[tile] = terms_ref[tile] + same
        out_ref[tiles + tile] = terms_ref[tiles + tile] + cross


def last_outer_body(cols, rows, probe_outer, probe_inner, got_ref, halo_2_ref, sorted_ref,
                    turned_ref, part_ref, terms_ref, weights_ref, cos_ref, sin_ref, same_ref,
                    cross_ref, out_ref, low_ref):
    tiles = 2 * cols
    weight, weight_next = weights_ref[3:4, 0:1], weights_ref[4:5, 0:1]
    places = [pl.ds(col * rows, rows) for col in range(cols)]

    def matrix(kind, tile):
        return sorted_ref[kind * tiles + tile]

    rims = [
        (got_ref[places[col], :].astype(jnp.float32) + halo_2_ref[col]).astype(jnp.bfloat16)
        for col in range(cols)
    ]
    fields = [
        part_ref[col] + 2.0 * product(rims[col], turned_ref[col]) for col in range(cols)
    ]
    for col in range(cols):
        low_ref[places[col], :] = fields[col].astype(jnp.bfloat16)
    totals = [beside(cols, rows, low_ref, col, matrix) for col in range(cols)]
    verts = [product(low_ref[places[col], :], matrix(VERT, col)) for col in range(cols)]
    shares = []
    for tile in range(tiles):
        row, col = divmod(tile, cols)
        one = pl.ds(tile, 1)
        if row == 0:
            following = 2.0 * totals[col] + kondo(fields[col], cos_ref[one, :], sin_ref[one, :])
            vectors = weight * fields[col] + weight_next * following
            probe = probe_outer[places[col], :]
        else:
            vectors = (2.0 * weight_next) * verts[col]
            probe = probe_inner[places[col], :]
        same, cross = overlap_terms(probe, vectors)
        shares.append(
            same_ref[one, :] * (terms_ref[tile] + same)
            + cross_ref[one, :] * (terms_ref[tiles + tile] + cross)
        )
    sent = got_ref[pl.ds(cols * rows, 16), :].astype(jnp.float32)
    sent = sent[:tiles] + sent[tiles:]
    across = same_ref[:cols, :] * sent[:cols] + cross_ref[:cols, :] * sent[cols:]
    share = row_sums(shares) + jnp.concatenate([across, jnp.zeros_like(across)], axis=0)
    for peer in range(out_ref.shape[0]):
        out_ref[peer] = share


def force_body(shares_ref, force_ref, largest_ref):
    force = shares_ref[0]
    for peer in range(1, shares_ref.shape[0]):
        force += shares_ref[peer]
    force_ref[...] = force
    largest_ref[...] = jnp.full(largest_ref.shape, jnp.max(jnp.abs(force)), jnp.float32)


def move_body(parity_ref, largest_ref, force_ref, angles_ref, noise_ref, next_ref, out_ref):
    parity = parity_ref[0]
    cols = out_ref.shape[1]
    largest = jnp.max(largest_ref[...])
    step_size = jnp.full((1, 1), STEP_MAX, jnp.float32) / (largest + 1e-06)
    kick = jnp.sqrt(TWO_TEMP * step_size)
    for row in range(2):
        origin = row + parity - 2 * row * parity
        force = force_ref[pl.ds(row * cols, cols), :]
        out_ref[origin] = force
        next_ref[origin] = angles_ref[origin] + step_size * force + kick * noise_ref[origin]


def exchange_outer(outer):
    count = lax.axis_size("site")
    pairs = [(i, (i + 1) % count if i % 2 else (i - 1) % count) for i in range(count)]
    return lax.ppermute(outer, "site", pairs)


def exchange_inner(inner):
    return lax.ppermute(inner, "site", [(i, i ^ 1) for i in range(lax.axis_size("site"))])


def local(angles, coupling, thermal_noise, coefficients, probes, hopping, offsets):
    cols, orbitals, share, width = probes.shape[1:]
    rows = orbitals * share
    tiles = 2 * cols
    f32, bf16 = jnp.float32, jnp.bfloat16
    side = ((cols * rows, width), bf16)
    pair = ((2 * cols * rows, width), bf16)
    row = ((cols, rows, width), f32)
    matrices = ((cols, width, width), bf16)
    terms_like = ((2 * tiles, 8, width), f32)
    row_like = ((tiles, width), f32)
    sites, peers = lax.axis_size("site"), lax.axis_size("probe")
    probe_total = peers * share
    local_flops = 2 * 3 * tiles * rows * width * width
    parity = (lax.axis_index("site") % 2).astype(jnp.int32).reshape(1)

    def run(body, outs, args, scratch=(), flops=0):
        return call(
            functools.partial(body, cols, rows), outs, [IN_VMEM] * len(args),
            tuple(held(x) for x in args), scratch=scratch, flops=flops,
        )

    fetched = pl.pallas_call(
        fetch_body,
        out_shape=[
            pltpu.VMEM(*side), pltpu.VMEM(*side), pltpu.SMEM(offsets.shape, jnp.int32),
            pltpu.SMEM(coefficients.shape, f32), pltpu.VMEM(angles.shape, f32),
            pltpu.VMEM(coupling.shape, f32),
        ],
        in_specs=[IN_SMEM] + [IN_HBM] * 5,
        out_specs=[IN_VMEM, IN_VMEM, IN_SMEM, IN_SMEM, IN_VMEM, IN_VMEM],
        scratch_shapes=[pltpu.SemaphoreType.DMA((6,))],
        compiler_params=pltpu.CompilerParams(vmem_limit_bytes=16 * 1024 * 1024),
        cost_estimate=pl.CostEstimate(flops=20 * local_flops, bytes_accessed=0, transcendentals=0),
    )(parity, *(held(x, pltpu.HBM) for x in (
        probes.reshape(2, cols * rows, width), offsets, coefficients, angles, coupling)))
    outer, inner, offsets_held, coef_held, angles_held, coupling_held = fetched
    probe_rows = [outer, inner]
    got_0 = exchange_outer(outer)

    (sorted_hop, part_outer, part_inner, send, send_pair, weights, twice_cos, twice_sin,
     same_factor, cross_factor) = call(
        functools.partial(first_body, cols, rows, probe_total),
        [((4 * tiles, width, width), bf16), row, row, side, pair, ((8, 128), f32)]
        + [row_like] * 4,
        [IN_SMEM] * 3 + [IN_VMEM] * 5,
        (parity, held(offsets_held, pltpu.SMEM), held(coef_held, pltpu.SMEM),
         *(held(x) for x in (hopping.reshape(-1, width, width), angles_held, coupling_held,
                             outer, inner))),
        flops=local_flops, moved=hopping.size * 2,
    )
    got_1 = exchange_outer(send)
    from_inner = exchange_inner(send_pair)
    trig = [twice_cos, twice_sin]

    field_1_outer, low_1_outer, turned_outer = run(
        first_outer_body, [row, side, matrices], [got_0, sorted_hop, part_outer],
        flops=20 * local_flops,
    )
    (field_1_inner, low_1_inner, part_outer, part_inner, send, terms, turned_inner) = run(
        first_inner_body, [row, side, row, row, side, terms_like, matrices],
        [*probe_rows, from_inner, sorted_hop, part_inner, weights, *trig,
         field_1_outer, low_1_outer],
        flops=local_flops,
    )
    inner_2 = exchange_inner(send)
    field_2_inner, low_2_inner, rim_share, vert = run(
        second_inner_body, [row, side, row, row],
        [*probe_rows, from_inner, sorted_hop, turned_inner, part_inner],
    )
    field_2_outer, low_2_outer, part_outer, send = run(
        second_outer_body, [row, side, row, ((cols * rows + 16, width), bf16)],
        [got_1, rim_share, vert, sorted_hop, turned_outer, part_outer, field_1_outer, *trig,
         got_0, weights],
    )
    got_2 = exchange_outer(send)
    part_inner, send, terms = run(
        second_rest_body, [row, side, terms_like],
        [*probe_rows, sorted_hop, terms, weights, *trig, field_2_outer, field_2_inner,
         low_2_outer, low_2_inner, field_1_inner],
    )
    inner_3 = exchange_inner(send)
    terms, halo_2 = run(
        last_inner_body, [terms_like, row],
        [*probe_rows, inner_2, inner_3, low_1_outer, low_1_inner, low_2_outer, low_2_inner,
         field_2_outer, field_2_inner, sorted_hop, turned_outer, turned_inner, part_inner,
         terms, weights, *trig],
        scratch=[pltpu.VMEM(*side)],
    )
    shares = run(
        last_outer_body, [((peers, tiles, width), f32)],
        [*probe_rows, got_2, halo_2, sorted_hop, turned_outer, part_outer, terms,
         weights, *trig, same_factor, cross_factor],
        scratch=[pltpu.VMEM(*side)], flops=local_flops,
    )[0]
    shares = lax.all_to_all(shares, "probe", 0, 0)
    force, largest = call(
        force_body, [row_like, ((sites, 1, 128), f32)], [IN_VMEM], (held(shares),)
    )
    near = [
        [strip * peers + (peer + strip // (sites // 2) * (peers // 2)) % peers
         for strip in range(sites)]
        for peer in range(peers)
    ]
    largest = lax.all_to_all(largest, ("site", "probe"), 0, 0, axis_index_groups=near)
    return pl.pallas_call(
        move_body,
        out_shape=[jax.ShapeDtypeStruct(angles.shape, f32)] * 2,
        in_specs=[IN_SMEM] + [IN_VMEM] * 4,
        out_specs=[IN_VMEM] * 2,
    )(parity, held(largest), held(force), held(angles), held(thermal_noise))


def solution(mesh):
    in_specs = (
        P("site", None, None),
        P("site", None, None),
        P("site", None, None),
        P(),
        P("site", None, None, "probe", None),
        P("site", None, None, None, None),
        P("site", None, None),
    )
    out_specs = (P("site", None, None), P("site", None, None))
    return jax.shard_map(local, mesh=mesh, in_specs=in_specs, out_specs=out_specs, check_vma=False)
```

```python
import functools
import jax
import jax.numpy as jnp
from jax import lax
from jax.experimental import pallas as pl
from jax.experimental.pallas import tpu as pltpu
from jax.sharding import PartitionSpec as P

BAND = 8.0
STEP_MAX = 0.3
TWO_TEMP = 0.1

VERT, LEFT, RIGHT, RIM = range(4)
IN_VMEM = pl.BlockSpec(memory_space=pltpu.VMEM)
IN_SMEM = pl.BlockSpec(memory_space=pltpu.SMEM)
IN_HBM = pl.BlockSpec(memory_space=pltpu.HBM)


def held(array, space=pltpu.VMEM):
    return pltpu.with_memory_space_constraint(array, space)


def call(body, outs, in_specs, args, scratch=(), flops=0, moved=0):
    return pl.pallas_call(
        body,
        out_shape=[pltpu.VMEM(shape, dtype) for shape, dtype in outs],
        in_specs=in_specs,
        out_specs=[IN_VMEM] * len(outs),
        scratch_shapes=list(scratch),
        compiler_params=pltpu.CompilerParams(vmem_limit_bytes=16 * 1024 * 1024),
        cost_estimate=pl.CostEstimate(flops=flops, bytes_accessed=moved, transcendentals=0),
    )(*args)


def product(vectors, matrix):
    return jnp.dot(vectors, matrix, preferred_element_type=jnp.float32)


def folded(values):
    return jnp.sum(values.reshape(-1, 8, values.shape[-1]), axis=0)


def overlap_terms(probe, vectors):
    half = probe.shape[0] // 2
    upper_r = probe[:half].astype(jnp.float32)
    lower_r = probe[half:].astype(jnp.float32)
    upper_w, lower_w = vectors[:half], vectors[half:]
    same = folded(upper_r * upper_w - lower_r * lower_w)
    cross = folded(upper_r * lower_w + lower_r * upper_w)
    return same, cross


def fetch_body(parity_ref, probes_hbm, offsets_hbm, coef_hbm, angles_hbm, coupling_hbm,
               outer_ref, inner_ref, offsets_ref, coef_ref, angles_ref, coupling_ref, sems):
    parity = parity_ref[0]
    copies = [
        pltpu.make_async_copy(source, target, sems.at[k])
        for k, (source, target) in enumerate((
            (probes_hbm.at[parity], outer_ref),
            (probes_hbm.at[1 - parity], inner_ref),
            (offsets_hbm, offsets_ref),
            (coef_hbm, coef_ref),
            (angles_hbm, angles_ref),
            (coupling_hbm, coupling_ref),
        ))
    ]
    for copy in copies:
        copy.start()
    for copy in copies:
        copy.wait()


def beside(cols, rows, low_ref, tile, matrix):
    row, col = divmod(tile, cols)
    right, left = (col + 1) % cols, (col - 1) % cols
    return product(
        low_ref[pl.ds(right * rows, rows), :], matrix(LEFT, row * cols + right)
    ) + product(low_ref[pl.ds(left * rows, rows), :], matrix(RIGHT, row * cols + left))


def local_hop(cols, rows, outer_ref, inner_ref, tile, matrix):
    refs = (outer_ref, inner_ref)
    row, col = divmod(tile, cols)
    total = product(
        refs[1 - row][pl.ds(col * rows, rows), :], matrix(VERT, (1 - row) * cols + col)
    )
    return total + beside(cols, rows, refs[row], tile, matrix)


def kondo(vectors, twice_cos, twice_sin):
    half = vectors.shape[0] // 2
    upper, lower = vectors[:half], vectors[half:]
    return jnp.concatenate(
        [twice_cos * upper + twice_sin * lower, twice_sin * upper - twice_cos * lower], axis=0
    )


def first_body(cols, rows, probe_total, parity_ref, offsets_ref, coef_ref, raw_ref, angles_ref,
               coupling_ref, outer_ref, inner_ref, sorted_ref, part_outer, part_inner, send_ref,
               pair_ref, weights_ref, cos_ref, sin_ref, same_ref, cross_ref):
    tiles = 2 * cols
    slots = offsets_ref.shape[2]
    parity = parity_ref[0]

    def tile_of(kind, tile):
        row, col = divmod(tile, cols)
        origin = row + parity - 2 * row * parity
        if kind == LEFT:
            code = 3
        elif kind == RIGHT:
            code = 5
        else:
            towards_high = (row == 0) == (kind == VERT)
            code = 7 - 6 * parity if towards_high else 1 + 6 * parity
        slot = jnp.int32(0)
        for k in range(1, slots):
            slot += jnp.where(offsets_ref[origin, col, k] == code, k, 0)
        return (origin * cols + col) * slots + slot

    def matrix(kind, tile):
        found = raw_ref[tile_of(kind, tile)]
        sorted_ref[kind * tiles + tile] = found
        return found

    for row in range(2):
        origin = row + parity - 2 * row * parity
        place = pl.ds(row * cols, cols)
        angles, strength = angles_ref[origin], coupling_ref[origin]
        cosines, sine_values = jnp.cos(angles), jnp.sin(angles)
        scale = (-BAND / probe_total) * strength
        cos_ref[place, :] = 2.0 * strength * cosines
        sin_ref[place, :] = 2.0 * strength * sine_values
        same_ref[place, :] = -scale * sine_values
        cross_ref[place, :] = scale * cosines
    for level in range(coef_ref.shape[0]):
        weights_ref[pl.ds(level, 1), :] = jnp.full(
            (1, weights_ref.shape[1]), (level + 1) * coef_ref[level], jnp.float32
        )
    for tile in range(tiles):
        row, col = divmod(tile, cols)
        place = pl.ds(col * rows, rows)
        probe = (outer_ref, inner_ref)[row][place, :]
        total = local_hop(cols, rows, outer_ref, inner_ref, tile, matrix)
        part = 2.0 * total + kondo(
            probe.astype(jnp.float32), cos_ref[pl.ds(tile, 1), :], sin_ref[pl.ds(tile, 1), :]
        )
        (part_outer, part_inner)[row][col] = part
        if row == 0:
            send_ref[place, :] = part.astype(jnp.bfloat16)
        else:
            pair_ref[place, :] = probe
            pair_ref[pl.ds((cols + col) * rows, rows), :] = part.astype(jnp.bfloat16)
    for tile in range(tiles):
        matrix(RIM, tile)


def first_outer_body(cols, rows, got_ref, sorted_ref, part_ref, field_ref, low_ref, turned_ref):
    for col in range(cols):
        place = pl.ds(col * rows, rows)
        turned = sorted_ref[RIM * 2 * cols + col].T
        turned_ref[col] = turned
        field = part_ref[col] + 2.0 * product(got_ref[place, :], turned)
        field_ref[col] = field
        low_ref[place, :] = field.astype(jnp.bfloat16)


def first_inner_body(cols, rows, probe_outer, probe_inner, got_ref, sorted_ref, part_ref,
                     weights_ref, cos_ref, sin_ref, field_outer, low_outer,
                     field_inner, low_inner, part_outer, part_inner, send_ref, terms_ref,
                     turned_ref):
    tiles = 2 * cols
    fields, low, probes = (field_outer, field_inner), (low_outer, low_inner), (probe_outer, probe_inner)
    for col in range(cols):
        place = pl.ds(col * rows, rows)
        turned = sorted_ref[RIM * tiles + cols + col].T
        turned_ref[col] = turned
        field = part_ref[col] + 2.0 * product(got_ref[place, :], turned)
        field_inner[col] = field
        low_inner[place, :] = field.astype(jnp.bfloat16)

    def matrix(kind, source):
        return sorted_ref[kind * tiles + source]

    for tile in range(tiles):
        row, col = divmod(tile, cols)
        place = pl.ds(col * rows, rows)
        probe_low = probes[row][place, :]
        probe = probe_low.astype(jnp.float32)
        field = fields[row][col]
        total = local_hop(cols, rows, *low, tile, matrix)
        following = 2.0 * total - probe + kondo(
            field, cos_ref[pl.ds(tile, 1), :], sin_ref[pl.ds(tile, 1), :]
        )
        (part_outer, part_inner)[row][col] = following
        if row == 1:
            send_ref[place, :] = following.astype(jnp.bfloat16)
        terms_ref[tile], terms_ref[tiles + tile] = overlap_terms(
            probe_low, weights_ref[0:1, 0:1] * probe + weights_ref[1:2, 0:1] * field
        )


def second_inner_body(cols, rows, probe_outer, probe_inner, got_ref, sorted_ref, turned_ref,
                      part_ref, field_ref, low_ref, share_ref, vert_ref):
    tiles = 2 * cols
    places = [pl.ds(col * rows, rows) for col in range(cols)]
    own = [
        2.0 * product(probe_inner[places[col], :], sorted_ref[RIM * tiles + cols + col])
        for col in range(cols)
    ]
    for col in range(cols):
        share_ref[col] = 2.0 * product(probe_outer[places[col], :], sorted_ref[RIM * tiles + col])
    sent = [
        got_ref[pl.ds((cols + col) * rows, rows), :].astype(jnp.float32) for col in range(cols)
    ]
    rims = [(sent[col] + own[col]).astype(jnp.bfloat16) for col in range(cols)]
    fields = [
        part_ref[col] + 2.0 * product(rims[col], turned_ref[col]) for col in range(cols)
    ]
    lows = [field.astype(jnp.bfloat16) for field in fields]
    verts = [product(lows[col], sorted_ref[VERT * tiles + cols + col]) for col in range(cols)]
    for col in range(cols):
        field_ref[col] = fields[col]
        low_ref[places[col], :] = lows[col]
        vert_ref[col] = 2.0 * verts[col]


def row_sums(blocks):
    index = lax.broadcasted_iota(jnp.int32, blocks[0].shape, 0)
    shift = 4
    while shift:
        low = (index & shift) == 0
        half = len(blocks) // 2
        joined = []
        for first, second in zip(blocks[:half], blocks[half:]):
            kept, moved = jnp.where(low, first, second), jnp.where(low, second, first)
            down = pltpu.roll(moved, shift, 0)
            if shift == 4:
                joined.append(kept + down)
            else:
                joined.append(kept + jnp.where(low, pltpu.roll(moved, 8 - shift, 0), down))
        blocks = joined
        shift //= 2
    return blocks[0]


def second_outer_body(cols, rows, got_ref, share_ref, vert_ref, sorted_ref, turned_ref, part_ref,
                      field_before, cos_ref, sin_ref, rim_probe, weights_ref,
                      field_ref, low_ref, next_ref, send_ref):
    tiles = 2 * cols
    places = [pl.ds(col * rows, rows) for col in range(cols)]
    rims = [
        (got_ref[places[col], :].astype(jnp.float32) + share_ref[col]).astype(jnp.bfloat16)
        for col in range(cols)
    ]
    fields = [
        part_ref[col] + 2.0 * product(rims[col], turned_ref[col]) for col in range(cols)
    ]
    for col in range(cols):
        field_ref[col] = fields[col]
        low_ref[places[col], :] = fields[col].astype(jnp.bfloat16)

    def matrix(kind, source):
        return sorted_ref[kind * tiles + source]

    totals = [beside(cols, rows, low_ref, col, matrix) for col in range(cols)]
    following = [
        2.0 * totals[col] + vert_ref[col] + kondo(
            fields[col], cos_ref[pl.ds(col, 1), :], sin_ref[pl.ds(col, 1), :]
        ) - field_before[col]
        for col in range(cols)
    ]
    crossed = [
        product(following[col].astype(jnp.bfloat16), matrix(RIM, col)) for col in range(cols)
    ]
    terms = [overlap_terms(rim_probe[places[col], :], crossed[col]) for col in range(cols)]
    sums = (2.0 * weights_ref[4:5, 0:1]) * row_sums(
        [same for same, _ in terms] + [cross for _, cross in terms]
    )
    rest = sums - sums.astype(jnp.bfloat16).astype(jnp.float32)
    for col in range(cols):
        next_ref[col] = following[col]
        send_ref[places[col], :] = part_ref[col].astype(jnp.bfloat16)
    send_ref[pl.ds(cols * rows, 16), :] = jnp.concatenate([sums, rest], axis=0).astype(jnp.bfloat16)


def second_rest_body(cols, rows, probe_outer, probe_inner, sorted_ref, terms_ref, weights_ref,
                     cos_ref, sin_ref, field_outer, field_inner, low_outer, low_inner,
                     field_before, next_ref, send_ref, out_ref):
    tiles = 2 * cols

    def matrix(kind, source):
        return sorted_ref[kind * tiles + source]

    for col in range(cols):
        tile = cols + col
        place = pl.ds(col * rows, rows)
        total = local_hop(cols, rows, low_outer, low_inner, tile, matrix)
        following = 2.0 * total - field_before[col] + kondo(
            field_inner[col], cos_ref[pl.ds(tile, 1), :], sin_ref[pl.ds(tile, 1), :]
        )
        next_ref[col] = following
        send_ref[place, :] = following.astype(jnp.bfloat16)
    weight = weights_ref[2:3, 0:1]
    for tile in range(tiles):
        row, col = divmod(tile, cols)
        probe = (probe_outer, probe_inner)[row][pl.ds(col * rows, rows), :]
        same, cross = overlap_terms(probe, (field_outer, field_inner)[row][col])
        out_ref[tile] = terms_ref[tile] + weight * same
        out_ref[tiles + tile] = terms_ref[tiles + tile] + weight * cross


def last_inner_body(cols, rows, probe_outer, probe_inner, got_2, got_3, low_1_outer, low_1_inner,
                    low_2_outer, low_2_inner, field_outer, field_inner, sorted_ref, turned_outer,
                    turned_inner, part_ref, terms_ref, weights_ref, cos_ref, sin_ref,
                    out_ref, halo_2_ref, low_ref):
    tiles = 2 * cols
    weight, weight_next = weights_ref[3:4, 0:1], weights_ref[4:5, 0:1]
    places = [pl.ds(col * rows, rows) for col in range(cols)]

    def matrix(kind, tile):
        return sorted_ref[kind * tiles + tile]

    def rims(got_ref, low_before):
        own = [
            2.0 * product(low_before[places[col], :], matrix(RIM, cols + col))
            for col in range(cols)
        ]
        return [
            (got_ref[places[col], :].astype(jnp.float32) + own[col]).astype(jnp.bfloat16)
            for col in range(cols)
        ]

    rim_2, rim_3 = rims(got_2, low_1_inner), rims(got_3, low_2_inner)
    crossed = [
        (2.0 * product(low_2_outer[places[col], :], matrix(RIM, col))).astype(jnp.bfloat16)
        for col in range(cols)
    ]
    fields = [
        part_ref[col] + 2.0 * product(rim_2[col], turned_inner[col]) for col in range(cols)
    ]
    for col in range(cols):
        low_ref[places[col], :] = fields[col].astype(jnp.bfloat16)
        halo_2_ref[col] = 2.0 * product(low_1_outer[places[col], :], matrix(RIM, col))
    for tile in range(tiles):
        row, col = divmod(tile, cols)
        if row == 0:
            total = product(low_ref[places[col], :], matrix(VERT, cols + col))
            total += product(crossed[col], turned_outer[col])
            vectors = weight_next * (2.0 * total - field_outer[col])
            probe = probe_outer[places[col], :]
        else:
            total = beside(cols, rows, low_ref, tile, matrix)
            total += product(rim_3[col], turned_inner[col])
            following = 2.0 * total - field_inner[col] + kondo(
                fields[col], cos_ref[pl.ds(tile, 1), :], sin_ref[pl.ds(tile, 1), :]
            )
            vectors = weight * fields[col] + weight_next * following
            probe = probe_inner[places[col], :]
        same, cross = overlap_terms(probe, vectors)
        out_ref[tile] = terms_ref[tile] + same
        out_ref[tiles + tile] = terms_ref[tiles + tile] + cross


def last_outer_body(cols, rows, probe_outer, probe_inner, got_ref, halo_2_ref, sorted_ref,
                    turned_ref, part_ref, terms_ref, weights_ref, cos_ref, sin_ref, same_ref,
                    cross_ref, out_ref, low_ref):
    tiles = 2 * cols
    weight, weight_next = weights_ref[3:4, 0:1], weights_ref[4:5, 0:1]
    places = [pl.ds(col * rows, rows) for col in range(cols)]

    def matrix(kind, tile):
        return sorted_ref[kind * tiles + tile]

    rims = [
        (got_ref[places[col], :].astype(jnp.float32) + halo_2_ref[col]).astype(jnp.bfloat16)
        for col in range(cols)
    ]
    fields = [
        part_ref[col] + 2.0 * product(rims[col], turned_ref[col]) for col in range(cols)
    ]
    for col in range(cols):
        low_ref[places[col], :] = fields[col].astype(jnp.bfloat16)
    totals = [beside(cols, rows, low_ref, col, matrix) for col in range(cols)]
    verts = [product(low_ref[places[col], :], matrix(VERT, col)) for col in range(cols)]
    shares = []
    for tile in range(tiles):
        row, col = divmod(tile, cols)
        one = pl.ds(tile, 1)
        if row == 0:
            following = 2.0 * totals[col] + kondo(fields[col], cos_ref[one, :], sin_ref[one, :])
            vectors = weight * fields[col] + weight_next * following
            probe = probe_outer[places[col], :]
        else:
            vectors = (2.0 * weight_next) * verts[col]
            probe = probe_inner[places[col], :]
        same, cross = overlap_terms(probe, vectors)
        shares.append(
            same_ref[one, :] * (terms_ref[tile] + same)
            + cross_ref[one, :] * (terms_ref[tiles + tile] + cross)
        )
    sent = got_ref[pl.ds(cols * rows, 16), :].astype(jnp.float32)
    sent = sent[:tiles] + sent[tiles:]
    across = same_ref[:cols, :] * sent[:cols] + cross_ref[:cols, :] * sent[cols:]
    share = row_sums(shares) + jnp.concatenate([across, jnp.zeros_like(across)], axis=0)
    for peer in range(out_ref.shape[0]):
        out_ref[peer] = share


def force_body(parity_ref, shares_ref, force_ref, largest_ref):
    peers = shares_ref.shape[0] // 2
    strips = []
    for strip in range(2):
        total = shares_ref[strip * peers]
        for peer in range(1, peers):
            total += shares_ref[strip * peers + peer]
        strips.append(total)
    force_ref[...] = jnp.where(parity_ref[0] == 0, strips[0], strips[1])
    largest = jnp.max(jnp.maximum(jnp.abs(strips[0]), jnp.abs(strips[1])))
    largest_ref[...] = jnp.full(largest_ref.shape, largest, jnp.float32)


def move_body(parity_ref, largest_ref, force_ref, angles_ref, noise_ref, next_ref, out_ref):
    parity = parity_ref[0]
    cols = out_ref.shape[1]
    largest = jnp.max(largest_ref[...])
    step_size = jnp.full((1, 1), STEP_MAX, jnp.float32) / (largest + 1e-06)
    kick = jnp.sqrt(TWO_TEMP * step_size)
    for row in range(2):
        origin = row + parity - 2 * row * parity
        force = force_ref[pl.ds(row * cols, cols), :]
        out_ref[origin] = force
        next_ref[origin] = angles_ref[origin] + step_size * force + kick * noise_ref[origin]


def exchange_outer(outer):
    count = lax.axis_size("site")
    pairs = [(i, (i + 1) % count if i % 2 else (i - 1) % count) for i in range(count)]
    return lax.ppermute(outer, "site", pairs)


def exchange_inner(inner):
    return lax.ppermute(inner, "site", [(i, i ^ 1) for i in range(lax.axis_size("site"))])


def local(angles, coupling, thermal_noise, coefficients, probes, hopping, offsets):
    cols, orbitals, share, width = probes.shape[1:]
    rows = orbitals * share
    tiles = 2 * cols
    f32, bf16 = jnp.float32, jnp.bfloat16
    side = ((cols * rows, width), bf16)
    pair = ((2 * cols * rows, width), bf16)
    row = ((cols, rows, width), f32)
    matrices = ((cols, width, width), bf16)
    terms_like = ((2 * tiles, 8, width), f32)
    row_like = ((tiles, width), f32)
    sites, peers = lax.axis_size("site"), lax.axis_size("probe")
    probe_total = peers * share
    local_flops = 2 * 3 * tiles * rows * width * width
    parity = (lax.axis_index("site") % 2).astype(jnp.int32).reshape(1)

    def run(body, outs, args, scratch=(), flops=0):
        return call(
            functools.partial(body, cols, rows), outs, [IN_VMEM] * len(args),
            tuple(held(x) for x in args), scratch=scratch, flops=flops,
        )

    fetched = pl.pallas_call(
        fetch_body,
        out_shape=[
            pltpu.VMEM(*side), pltpu.VMEM(*side), pltpu.SMEM(offsets.shape, jnp.int32),
            pltpu.SMEM(coefficients.shape, f32), pltpu.VMEM(angles.shape, f32),
            pltpu.VMEM(coupling.shape, f32),
        ],
        in_specs=[IN_SMEM] + [IN_HBM] * 5,
        out_specs=[IN_VMEM, IN_VMEM, IN_SMEM, IN_SMEM, IN_VMEM, IN_VMEM],
        scratch_shapes=[pltpu.SemaphoreType.DMA((6,))],
        compiler_params=pltpu.CompilerParams(vmem_limit_bytes=16 * 1024 * 1024),
        cost_estimate=pl.CostEstimate(flops=20 * local_flops, bytes_accessed=0, transcendentals=0),
    )(parity, *(held(x, pltpu.HBM) for x in (
        probes.reshape(2, cols * rows, width), offsets, coefficients, angles, coupling)))
    outer, inner, offsets_held, coef_held, angles_held, coupling_held = fetched
    probe_rows = [outer, inner]
    got_0 = exchange_outer(outer)

    (sorted_hop, part_outer, part_inner, send, send_pair, weights, twice_cos, twice_sin,
     same_factor, cross_factor) = call(
        functools.partial(first_body, cols, rows, probe_total),
        [((4 * tiles, width, width), bf16), row, row, side, pair, ((8, 128), f32)]
        + [row_like] * 4,
        [IN_SMEM] * 3 + [IN_VMEM] * 5,
        (parity, held(offsets_held, pltpu.SMEM), held(coef_held, pltpu.SMEM),
         *(held(x) for x in (hopping.reshape(-1, width, width), angles_held, coupling_held,
                             outer, inner))),
        flops=local_flops, moved=hopping.size * 2,
    )
    got_1 = exchange_outer(send)
    from_inner = exchange_inner(send_pair)
    trig = [twice_cos, twice_sin]

    field_1_outer, low_1_outer, turned_outer = run(
        first_outer_body, [row, side, matrices], [got_0, sorted_hop, part_outer],
        flops=20 * local_flops,
    )
    (field_1_inner, low_1_inner, part_outer, part_inner, send, terms, turned_inner) = run(
        first_inner_body, [row, side, row, row, side, terms_like, matrices],
        [*probe_rows, from_inner, sorted_hop, part_inner, weights, *trig,
         field_1_outer, low_1_outer],
        flops=local_flops,
    )
    inner_2 = exchange_inner(send)
    field_2_inner, low_2_inner, rim_share, vert = run(
        second_inner_body, [row, side, row, row],
        [*probe_rows, from_inner, sorted_hop, turned_inner, part_inner],
    )
    field_2_outer, low_2_outer, part_outer, send = run(
        second_outer_body, [row, side, row, ((cols * rows + 16, width), bf16)],
        [got_1, rim_share, vert, sorted_hop, turned_outer, part_outer, field_1_outer, *trig,
         got_0, weights],
    )
    got_2 = exchange_outer(send)
    part_inner, send, terms = run(
        second_rest_body, [row, side, terms_like],
        [*probe_rows, sorted_hop, terms, weights, *trig, field_2_outer, field_2_inner,
         low_2_outer, low_2_inner, field_1_inner],
    )
    inner_3 = exchange_inner(send)
    terms, halo_2 = run(
        last_inner_body, [terms_like, row],
        [*probe_rows, inner_2, inner_3, low_1_outer, low_1_inner, low_2_outer, low_2_inner,
         field_2_outer, field_2_inner, sorted_hop, turned_outer, turned_inner, part_inner,
         terms, weights, *trig],
        scratch=[pltpu.VMEM(*side)],
    )
    shares = run(
        last_outer_body, [((2 * peers, tiles, width), f32)],
        [*probe_rows, got_2, halo_2, sorted_hop, turned_outer, part_outer, terms,
         weights, *trig, same_factor, cross_factor],
        scratch=[pltpu.VMEM(*side)], flops=local_flops,
    )[0]
    chips = [list(range(i * 2 * peers, (i + 1) * 2 * peers)) for i in range(sites // 2)]
    shares = lax.all_to_all(shares, ("site", "probe"), 0, 0, axis_index_groups=chips)
    force, largest = call(
        force_body, [row_like, ((sites // 2, 1, 128), f32)], [IN_SMEM, IN_VMEM],
        (parity, held(shares)),
    )
    near = [
        [strip * peers + (peer + strip // (sites // 2) * (peers // 2)) % peers
         for strip in range(core, sites, 2)]
        for core in range(2) for peer in range(peers)
    ]
    largest = lax.all_to_all(largest, ("site", "probe"), 0, 0, axis_index_groups=near)
    return pl.pallas_call(
        move_body,
        out_shape=[jax.ShapeDtypeStruct(angles.shape, f32)] * 2,
        in_specs=[IN_SMEM] + [IN_VMEM] * 4,
        out_specs=[IN_VMEM] * 2,
    )(parity, held(largest), held(force), held(angles), held(thermal_noise))


def solution(mesh):
    in_specs = (
        P("site", None, None),
        P("site", None, None),
        P("site", None, None),
        P(),
        P("site", None, None, "probe", None),
        P("site", None, None, None, None),
        P("site", None, None),
    )
    out_specs = (P("site", None, None), P("site", None, None))
    return jax.shard_map(local, mesh=mesh, in_specs=in_specs, out_specs=out_specs, check_vma=False)
```

```python
import functools
import jax
import jax.numpy as jnp
from jax import lax
from jax.experimental import pallas as pl
from jax.experimental.pallas import tpu as pltpu
from jax.sharding import PartitionSpec as P

BAND = 8.0
STEP_MAX = 0.3
TWO_TEMP = 0.1

VERT, LEFT, RIGHT, RIM = range(4)
IN_VMEM = pl.BlockSpec(memory_space=pltpu.VMEM)
IN_SMEM = pl.BlockSpec(memory_space=pltpu.SMEM)
IN_HBM = pl.BlockSpec(memory_space=pltpu.HBM)


def held(array, space=pltpu.VMEM):
    return pltpu.with_memory_space_constraint(array, space)


def call(body, outs, in_specs, args, scratch=(), flops=0, moved=0):
    return pl.pallas_call(
        body,
        out_shape=[pltpu.VMEM(shape, dtype) for shape, dtype in outs],
        in_specs=in_specs,
        out_specs=[IN_VMEM] * len(outs),
        scratch_shapes=list(scratch),
        compiler_params=pltpu.CompilerParams(vmem_limit_bytes=16 * 1024 * 1024),
        cost_estimate=pl.CostEstimate(flops=flops, bytes_accessed=moved, transcendentals=0),
    )(*args)


def product(vectors, matrix):
    return jnp.dot(vectors, matrix, preferred_element_type=jnp.float32)


def folded(values):
    return jnp.sum(values.reshape(-1, 8, values.shape[-1]), axis=0)


def overlap_terms(probe, vectors):
    half = probe.shape[0] // 2
    upper_r = probe[:half].astype(jnp.float32)
    lower_r = probe[half:].astype(jnp.float32)
    upper_w, lower_w = vectors[:half], vectors[half:]
    same = folded(upper_r * upper_w - lower_r * lower_w)
    cross = folded(upper_r * lower_w + lower_r * upper_w)
    return same, cross


def fetch_body(parity_ref, probes_hbm, offsets_hbm, coef_hbm, angles_hbm, coupling_hbm,
               outer_ref, inner_ref, offsets_ref, coef_ref, angles_ref, coupling_ref, sems):
    parity = parity_ref[0]
    copies = [
        pltpu.make_async_copy(source, target, sems.at[k])
        for k, (source, target) in enumerate((
            (probes_hbm.at[parity], outer_ref),
            (probes_hbm.at[1 - parity], inner_ref),
            (offsets_hbm, offsets_ref),
            (coef_hbm, coef_ref),
            (angles_hbm, angles_ref),
            (coupling_hbm, coupling_ref),
        ))
    ]
    for copy in copies:
        copy.start()
    for copy in copies:
        copy.wait()


def beside(cols, rows, low_ref, tile, matrix):
    row, col = divmod(tile, cols)
    right, left = (col + 1) % cols, (col - 1) % cols
    return product(
        low_ref[pl.ds(right * rows, rows), :], matrix(LEFT, row * cols + right)
    ) + product(low_ref[pl.ds(left * rows, rows), :], matrix(RIGHT, row * cols + left))


def local_hop(cols, rows, outer_ref, inner_ref, tile, matrix):
    refs = (outer_ref, inner_ref)
    row, col = divmod(tile, cols)
    total = product(
        refs[1 - row][pl.ds(col * rows, rows), :], matrix(VERT, (1 - row) * cols + col)
    )
    return total + beside(cols, rows, refs[row], tile, matrix)


def kondo(vectors, twice_cos, twice_sin):
    half = vectors.shape[0] // 2
    upper, lower = vectors[:half], vectors[half:]
    return jnp.concatenate(
        [twice_cos * upper + twice_sin * lower, twice_sin * upper - twice_cos * lower], axis=0
    )


def sorter(cols, parity, offsets_ref, raw_ref, sorted_ref):
    tiles = 2 * cols
    slots = offsets_ref.shape[2]

    def tile_of(kind, tile):
        row, col = divmod(tile, cols)
        origin = row + parity - 2 * row * parity
        if kind == LEFT:
            code = 3
        elif kind == RIGHT:
            code = 5
        else:
            towards_high = (row == 0) == (kind == VERT)
            code = 7 - 6 * parity if towards_high else 1 + 6 * parity
        slot = jnp.int32(0)
        for k in range(1, slots):
            slot += jnp.where(offsets_ref[origin, col, k] == code, k, 0)
        return (origin * cols + col) * slots + slot

    def matrix(kind, tile):
        found = raw_ref[tile_of(kind, tile)]
        sorted_ref[kind * tiles + tile] = found
        return found

    return matrix


def first_body(cols, rows, probe_total, parity_ref, offsets_ref, coef_ref, raw_ref, angles_ref,
               coupling_ref, outer_ref, inner_ref, sorted_ref, part_ref, send_ref,
               weights_ref, cos_ref, sin_ref, same_ref, cross_ref):
    parity = parity_ref[0]
    matrix = sorter(cols, parity, offsets_ref, raw_ref, sorted_ref)
    for row in range(2):
        origin = row + parity - 2 * row * parity
        place = pl.ds(row * cols, cols)
        angles, strength = angles_ref[origin], coupling_ref[origin]
        cosines, sine_values = jnp.cos(angles), jnp.sin(angles)
        scale = (-BAND / probe_total) * strength
        cos_ref[place, :] = 2.0 * strength * cosines
        sin_ref[place, :] = 2.0 * strength * sine_values
        same_ref[place, :] = -scale * sine_values
        cross_ref[place, :] = scale * cosines
    for level in range(coef_ref.shape[0]):
        weights_ref[pl.ds(level, 1), :] = jnp.full(
            (1, weights_ref.shape[1]), (level + 1) * coef_ref[level], jnp.float32
        )
    for col in range(cols):
        place = pl.ds(col * rows, rows)
        total = local_hop(cols, rows, outer_ref, inner_ref, col, matrix)
        part = 2.0 * total + kondo(
            outer_ref[place, :].astype(jnp.float32), cos_ref[pl.ds(col, 1), :],
            sin_ref[pl.ds(col, 1), :]
        )
        part_ref[col] = part
        send_ref[place, :] = part.astype(jnp.bfloat16)


def first_rest_body(cols, rows, parity_ref, offsets_ref, raw_ref, outer_ref, inner_ref, cos_ref,
                    sin_ref, before_ref, sorted_ref, part_ref, pair_ref):
    tiles = 2 * cols
    for kind in (VERT, LEFT, RIGHT):
        for col in range(cols):
            place = kind * tiles + col + (cols if kind == VERT else 0)
            sorted_ref[place] = before_ref[place]
    matrix = sorter(cols, parity_ref[0], offsets_ref, raw_ref, sorted_ref)
    for col in range(cols):
        place = pl.ds(col * rows, rows)
        tile = cols + col
        probe = inner_ref[place, :]
        total = local_hop(cols, rows, outer_ref, inner_ref, tile, matrix)
        part = 2.0 * total + kondo(
            probe.astype(jnp.float32), cos_ref[pl.ds(tile, 1), :], sin_ref[pl.ds(tile, 1), :]
        )
        part_ref[col] = part
        pair_ref[place, :] = probe
        pair_ref[pl.ds(tile * rows, rows), :] = part.astype(jnp.bfloat16)
    for tile in range(2 * cols):
        matrix(RIM, tile)


def first_outer_body(cols, rows, got_ref, sorted_ref, part_ref, field_ref, low_ref, turned_ref):
    for col in range(cols):
        place = pl.ds(col * rows, rows)
        turned = sorted_ref[RIM * 2 * cols + col].T
        turned_ref[col] = turned
        field = part_ref[col] + 2.0 * product(got_ref[place, :], turned)
        field_ref[col] = field
        low_ref[place, :] = field.astype(jnp.bfloat16)


def first_inner_body(cols, rows, probe_outer, probe_inner, got_ref, sorted_ref, part_ref,
                     weights_ref, cos_ref, sin_ref, field_outer, low_outer,
                     field_inner, low_inner, part_outer, part_inner, send_ref, terms_ref,
                     turned_ref):
    tiles = 2 * cols
    fields, low, probes = (field_outer, field_inner), (low_outer, low_inner), (probe_outer, probe_inner)
    for col in range(cols):
        place = pl.ds(col * rows, rows)
        turned = sorted_ref[RIM * tiles + cols + col].T
        turned_ref[col] = turned
        field = part_ref[col] + 2.0 * product(got_ref[place, :], turned)
        field_inner[col] = field
        low_inner[place, :] = field.astype(jnp.bfloat16)

    def matrix(kind, source):
        return sorted_ref[kind * tiles + source]

    for tile in range(tiles):
        row, col = divmod(tile, cols)
        place = pl.ds(col * rows, rows)
        probe_low = probes[row][place, :]
        probe = probe_low.astype(jnp.float32)
        field = fields[row][col]
        total = local_hop(cols, rows, *low, tile, matrix)
        following = 2.0 * total - probe + kondo(
            field, cos_ref[pl.ds(tile, 1), :], sin_ref[pl.ds(tile, 1), :]
        )
        (part_outer, part_inner)[row][col] = following
        if row == 1:
            send_ref[place, :] = following.astype(jnp.bfloat16)
        terms_ref[tile], terms_ref[tiles + tile] = overlap_terms(
            probe_low, weights_ref[0:1, 0:1] * probe + weights_ref[1:2, 0:1] * field
        )


def second_inner_body(cols, rows, probe_outer, probe_inner, got_ref, sorted_ref, turned_ref,
                      part_ref, field_ref, low_ref, share_ref, vert_ref):
    tiles = 2 * cols
    places = [pl.ds(col * rows, rows) for col in range(cols)]
    own = [
        2.0 * product(probe_inner[places[col], :], sorted_ref[RIM * tiles + cols + col])
        for col in range(cols)
    ]
    for col in range(cols):
        share_ref[col] = 2.0 * product(probe_outer[places[col], :], sorted_ref[RIM * tiles + col])
    sent = [
        got_ref[pl.ds((cols + col) * rows, rows), :].astype(jnp.float32) for col in range(cols)
    ]
    rims = [(sent[col] + own[col]).astype(jnp.bfloat16) for col in range(cols)]
    fields = [
        part_ref[col] + 2.0 * product(rims[col], turned_ref[col]) for col in range(cols)
    ]
    lows = [field.astype(jnp.bfloat16) for field in fields]
    verts = [product(lows[col], sorted_ref[VERT * tiles + cols + col]) for col in range(cols)]
    for col in range(cols):
        field_ref[col] = fields[col]
        low_ref[places[col], :] = lows[col]
        vert_ref[col] = 2.0 * verts[col]


def row_sums(blocks):
    index = lax.broadcasted_iota(jnp.int32, blocks[0].shape, 0)
    shift = 4
    while shift:
        low = (index & shift) == 0
        half = len(blocks) // 2
        joined = []
        for first, second in zip(blocks[:half], blocks[half:]):
            kept, moved = jnp.where(low, first, second), jnp.where(low, second, first)
            down = pltpu.roll(moved, shift, 0)
            if shift == 4:
                joined.append(kept + down)
            else:
                joined.append(kept + jnp.where(low, pltpu.roll(moved, 8 - shift, 0), down))
        blocks = joined
        shift //= 2
    return blocks[0]


def second_outer_body(cols, rows, got_ref, share_ref, vert_ref, sorted_ref, turned_ref, part_ref,
                      field_before, cos_ref, sin_ref, rim_probe, weights_ref,
                      field_ref, low_ref, next_ref, send_ref):
    tiles = 2 * cols
    places = [pl.ds(col * rows, rows) for col in range(cols)]
    rims = [
        (got_ref[places[col], :].astype(jnp.float32) + share_ref[col]).astype(jnp.bfloat16)
        for col in range(cols)
    ]
    fields = [
        part_ref[col] + 2.0 * product(rims[col], turned_ref[col]) for col in range(cols)
    ]
    for col in range(cols):
        field_ref[col] = fields[col]
        low_ref[places[col], :] = fields[col].astype(jnp.bfloat16)

    def matrix(kind, source):
        return sorted_ref[kind * tiles + source]

    totals = [beside(cols, rows, low_ref, col, matrix) for col in range(cols)]
    following = [
        2.0 * totals[col] + vert_ref[col] + kondo(
            fields[col], cos_ref[pl.ds(col, 1), :], sin_ref[pl.ds(col, 1), :]
        ) - field_before[col]
        for col in range(cols)
    ]
    crossed = [
        product(following[col].astype(jnp.bfloat16), matrix(RIM, col)) for col in range(cols)
    ]
    terms = [overlap_terms(rim_probe[places[col], :], crossed[col]) for col in range(cols)]
    sums = (2.0 * weights_ref[4:5, 0:1]) * row_sums(
        [same for same, _ in terms] + [cross for _, cross in terms]
    )
    rest = sums - sums.astype(jnp.bfloat16).astype(jnp.float32)
    for col in range(cols):
        next_ref[col] = following[col]
        send_ref[places[col], :] = part_ref[col].astype(jnp.bfloat16)
    send_ref[pl.ds(cols * rows, 16), :] = jnp.concatenate([sums, rest], axis=0).astype(jnp.bfloat16)


def second_rest_body(cols, rows, probe_outer, probe_inner, sorted_ref, terms_ref, weights_ref,
                     cos_ref, sin_ref, field_outer, field_inner, low_outer, low_inner,
                     field_before, next_ref, send_ref, out_ref):
    tiles = 2 * cols

    def matrix(kind, source):
        return sorted_ref[kind * tiles + source]

    for col in range(cols):
        tile = cols + col
        place = pl.ds(col * rows, rows)
        total = local_hop(cols, rows, low_outer, low_inner, tile, matrix)
        following = 2.0 * total - field_before[col] + kondo(
            field_inner[col], cos_ref[pl.ds(tile, 1), :], sin_ref[pl.ds(tile, 1), :]
        )
        next_ref[col] = following
        send_ref[place, :] = following.astype(jnp.bfloat16)
    weight = weights_ref[2:3, 0:1]
    for tile in range(tiles):
        row, col = divmod(tile, cols)
        probe = (probe_outer, probe_inner)[row][pl.ds(col * rows, rows), :]
        same, cross = overlap_terms(probe, (field_outer, field_inner)[row][col])
        out_ref[tile] = terms_ref[tile] + weight * same
        out_ref[tiles + tile] = terms_ref[tiles + tile] + weight * cross


def last_inner_body(cols, rows, probe_outer, probe_inner, got_2, got_3, low_1_outer, low_1_inner,
                    low_2_outer, low_2_inner, field_outer, field_inner, sorted_ref, turned_outer,
                    turned_inner, part_ref, terms_ref, weights_ref, cos_ref, sin_ref,
                    out_ref, halo_2_ref, low_ref):
    tiles = 2 * cols
    weight, weight_next = weights_ref[3:4, 0:1], weights_ref[4:5, 0:1]
    places = [pl.ds(col * rows, rows) for col in range(cols)]

    def matrix(kind, tile):
        return sorted_ref[kind * tiles + tile]

    def rims(got_ref, low_before):
        own = [
            2.0 * product(low_before[places[col], :], matrix(RIM, cols + col))
            for col in range(cols)
        ]
        return [
            (got_ref[places[col], :].astype(jnp.float32) + own[col]).astype(jnp.bfloat16)
            for col in range(cols)
        ]

    rim_2, rim_3 = rims(got_2, low_1_inner), rims(got_3, low_2_inner)
    crossed = [
        (2.0 * product(low_2_outer[places[col], :], matrix(RIM, col))).astype(jnp.bfloat16)
        for col in range(cols)
    ]
    fields = [
        part_ref[col] + 2.0 * product(rim_2[col], turned_inner[col]) for col in range(cols)
    ]
    for col in range(cols):
        low_ref[places[col], :] = fields[col].astype(jnp.bfloat16)
        halo_2_ref[col] = 2.0 * product(low_1_outer[places[col], :], matrix(RIM, col))
    for tile in range(tiles):
        row, col = divmod(tile, cols)
        if row == 0:
            total = product(low_ref[places[col], :], matrix(VERT, cols + col))
            total += product(crossed[col], turned_outer[col])
            vectors = weight_next * (2.0 * total - field_outer[col])
            probe = probe_outer[places[col], :]
        else:
            total = beside(cols, rows, low_ref, tile, matrix)
            total += product(rim_3[col], turned_inner[col])
            following = 2.0 * total - field_inner[col] + kondo(
                fields[col], cos_ref[pl.ds(tile, 1), :], sin_ref[pl.ds(tile, 1), :]
            )
            vectors = weight * fields[col] + weight_next * following
            probe = probe_inner[places[col], :]
        same, cross = overlap_terms(probe, vectors)
        out_ref[tile] = terms_ref[tile] + same
        out_ref[tiles + tile] = terms_ref[tiles + tile] + cross


def last_outer_body(cols, rows, probe_outer, probe_inner, got_ref, halo_2_ref, sorted_ref,
                    turned_ref, part_ref, terms_ref, weights_ref, cos_ref, sin_ref, same_ref,
                    cross_ref, out_ref, low_ref):
    tiles = 2 * cols
    weight, weight_next = weights_ref[3:4, 0:1], weights_ref[4:5, 0:1]
    places = [pl.ds(col * rows, rows) for col in range(cols)]

    def matrix(kind, tile):
        return sorted_ref[kind * tiles + tile]

    rims = [
        (got_ref[places[col], :].astype(jnp.float32) + halo_2_ref[col]).astype(jnp.bfloat16)
        for col in range(cols)
    ]
    fields = [
        part_ref[col] + 2.0 * product(rims[col], turned_ref[col]) for col in range(cols)
    ]
    for col in range(cols):
        low_ref[places[col], :] = fields[col].astype(jnp.bfloat16)
    totals = [beside(cols, rows, low_ref, col, matrix) for col in range(cols)]
    verts = [product(low_ref[places[col], :], matrix(VERT, col)) for col in range(cols)]
    shares = []
    for tile in range(tiles):
        row, col = divmod(tile, cols)
        one = pl.ds(tile, 1)
        if row == 0:
            following = 2.0 * totals[col] + kondo(fields[col], cos_ref[one, :], sin_ref[one, :])
            vectors = weight * fields[col] + weight_next * following
            probe = probe_outer[places[col], :]
        else:
            vectors = (2.0 * weight_next) * verts[col]
            probe = probe_inner[places[col], :]
        same, cross = overlap_terms(probe, vectors)
        shares.append(
            same_ref[one, :] * (terms_ref[tile] + same)
            + cross_ref[one, :] * (terms_ref[tiles + tile] + cross)
        )
    sent = got_ref[pl.ds(cols * rows, 16), :].astype(jnp.float32)
    sent = sent[:tiles] + sent[tiles:]
    across = same_ref[:cols, :] * sent[:cols] + cross_ref[:cols, :] * sent[cols:]
    share = row_sums(shares) + jnp.concatenate([across, jnp.zeros_like(across)], axis=0)
    for peer in range(out_ref.shape[0]):
        out_ref[peer] = share


def force_body(parity_ref, shares_ref, force_ref, largest_ref):
    peers = shares_ref.shape[0] // 2
    strips = []
    for strip in range(2):
        total = shares_ref[strip * peers]
        for peer in range(1, peers):
            total += shares_ref[strip * peers + peer]
        strips.append(total)
    force_ref[...] = jnp.where(parity_ref[0] == 0, strips[0], strips[1])
    largest = jnp.max(jnp.maximum(jnp.abs(strips[0]), jnp.abs(strips[1])))
    largest_ref[...] = jnp.full(largest_ref.shape, largest, jnp.float32)


def move_body(parity_ref, largest_ref, force_ref, angles_ref, noise_ref, next_ref, out_ref):
    parity = parity_ref[0]
    cols = out_ref.shape[1]
    largest = jnp.max(largest_ref[...])
    step_size = jnp.full((1, 1), STEP_MAX, jnp.float32) / (largest + 1e-06)
    kick = jnp.sqrt(TWO_TEMP * step_size)
    for row in range(2):
        origin = row + parity - 2 * row * parity
        force = force_ref[pl.ds(row * cols, cols), :]
        out_ref[origin] = force
        next_ref[origin] = angles_ref[origin] + step_size * force + kick * noise_ref[origin]


def exchange_outer(outer):
    count = lax.axis_size("site")
    pairs = [(i, (i + 1) % count if i % 2 else (i - 1) % count) for i in range(count)]
    return lax.ppermute(outer, "site", pairs)


def exchange_inner(inner):
    return lax.ppermute(inner, "site", [(i, i ^ 1) for i in range(lax.axis_size("site"))])


def local(angles, coupling, thermal_noise, coefficients, probes, hopping, offsets):
    cols, orbitals, share, width = probes.shape[1:]
    rows = orbitals * share
    tiles = 2 * cols
    f32, bf16 = jnp.float32, jnp.bfloat16
    side = ((cols * rows, width), bf16)
    pair = ((2 * cols * rows, width), bf16)
    row = ((cols, rows, width), f32)
    matrices = ((cols, width, width), bf16)
    terms_like = ((2 * tiles, 8, width), f32)
    row_like = ((tiles, width), f32)
    sites, peers = lax.axis_size("site"), lax.axis_size("probe")
    probe_total = peers * share
    local_flops = 2 * 3 * tiles * rows * width * width
    parity = (lax.axis_index("site") % 2).astype(jnp.int32).reshape(1)

    def run(body, outs, args, scratch=(), flops=0):
        return call(
            functools.partial(body, cols, rows), outs, [IN_VMEM] * len(args),
            tuple(held(x) for x in args), scratch=scratch, flops=flops,
        )

    fetched = pl.pallas_call(
        fetch_body,
        out_shape=[
            pltpu.VMEM(*side), pltpu.VMEM(*side), pltpu.SMEM(offsets.shape, jnp.int32),
            pltpu.SMEM(coefficients.shape, f32), pltpu.VMEM(angles.shape, f32),
            pltpu.VMEM(coupling.shape, f32),
        ],
        in_specs=[IN_SMEM] + [IN_HBM] * 5,
        out_specs=[IN_VMEM, IN_VMEM, IN_SMEM, IN_SMEM, IN_VMEM, IN_VMEM],
        scratch_shapes=[pltpu.SemaphoreType.DMA((6,))],
        compiler_params=pltpu.CompilerParams(vmem_limit_bytes=16 * 1024 * 1024),
        cost_estimate=pl.CostEstimate(flops=20 * local_flops, bytes_accessed=0, transcendentals=0),
    )(parity, *(held(x, pltpu.HBM) for x in (
        probes.reshape(2, cols * rows, width), offsets, coefficients, angles, coupling)))
    outer, inner, offsets_held, coef_held, angles_held, coupling_held = fetched
    probe_rows = [outer, inner]
    got_0 = exchange_outer(outer)

    raw = hopping.reshape(-1, width, width)
    sorted_like = ((4 * tiles, width, width), bf16)
    sorted_hop, part_outer, send, weights, twice_cos, twice_sin, same_factor, cross_factor = call(
        functools.partial(first_body, cols, rows, probe_total),
        [sorted_like, row, side, ((8, 128), f32)] + [row_like] * 4,
        [IN_SMEM] * 3 + [IN_VMEM] * 5,
        (parity, held(offsets_held, pltpu.SMEM), held(coef_held, pltpu.SMEM),
         *(held(x) for x in (raw, angles_held, coupling_held, outer, inner))),
        flops=local_flops, moved=hopping.size * 2,
    )
    got_1 = exchange_outer(send)
    sorted_hop, part_inner, send_pair = call(
        functools.partial(first_rest_body, cols, rows), [sorted_like, row, pair],
        [IN_SMEM] * 2 + [IN_VMEM] * 6,
        (parity, held(offsets_held, pltpu.SMEM),
         *(held(x) for x in (raw, outer, inner, twice_cos, twice_sin, sorted_hop))),
        flops=local_flops,
    )
    from_inner = exchange_inner(send_pair)
    trig = [twice_cos, twice_sin]

    field_1_outer, low_1_outer, turned_outer = run(
        first_outer_body, [row, side, matrices], [got_0, sorted_hop, part_outer],
        flops=20 * local_flops,
    )
    (field_1_inner, low_1_inner, part_outer, part_inner, send, terms, turned_inner) = run(
        first_inner_body, [row, side, row, row, side, terms_like, matrices],
        [*probe_rows, from_inner, sorted_hop, part_inner, weights, *trig,
         field_1_outer, low_1_outer],
        flops=local_flops,
    )
    inner_2 = exchange_inner(send)
    field_2_inner, low_2_inner, rim_share, vert = run(
        second_inner_body, [row, side, row, row],
        [*probe_rows, from_inner, sorted_hop, turned_inner, part_inner],
    )
    field_2_outer, low_2_outer, part_outer, send = run(
        second_outer_body, [row, side, row, ((cols * rows + 16, width), bf16)],
        [got_1, rim_share, vert, sorted_hop, turned_outer, part_outer, field_1_outer, *trig,
         got_0, weights],
    )
    got_2 = exchange_outer(send)
    part_inner, send, terms = run(
        second_rest_body, [row, side, terms_like],
        [*probe_rows, sorted_hop, terms, weights, *trig, field_2_outer, field_2_inner,
         low_2_outer, low_2_inner, field_1_inner],
    )
    inner_3 = exchange_inner(send)
    terms, halo_2 = run(
        last_inner_body, [terms_like, row],
        [*probe_rows, inner_2, inner_3, low_1_outer, low_1_inner, low_2_outer, low_2_inner,
         field_2_outer, field_2_inner, sorted_hop, turned_outer, turned_inner, part_inner,
         terms, weights, *trig],
        scratch=[pltpu.VMEM(*side)],
    )
    shares = run(
        last_outer_body, [((2 * peers, tiles, width), f32)],
        [*probe_rows, got_2, halo_2, sorted_hop, turned_outer, part_outer, terms,
         weights, *trig, same_factor, cross_factor],
        scratch=[pltpu.VMEM(*side)], flops=local_flops,
    )[0]
    chips = [list(range(i * 2 * peers, (i + 1) * 2 * peers)) for i in range(sites // 2)]
    shares = lax.all_to_all(shares, ("site", "probe"), 0, 0, axis_index_groups=chips)
    force, largest = call(
        force_body, [row_like, ((sites // 2, 1, 128), f32)], [IN_SMEM, IN_VMEM],
        (parity, held(shares)),
    )
    near = [
        [strip * peers + (peer + strip // (sites // 2) * (peers // 2)) % peers
         for strip in range(core, sites, 2)]
        for core in range(2) for peer in range(peers)
    ]
    largest = lax.all_to_all(largest, ("site", "probe"), 0, 0, axis_index_groups=near)
    return pl.pallas_call(
        move_body,
        out_shape=[jax.ShapeDtypeStruct(angles.shape, f32)] * 2,
        in_specs=[IN_SMEM] + [IN_VMEM] * 4,
        out_specs=[IN_VMEM] * 2,
    )(parity, held(largest), held(force), held(angles), held(thermal_noise))


def solution(mesh):
    in_specs = (
        P("site", None, None),
        P("site", None, None),
        P("site", None, None),
        P(),
        P("site", None, None, "probe", None),
        P("site", None, None, None, None),
        P("site", None, None),
    )
    out_specs = (P("site", None, None), P("site", None, None))
    return jax.shard_map(local, mesh=mesh, in_specs=in_specs, out_specs=out_specs, check_vma=False)
```
